32 devices in a mesh: dp: 4 (over x, core), fsdp: 8 (over z, y).
Axes of the slice: x: 2, y: 2, z: 4, core: 2. Of those that a mesh axis runs over, the one named last changes fastest.
Arguments:
- query_key_value: bfloat16 [3, 14336, 1664], P(None, ('dp', 'fsdp')), may hold values from -60 to 60
- cotangent: bfloat16 [14336, 3200], P(('dp', 'fsdp')), may hold values from -6 to 6
- proj_weight: bfloat16 [1664, 3200], P('fsdp'), may hold values from -0.15625 to 0.15625
- layer_scale: float32 [3200], replicated, may hold values from 0.3 to 3
- lengths: int32 [4, 8, 4], P(None, 'fsdp'), may hold values from 0 to 192, as said below
Outputs:
- grad_qkv: bfloat16 [3, 14336, 1664], P(None, ('dp', 'fsdp'))
- grad_proj: float32 [1664, 3200], P('fsdp', 'dp')
The draws below stay inside these ranges and needn't reach their ends.
Inputs may be any that keep to these rules, and one draw needn't show every extreme that they name: lengths[a, b, 0] + lengths[a, b, 1] = 256, each at least 64; lengths[a, b, 2] and lengths[a, b, 3] are both 0 or both from 64 to 96; of the devices a and a + 4 / 2 (a < 2) of one fsdp index exactly one has them nonzero; in every fsdp index the nonzero one of the pair a = 0 has lengths[., b, 3] = 96.
All inputs are finite; a program needn't handle non-finite values.
Results may differ from the reference program's by a relative error of at most 0.011.
Values may be sent and summed in bfloat16 or wider, within the bound.
No kernel may reach another device: no remote copies, remote signals or barrier semaphores. Data moves between devices by JAX's collectives and lax.ppermute only.
A program may use at most 128 MiB of HBM per device.

```python
import math
import jax
import jax.numpy as jnp
from jax import lax

D = 3200
HEADS = 13
HS = 128
HD = 1664
MAIN = 256
SLOT = 96
TOK_DEV = 448
TOKENS = 14336
N_DP = 4
N_FSDP = 8


def draw_lengths(key, part):
    key = jax.random.fold_in(key, 11)
    first_key, second_key, third_key = jax.random.split(key, 3)
    low = MAIN // 4
    first = jax.random.randint(first_key, (N_DP, N_FSDP, 1), low, MAIN - low + 1)
    second = MAIN - first
    tail_low = 2 * SLOT // 3
    tails = jax.random.randint(second_key, (N_DP, N_FSDP, 2), tail_low, SLOT + 1)
    half = N_DP // 2
    flips = jax.random.randint(third_key, (half, N_FSDP, 1), 0, 2)
    flips_full = jnp.concatenate([flips, flips], axis=0)
    rows = jnp.arange(N_DP)[:, None, None]
    heavy = jnp.where(rows < half, flips_full == 0, flips_full == 1)
    pinned = (rows % half == 0) & (jnp.arange(2)[None, None, :] == 1)
    tails = jnp.where(pinned, SLOT, tails)
    tails = jnp.where(heavy, tails, 0)
    return jnp.concatenate([first, second, tails], axis=2).astype(jnp.int32)


def draw_query_key_value(key, part):
    key = jax.random.fold_in(key, 5)
    first_key = jax.random.fold_in(key, 0)
    return jnp.clip(jax.random.normal(first_key, (3, TOKENS, HEADS * HS)), -6.0, 6.0).astype(jnp.bfloat16)


def with_spikes(values, stream_key, source, target, shards_of, factor):
    def block_of(position):
        return (jnp.arange(values.shape[position]) // (values.shape[position] // shards_of)).reshape((-1,) + (1,) * (values.ndim - 1 - position))

    first = jax.random.permutation(stream_key, shards_of)[block_of(target)]
    far = (block_of(target) + shards_of // 2) % shards_of
    return jnp.where((block_of(source) == first) | (block_of(source) == far), factor * values, values)


def level_of(stream_key, dims, cuts, low, top_value):
    def one(position, parts):
        heights = jax.random.uniform(jax.random.fold_in(jax.random.fold_in(stream_key, 6), position), (parts,), jnp.float32, low / len(cuts), top_value / len(cuts))
        return jnp.repeat(jnp.exp(heights), dims[position] // parts).reshape((-1,) + (1,) * (len(dims) - position - 1))

    level = one(*cuts[0])
    for cut in cuts[1:]:
        level = level * one(*cut)
    return level


def scatter_about(key, extent, width, reach, shards=(), kind=jnp.bfloat16):
    factor_of = level_of(key, extent, shards, -0.22, 0.18) if shards else 1.0
    result = jax.random.normal(key, extent, jnp.float32) * width * factor_of
    return jnp.minimum(jnp.maximum(result, -reach), reach).astype(kind)


def gaussian_with(rng, shape, scale, limit, cuts, heavy, held_as=jnp.bfloat16):
    values = scale * jax.random.normal(rng, shape, jnp.float32)
    if cuts:
        values = values * level_of(rng, shape, cuts, -0.22, 0.18)
    return jnp.clip(with_spikes(values, jax.random.fold_in(rng, 3), *heavy), -limit, limit).astype(held_as)


def setup_inputs(seed: int = 0) -> dict:
    splits = jax.random.split(jax.random.key(seed), 6)
    query_key_value = draw_query_key_value(jax.random.fold_in(splits[5], 71), 0)
    cotangent = gaussian_with(splits[1], (TOKENS, D), 1.0, 6.0, ((0, 32),), (0, 1, 32, 2.75))
    proj_weight = scatter_about(splits[2], (HD, D), HD ** -0.5, 0.15625, ((0, 8),))
    layer_scale = jnp.clip(jnp.exp(jax.random.uniform(splits[3], (D,), jnp.float32, math.log(0.3), math.log(3.0))), 0.3, 3.0)
    lengths = draw_lengths(jax.random.fold_in(splits[5], 71), 0)
    return {"query_key_value": query_key_value, "cotangent": cotangent, "proj_weight": proj_weight, "layer_scale": layer_scale, "lengths": lengths}


def segments(counts):
    main_pos = jnp.arange(MAIN, dtype=jnp.int32)
    slot_pos = jnp.arange(SLOT, dtype=jnp.int32)
    main_ids = (main_pos >= counts[0]).astype(jnp.int32)
    first_ids = jnp.where(slot_pos < counts[2], 2, -1).astype(jnp.int32)
    second_ids = jnp.where(slot_pos < counts[3], 3, -1).astype(jnp.int32)
    return jnp.concatenate([main_ids, first_ids, second_ids])


def attend(query_rows, key_rows, value_rows, grad_rows, segment):
    rows = query_rows.shape[0]
    factor = HS ** -0.5
    query_h = query_rows.reshape(rows, HEADS, HS).astype(jnp.float32)
    key_h = key_rows.reshape(rows, HEADS, HS).astype(jnp.float32)
    value_h = value_rows.reshape(rows, HEADS, HS).astype(jnp.float32)
    grad_h = grad_rows.reshape(rows, HEADS, HS).astype(jnp.float32)
    scores = jnp.einsum("qhd,khd->hqk", query_h, key_h) * factor
    valid = segment >= 0
    allowed = (segment[:, None] == segment[None, :]) & valid[:, None]
    scores = jnp.where(allowed[None], scores, -1e30)
    highest = jnp.max(scores, axis=2, keepdims=True)
    weights = jnp.exp(scores - highest)
    probs = weights / jnp.sum(weights, axis=2, keepdims=True)
    probs = jnp.where(valid[None, :, None], probs, jnp.zeros_like(probs))
    probs_b = probs.astype(jnp.bfloat16).astype(jnp.float32)
    attended = jnp.einsum("hqk,khd->qhd", probs_b, value_h).reshape(rows, HD).astype(jnp.bfloat16)
    dprob = jnp.einsum("qhd,khd->hqk", grad_h, value_h)
    delta = jnp.sum(probs * dprob, axis=2, keepdims=True)
    dscore = (probs * (dprob - delta) * factor).astype(jnp.bfloat16).astype(jnp.float32)
    grad_query = jnp.einsum("hqk,khd->qhd", dscore, key_h).reshape(rows, HD).astype(jnp.bfloat16)
    grad_key = jnp.einsum("hqk,qhd->khd", dscore, query_h).reshape(rows, HD).astype(jnp.bfloat16)
    grad_value = jnp.einsum("hqk,qhd->khd", probs_b, grad_h).reshape(rows, HD).astype(jnp.bfloat16)
    return attended, grad_query, grad_key, grad_value


def reference(query_key_value, cotangent, proj_weight, layer_scale, lengths):
    scaled = (cotangent.astype(jnp.float32) * layer_scale[None, :]).astype(jnp.bfloat16)
    grad_out = jnp.dot(scaled, proj_weight.T, preferred_element_type=jnp.float32).astype(jnp.bfloat16)
    groups_all = N_DP * N_FSDP
    split = query_key_value.reshape(3, groups_all, TOK_DEV, HD)
    grad_groups = grad_out.reshape(groups_all, TOK_DEV, HD)
    scaled_groups = scaled.reshape(groups_all, TOK_DEV, D)
    counts_all = lengths.reshape(groups_all, 4)

    def one_group(total, items):
        query_rows, key_rows, value_rows, grad_rows, scaled_rows, counts = items
        segment = segments(counts)
        attended, grad_query, grad_key, grad_value = attend(query_rows, key_rows, value_rows, grad_rows, segment)
        term = jnp.dot(attended.T, scaled_rows, preferred_element_type=jnp.float32)
        return total + term, jnp.stack([grad_query, grad_key, grad_value])

    total, stacked = lax.scan(one_group, jnp.zeros((HD, D), jnp.float32),
                              (split[0], split[1], split[2], grad_groups, scaled_groups, counts_all))
    grad_qkv = jnp.transpose(stacked, (1, 0, 2, 3)).reshape(3, TOKENS, HD)
    return grad_qkv, total
```

```python
import functools

import jax
import jax.numpy as jnp
from jax import lax
from jax.experimental import pallas as pl
from jax.experimental.pallas import tpu as pltpu
from jax.sharding import PartitionSpec as P

HS = 128
MAIN = 256
SLOT = 96
LANE = 128
FACTOR = HS ** (-0.5)
VMEM_BYTES = 32 * 1024 * 1024
LONG = pl.CostEstimate(flops=10 ** 11, bytes_accessed=10 ** 8, transcendentals=0)
SHORT = pl.CostEstimate(flops=1000, bytes_accessed=1000, transcendentals=0)


def dot(left, right, left_dim, right_dim):
    return lax.dot_general(left, right, (((left_dim,), (right_dim,)), ((), ())), preferred_element_type=jnp.float32)


def prepare_kernel(steps, width, starts, cotangent, layer_scale, scaled, turned, *windows):
    block = cotangent.shape[1]
    values = cotangent[...].astype(jnp.float32) * layer_scale[...]
    at = pl.ds(pl.multiple_of(pl.program_id(0) * block, LANE), block)
    scaled[:, at] = values.astype(jnp.bfloat16)
    spare = jnp.zeros((turned.shape[1] - values.shape[0], block), jnp.float32)
    turned[...] = jnp.concatenate([values, spare], axis=0).T.astype(jnp.bfloat16)

    @pl.when(pl.program_id(0) == steps - 1)
    def _():
        for k, window in enumerate(windows):
            window[...] = scaled[:, pl.ds(pl.multiple_of(starts[k], LANE), width)]


def prepare(starts, cotangent, layer_scale, peers, width):
    rows, total = cotangent.shape
    lanes = -(-rows // LANE) * LANE
    steps = 5
    block = total // steps
    return pl.pallas_call(
        functools.partial(prepare_kernel, steps, width),
        grid_spec=pltpu.PrefetchScalarGridSpec(
            num_scalar_prefetch=1,
            grid=(steps,),
            in_specs=[
                pl.BlockSpec((rows, block), lambda i, s: (0, i)),
                pl.BlockSpec((1, block), lambda i, s: (0, i)),
            ],
            out_specs=[
                pl.BlockSpec((rows, total), lambda i, s: (0, 0)),
                pl.BlockSpec((block, lanes), lambda i, s: (i, 0)),
            ]
            + [pl.BlockSpec((rows, width), lambda i, s: (0, 0))] * peers,
        ),
        out_shape=[
            jax.ShapeDtypeStruct((rows, total), jnp.bfloat16),
            jax.ShapeDtypeStruct((total, lanes), jnp.bfloat16),
        ]
        + [jax.ShapeDtypeStruct((rows, width), jnp.bfloat16)] * peers,
        compiler_params=pltpu.CompilerParams(vmem_limit_bytes=VMEM_BYTES),
        cost_estimate=LONG,
        name="scaled_cotangent",
    )(starts, cotangent, layer_scale.reshape(1, total))


def arrange_kernel(sizes, order, attended, *refs):
    *outs, sems = refs
    copies = []
    for out, size in zip(outs, sizes):
        for j in range(size):
            n = len(copies)
            copies.append(pltpu.make_async_copy(attended.at[order[n]], out.at[j], sems.at[n]))
    for copy in copies:
        copy.start()
    for copy in copies:
        copy.wait()


def arrange(order, attended, sizes):
    _, depth, rows = attended.shape
    return pl.pallas_call(
        functools.partial(arrange_kernel, sizes),
        grid_spec=pltpu.PrefetchScalarGridSpec(
            num_scalar_prefetch=1,
            grid=(1,),
            in_specs=[pl.BlockSpec(memory_space=pl.ANY)],
            out_specs=[pl.BlockSpec(memory_space=pl.ANY)] * len(sizes),
            scratch_shapes=[pltpu.SemaphoreType.DMA((sum(sizes),))],
        ),
        out_shape=[jax.ShapeDtypeStruct((size, depth, rows), attended.dtype) for size in sizes],
        compiler_params=pltpu.CompilerParams(vmem_limit_bytes=VMEM_BYTES),
        cost_estimate=SHORT,
        name="attended_chunks",
    )(order, attended)


PAIR = 2
EXPONENT = FACTOR * 1.4426950408889634


def forward_kernel(counts, qkv, attended, main_probs, slot_probs):
    def marks(image, ids):
        lane = lax.broadcasted_iota(jnp.int32, (image.shape[0], HS), 1)
        first = jnp.where(image == ids[0], 1.0, 0.0)
        second = jnp.where(image == ids[1], 1.0, 0.0)
        own = jnp.where(lane == 0, first, jnp.where(lane == 1, second, 0.0))
        other = jnp.where(lane == 0, 1.0 - first, jnp.where(lane == 1, 1.0 - second, 0.0)) * -1e30
        return own.astype(jnp.bfloat16), other.astype(jnp.bfloat16)

    main_at = lax.broadcasted_iota(jnp.int32, (MAIN, HS), 0)
    main_marks = marks(jnp.where(main_at >= counts[0], 1, 0), (0, 1))

    def image(at):
        first = jnp.where(at < counts[2], 2, -1)
        return jnp.where(at < SLOT, first, jnp.where(at - SLOT < counts[3], 3, -1))

    slot_marks = marks(image(lax.broadcasted_iota(jnp.int32, (2 * SLOT, HS), 0)), (2, 3))
    valid = image(lax.broadcasted_iota(jnp.int32, (1, 2 * SLOT), 1)) >= 0
    parts = []
    for head in range(PAIR):
        lanes = slice(head * HS, (head + 1) * HS)
        parts.append((head, 0, MAIN, lanes, main_marks, None, main_probs))
        parts.append((head, MAIN, 2 * SLOT, lanes, slot_marks, valid, slot_probs))
    scores = []
    for head, first, rows, lanes, (mark_query, mark_key), _, _ in parts:
        query = jnp.concatenate([qkv[0, first:first + rows, lanes], mark_query], axis=1)
        key = jnp.concatenate([qkv[1, first:first + rows, lanes], mark_key], axis=1)
        scores.append(dot(key, query, 1, 1))
    probs = []
    for score, (_, _, _, _, _, good, _) in zip(scores, parts):
        weights = jnp.exp2((score - jnp.max(score, axis=0, keepdims=True)) * EXPONENT)
        scale = 1.0 / jnp.sum(weights, axis=0, keepdims=True)
        probs.append(weights * (scale if good is None else jnp.where(good, scale, 0.0)))
    for prob, (head, first, rows, lanes, _, _, probs_ref) in zip(probs, parts):
        probs_ref[head] = prob
        result = dot(qkv[2, first:first + rows, lanes], prob.astype(jnp.bfloat16), 0, 0)
        attended[lanes, first:first + rows] = result.astype(jnp.bfloat16)


def forward(counts, qkv):
    _, rows, width = qkv.shape
    heads = width // HS
    return pl.pallas_call(
        forward_kernel,
        grid_spec=pltpu.PrefetchScalarGridSpec(
            num_scalar_prefetch=1,
            grid=(-(-heads // PAIR),),
            in_specs=[pl.BlockSpec((3, rows, PAIR * HS), lambda h, c: (0, 0, h))],
            out_specs=[
                pl.BlockSpec((PAIR * HS, rows), lambda h, c: (h, 0)),
                pl.BlockSpec((PAIR, MAIN, MAIN), lambda h, c: (h, 0, 0)),
                pl.BlockSpec((PAIR, 2 * SLOT, 2 * SLOT), lambda h, c: (h, 0, 0)),
            ],
        ),
        out_shape=[
            jax.ShapeDtypeStruct((width, rows), jnp.bfloat16),
            jax.ShapeDtypeStruct((heads, MAIN, MAIN), jnp.float32),
            jax.ShapeDtypeStruct((heads, 2 * SLOT, 2 * SLOT), jnp.float32),
        ],
        compiler_params=pltpu.CompilerParams(vmem_limit_bytes=VMEM_BYTES),
        cost_estimate=LONG,
        name="attention_forward",
    )(counts, qkv)


def backward_kernel(qkv, grad_mine, grad_other, main_probs, slot_probs, *rest):
    grads = rest[-1]
    parts = []
    for head in range(PAIR):
        lanes = slice(head * HS, (head + 1) * HS)
        for first, rows, probs_ref in ((0, MAIN, main_probs), (MAIN, 2 * SLOT, slot_probs)):
            parts.append((head, slice(first, first + rows), lanes, probs_ref))
    grad, dprobs, dscores = [], [], []
    for head, at, lanes, _ in parts:
        both = grad_mine[lanes, at] + grad_other[lanes, at].astype(jnp.float32)
        grad.append(both.astype(jnp.bfloat16))
    for g, (head, at, lanes, _) in zip(grad, parts):
        dprobs.append(dot(qkv[2, at, lanes], g, 1, 0))
    for g, (head, at, lanes, probs_ref) in zip(grad, parts):
        grads[2, at, lanes] = dot(probs_ref[head].astype(jnp.bfloat16), g, 1, 1).astype(jnp.bfloat16)
    for dprob, (head, at, lanes, probs_ref) in zip(dprobs, parts):
        probs = probs_ref[head]
        delta = jnp.sum(probs * dprob, axis=0, keepdims=True)
        dscores.append((probs * (dprob - delta) * FACTOR).astype(jnp.bfloat16))
    for dscore, (head, at, lanes, _) in zip(dscores, parts):
        grads[1, at, lanes] = dot(dscore, qkv[0, at, lanes], 1, 0).astype(jnp.bfloat16)
        grads[0, at, lanes] = dot(dscore, qkv[1, at, lanes], 0, 0).astype(jnp.bfloat16)


def backward(qkv, grad_mine, grad_other, main_probs, slot_probs, low, high, grads):
    _, rows, width = qkv.shape
    held = [] if grads is None else [grads]
    return pl.pallas_call(
        backward_kernel,
        grid=(high - low,),
        in_specs=[
            pl.BlockSpec((3, rows, PAIR * HS), lambda h: (0, 0, h + low)),
            pl.BlockSpec((PAIR * HS, rows), lambda h: (h + low, 0)),
            pl.BlockSpec((PAIR * HS, rows), lambda h: (h + low, 0)),
            pl.BlockSpec((PAIR, MAIN, MAIN), lambda h: (h + low, 0, 0)),
            pl.BlockSpec((PAIR, 2 * SLOT, 2 * SLOT), lambda h: (h + low, 0, 0)),
        ] + [pl.BlockSpec(memory_space=pl.ANY)] * len(held),
        out_specs=pl.BlockSpec((3, rows, PAIR * HS), lambda h: (0, 0, h + low)),
        out_shape=jax.ShapeDtypeStruct(qkv.shape, jnp.bfloat16),
        input_output_aliases={5: 0} if held else {},
        compiler_params=pltpu.CompilerParams(vmem_limit_bytes=VMEM_BYTES),
        cost_estimate=LONG,
        name="attention_backward",
    )(qkv, grad_mine, grad_other, main_probs, slot_probs, *held)


def grad_out_kernel(sizes, split, total, info, turned, turned_other, *refs):
    columns, sems = refs[-2:]
    mine, other = refs[-4:-2]
    step = pl.program_id(0)
    core = info[0]
    at = pl.ds(pl.multiple_of(core * (total - split), LANE), split)
    copies = [
        pltpu.make_async_copy(source.at[at], columns.at[i], sems.at[i]) for i, source in enumerate((turned, turned_other))
    ]

    @pl.when(step == 0)
    def _():
        for copy in copies:
            copy.start()
        for copy in copies:
            copy.wait()

        @pl.when(core == 1)
        def _():
            shared = 2 * split - total
            columns[:, :shared, :] = jnp.zeros((2, shared, columns.shape[2]), jnp.bfloat16)

    index = 0
    for j, size in enumerate(sizes):

        @pl.when(step == j)
        def _(index=index, size=size):
            first = 0
            for piece in refs[index:index + size]:
                at = slice(first, first + piece.shape[0])
                rows = mine.shape[2]
                mine[0, at, :] = dot(piece[...], columns[0], 1, 0)[:, :rows]
                other[0, at, :] = dot(piece[...], columns[1], 1, 0)[:, :rows].astype(jnp.bfloat16)
                first += piece.shape[0]

        index += size


def grad_out_rows(info, turned, turned_other, rows, pieces, shards, held):
    total, lanes = turned.shape
    split = pieces[0][0].shape[1]
    depth = sum(p.shape[0] for p in pieces[0])
    sizes = [len(p) for p in pieces]
    arrays = [a for p in pieces for a in p]
    held = [] if held is None else list(held)
    return pl.pallas_call(
        functools.partial(grad_out_kernel, sizes, split, total),
        grid_spec=pltpu.PrefetchScalarGridSpec(
            num_scalar_prefetch=1,
            grid=(len(pieces),),
            in_specs=[pl.BlockSpec(memory_space=pl.ANY)] * 2
            + [pl.BlockSpec(a.shape, lambda j, info: (0, 0)) for a in arrays]
            + [pl.BlockSpec(memory_space=pl.ANY)] * len(held),
            out_specs=[pl.BlockSpec((1, depth, rows), lambda j, info: (info[1 + j], 0, 0))] * 2,
            scratch_shapes=[pltpu.VMEM((2, split, lanes), jnp.bfloat16), pltpu.SemaphoreType.DMA((2,))],
        ),
        out_shape=[
            jax.ShapeDtypeStruct((shards, depth, rows), jnp.float32),
            jax.ShapeDtypeStruct((shards, depth, rows), jnp.bfloat16),
        ],
        input_output_aliases={3 + len(arrays) + i: i for i in range(len(held))},
        compiler_params=pltpu.CompilerParams(vmem_limit_bytes=VMEM_BYTES),
        cost_estimate=LONG,
        name="grad_out_rows",
    )(info, turned, turned_other, *arrays, *held)


def partial_kernel(sources, count, window, order, starts, *refs):
    attended, columns = refs[:sources], refs[sources:2 * sources]
    outs, (chunks, held, sems) = refs[2 * sources:-3], refs[-3:]
    depth = chunks.shape[2]
    copies = []
    for i in range(sources):
        at = pl.ds(pl.multiple_of(starts[min(i // 2, 1)], LANE), window)
        some = [pltpu.make_async_copy(columns[i].at[:, at], held.at[i], sems.at[i, count])]
        for j in range(count):
            source = attended[i].at[order[j] if i < 2 else j]
            some.append(pltpu.make_async_copy(source, chunks.at[i, j], sems.at[i, j]))
        copies.append(some)
    for some in copies:
        for copy in some:
            copy.start()
    together = depth % 16 == 0
    for i, some in enumerate(copies):
        for copy in some:
            copy.wait()
        if together:
            product = dot(chunks[i].reshape(count * depth, chunks.shape[3]), held[i], 1, 0)
        for j, out in enumerate(outs):
            part = product[j * depth:(j + 1) * depth] if together else dot(chunks[i, j], held[i], 1, 0)
            if i == 0:
                out[...] = part
            else:
                out[...] += part


def partial_products(order, starts, attended, columns, window):
    _, depth, rows = attended[0].shape
    count, sources = order.shape[0], len(attended)
    return pl.pallas_call(
        functools.partial(partial_kernel, sources, count, window),
        grid_spec=pltpu.PrefetchScalarGridSpec(
            num_scalar_prefetch=2,
            grid=(1,),
            in_specs=[pl.BlockSpec(memory_space=pl.ANY)] * (2 * sources),
            out_specs=[pl.BlockSpec((depth, window), lambda j, o, s: (0, 0))] * count,
            scratch_shapes=[
                pltpu.VMEM((sources, count, depth, rows), jnp.bfloat16),
                pltpu.VMEM((sources, rows, window), jnp.bfloat16),
                pltpu.SemaphoreType.DMA((sources, count + 1)),
            ],
        ),
        out_shape=[jax.ShapeDtypeStruct((depth, window), jnp.float32)] * count,
        compiler_params=pltpu.CompilerParams(vmem_limit_bytes=VMEM_BYTES),
        cost_estimate=LONG,
        name="projection_partial",
    )(order, starts, *attended, *columns)


def windows_of(groups, owned, total):
    lows = [g * owned // LANE * LANE for g in range(groups)]
    width = max(-(-((g + 1) * owned) // LANE) * LANE - low for g, low in enumerate(lows))
    return width


def ring_of(count):
    return list(range(0, count, 2)) + list(range(count - 1, 0, -2))


def local(members, shards, query_key_value, cotangent, proj_weight, layer_scale, lengths):
    member = lax.axis_index("dp")
    shard = lax.axis_index("fsdp")
    core, chip, peers = member % 2, member // 2, members // 2
    ring = ring_of(shards)
    place = jnp.where(shard % 2 == 0, shard // 2, shards - 1 - shard // 2)
    ahead = [(ring[i], ring[(i + 1) % shards]) for i in range(shards)]
    behind = [(ring[i], ring[(i - 1) % shards]) for i in range(shards)]
    half = shards // 2
    depth, total = proj_weight.shape
    rows, width = query_key_value.shape[1:]
    owned = total // members
    counts = lax.dynamic_index_in_dim(lengths[:, 0, :], member, 0, keepdims=False)

    def swap(array, bit):
        return lax.ppermute(array, "dp", [(i, i ^ bit) for i in range(members)])

    def shard_at(offset):
        at = (place + offset + shards) % shards
        return jnp.where(at < half, 2 * at, 2 * (shards - 1 - at) + 1)

    def table(values):
        return jnp.stack([jnp.asarray(v) for v in values]).astype(jnp.int32)

    chip_width, window = windows_of(peers, 2 * owned, total), windows_of(members, owned, total)

    def chip_start(chip):
        return jnp.minimum(chip * 2 * owned // LANE * LANE, total - chip_width)

    my_start = jnp.minimum(member * owned // LANE * LANE, chip_start(chip) + chip_width - window)
    starts = table([my_start, my_start - chip_start(chip)])

    split = -(-(total // LANE) // 2) * LANE
    mine = jnp.where(core == 0, proj_weight[:, :split], proj_weight[:, total - split:])
    cut = -(-depth // 32) * 16
    up, down = [mine], [mine]
    up.append(lax.ppermute(up[-1], "fsdp", ahead))
    down.append(lax.ppermute(down[-1], "fsdp", behind))

    mine, cotangent = lax.optimization_barrier((mine, cotangent))
    scaled, turned, *sent = prepare(
        table([chip_start(chip ^ k) for k in range(1, peers)] or [0]), cotangent, layer_scale, peers - 1, chip_width
    )
    columns = [scaled, swap(scaled, 1)]
    turned_other = swap(turned, 1)
    attended, main_probs, slot_probs = forward(counts, query_key_value)
    attended = attended.reshape(shards, depth, rows)
    near = [[o, -o] for o in range(half - 1, 0, -1)]
    groups = [[half] + near[0]] + near[1:-1] + [near[-1] + [0]]
    came_columns = [swap(sent[k - 1], 2 * k) for k in range(1, peers)]
    flat = table([shard_at(o) for group in groups for o in group])
    sizes = [len(group) for group in groups]
    orders = [flat[sum(sizes[:g]):sum(sizes[:g + 1])] for g in range(len(groups))]
    chunks = list(arrange(flat, attended, sizes))
    came = [[swap(chunks[0], 2 * k) for k in range(1, peers)]]

    def rows_of(some, held):
        info = table([core] + [shard_at(o) for _, o in some])
        return grad_out_rows(info, turned, turned_other, rows, [p for p, _ in some], shards, held)

    up[1], down[1], attended = lax.optimization_barrier((up[1], down[1], attended))
    both = [attended, swap(attended, 1)]
    for _ in range(half - 3):
        up.append(lax.ppermute(up[-1], "fsdp", ahead))
        down.append(lax.ppermute(down[-1], "fsdp", behind))
    up[-1], down[-1], columns[1], turned_other = lax.optimization_barrier((up[-1], down[-1], columns[1], turned_other))
    came_columns, near_up, near_down, chunks = lax.optimization_barrier((came_columns, up[-1], down[-1], chunks))
    came.append([swap(chunks[1], 2 * k) for k in range(1, peers)])
    pieces = [([mine], 0)]
    for step in range(1, half - 1):
        last = step == half - 2
        pieces += [([near_up if last else up[step]], -step), ([near_down if last else down[step]], step)]
    grad_out = rows_of(pieces, None)
    for c in came_columns:
        columns += [c, swap(c, 1)]
    up.append(lax.ppermute(up[-1], "fsdp", ahead))
    down.append(lax.ppermute(down[-1], "fsdp", behind))
    up[-1], down[-1], grad_out, both[1] = lax.optimization_barrier((up[-1], down[-1], grad_out, both[1]))
    came[0], near_up, near_down, chunks = lax.optimization_barrier((came[0], up[-1], down[-1], chunks))
    came += [[swap(some, 2 * k) for k in range(1, peers)] for some in chunks[2:]]
    far_up = lax.ppermute(up[-1][:cut], "fsdp", ahead)
    far_down = lax.ppermute(down[-1][cut:], "fsdp", behind)

    def products(index):
        taken = list(both)
        for c in came[index]:
            taken += [c, swap(c, 1)]
        result = partial_products(orders[index], starts, taken, columns, window)
        return {o: result[j] for j, o in enumerate(groups[index])}

    terms = products(0)
    first = terms[half].astype(jnp.bfloat16)
    far_up, far_down, terms = lax.optimization_barrier((far_up, far_down, terms))
    going_up, going_down = first[:cut], first[cut:]
    came_up = lax.ppermute(going_up, "fsdp", ahead)
    came_down = lax.ppermute(going_down, "fsdp", behind)

    grad_out = rows_of([([near_up], 1 - half), ([near_down], half - 1), ([far_up, far_down], half)], grad_out)
    grad_mine = grad_out[0].reshape(width, rows)
    grad_other = swap(grad_out[1], 1).reshape(width, rows)
    pairs = -(-(width // HS) // PAIR)
    bounds = [0, 3, 5, pairs]

    def back(index, held):
        return backward(
            query_key_value, grad_mine, grad_other, main_probs, slot_probs, bounds[index], bounds[index + 1], held
        )

    grads = None
    for step in range(half, 1, -1):
        if step == half:
            came_up = jnp.pad(came_up, ((0, depth - cut), (0, 0)))
            came_down = jnp.pad(came_down, ((cut, 0), (0, 0)))
        else:
            terms.update(products(half - step))
        going_up = (terms[step - 1] + came_up.astype(jnp.float32)).astype(jnp.bfloat16)
        going_down = (terms[1 - step] + came_down.astype(jnp.float32)).astype(jnp.bfloat16)
        beside = []
        if step > 2:
            beside.append(came[half - step + 1])
        if step == 3:
            beside.append(grad_mine)
        if step == 2:
            grads = back(0, grads)
            beside.append(grads)
        going_up, going_down, *beside = lax.optimization_barrier((going_up, going_down, *beside))
        if step > 2:
            came[half - step + 1] = beside[0]
        if step == 3:
            grad_mine = beside[1]
        if step == 2:
            grads = beside[0]
        came_up = lax.ppermute(going_up, "fsdp", ahead)
        came_down = lax.ppermute(going_down, "fsdp", behind)
    grads = back(2, back(1, grads))
    came_up, came_down, grads = lax.optimization_barrier((came_up, came_down, grads))
    reduced = terms[0] + came_up.astype(jnp.float32) + came_down.astype(jnp.float32)
    grad_proj = lax.dynamic_slice_in_dim(reduced, member * owned - my_start, owned, 1)
    return grads, grad_proj


def solution(mesh):
    members, shards = mesh.shape["dp"], mesh.shape["fsdp"]
    placed = (
        P(None, ("dp", "fsdp"), None),
        P(("dp", "fsdp"), None),
        P("fsdp", None),
        P(),
        P(None, "fsdp", None),
    )
    return jax.shard_map(
        functools.partial(local, members, shards),
        mesh=mesh,
        in_specs=placed,
        out_specs=(P(None, ("dp", "fsdp"), None), P("fsdp", "dp")),
        check_vma=False,
    )
```

```python
import functools

import jax
import jax.numpy as jnp
from jax import lax
from jax.experimental import pallas as pl
from jax.experimental.pallas import tpu as pltpu
from jax.sharding import PartitionSpec as P

HS = 128
MAIN = 256
SLOT = 96
LANE = 128
FACTOR = HS ** (-0.5)
VMEM_BYTES = 32 * 1024 * 1024
LONG = pl.CostEstimate(flops=10 ** 11, bytes_accessed=10 ** 8, transcendentals=0)
SHORT = pl.CostEstimate(flops=1000, bytes_accessed=1000, transcendentals=0)


def dot(left, right, left_dim, right_dim):
    return lax.dot_general(left, right, (((left_dim,), (right_dim,)), ((), ())), preferred_element_type=jnp.float32)


def in_hbm(array):
    return pltpu.with_memory_space_constraint(array, pltpu.HBM)


def prepare_kernel(steps, width, starts, cotangent, layer_scale, scaled, turned, *windows):
    block = cotangent.shape[1]
    values = cotangent[...].astype(jnp.float32) * layer_scale[...]
    at = pl.ds(pl.multiple_of(pl.program_id(0) * block, LANE), block)
    scaled[:, at] = values.astype(jnp.bfloat16)
    spare = jnp.zeros((turned.shape[1] - values.shape[0], block), jnp.float32)
    turned[...] = jnp.concatenate([values, spare], axis=0).T.astype(jnp.bfloat16)

    @pl.when(pl.program_id(0) == steps - 1)
    def _():
        for k, window in enumerate(windows):
            window[...] = scaled[:, pl.ds(pl.multiple_of(starts[k], LANE), width)]


def prepare(starts, cotangent, layer_scale, peers, width):
    rows, total = cotangent.shape
    lanes = -(-rows // LANE) * LANE
    steps = 5
    block = total // steps
    return pl.pallas_call(
        functools.partial(prepare_kernel, steps, width),
        grid_spec=pltpu.PrefetchScalarGridSpec(
            num_scalar_prefetch=1,
            grid=(steps,),
            in_specs=[
                pl.BlockSpec((rows, block), lambda i, s: (0, i)),
                pl.BlockSpec((1, block), lambda i, s: (0, i)),
            ],
            out_specs=[
                pl.BlockSpec((rows, total), lambda i, s: (0, 0)),
                pl.BlockSpec((block, lanes), lambda i, s: (i, 0)),
            ]
            + [pl.BlockSpec((rows, width), lambda i, s: (0, 0))] * peers,
        ),
        out_shape=[
            jax.ShapeDtypeStruct((rows, total), jnp.bfloat16),
            jax.ShapeDtypeStruct((total, lanes), jnp.bfloat16),
        ]
        + [jax.ShapeDtypeStruct((rows, width), jnp.bfloat16)] * peers,
        compiler_params=pltpu.CompilerParams(vmem_limit_bytes=VMEM_BYTES),
        cost_estimate=LONG,
        name="scaled_cotangent",
    )(starts, in_hbm(cotangent), layer_scale.reshape(1, total))


def arrange_kernel(sizes, order, attended, *refs):
    *outs, sems = refs
    copies = []
    for out, size in zip(outs, sizes):
        for j in range(size):
            n = len(copies)
            copies.append(pltpu.make_async_copy(attended.at[order[n]], out.at[j], sems.at[n]))
    for copy in copies:
        copy.start()
    for copy in copies:
        copy.wait()


def arrange(order, attended, sizes):
    _, depth, rows = attended.shape
    return pl.pallas_call(
        functools.partial(arrange_kernel, sizes),
        grid_spec=pltpu.PrefetchScalarGridSpec(
            num_scalar_prefetch=1,
            grid=(1,),
            in_specs=[pl.BlockSpec(memory_space=pl.ANY)],
            out_specs=[pl.BlockSpec(memory_space=pl.ANY)] * len(sizes),
            scratch_shapes=[pltpu.SemaphoreType.DMA((sum(sizes),))],
        ),
        out_shape=[jax.ShapeDtypeStruct((size, depth, rows), attended.dtype) for size in sizes],
        compiler_params=pltpu.CompilerParams(vmem_limit_bytes=VMEM_BYTES),
        cost_estimate=SHORT,
        name="attended_chunks",
    )(order, attended)


PAIR = 2
EXPONENT = FACTOR * 1.4426950408889634


def forward_kernel(counts, qkv, attended, main_probs, slot_probs):
    def marks(image, ids):
        lane = lax.broadcasted_iota(jnp.int32, (image.shape[0], HS), 1)
        first = jnp.where(image == ids[0], 1.0, 0.0)
        second = jnp.where(image == ids[1], 1.0, 0.0)
        own = jnp.where(lane == 0, first, jnp.where(lane == 1, second, 0.0))
        other = jnp.where(lane == 0, 1.0 - first, jnp.where(lane == 1, 1.0 - second, 0.0)) * -1e30
        return own.astype(jnp.bfloat16), other.astype(jnp.bfloat16)

    main_at = lax.broadcasted_iota(jnp.int32, (MAIN, HS), 0)
    main_marks = marks(jnp.where(main_at >= counts[0], 1, 0), (0, 1))

    def image(at):
        first = jnp.where(at < counts[2], 2, -1)
        return jnp.where(at < SLOT, first, jnp.where(at - SLOT < counts[3], 3, -1))

    slot_marks = marks(image(lax.broadcasted_iota(jnp.int32, (2 * SLOT, HS), 0)), (2, 3))
    valid = image(lax.broadcasted_iota(jnp.int32, (1, 2 * SLOT), 1)) >= 0
    parts = []
    for head in range(PAIR):
        lanes = slice(head * HS, (head + 1) * HS)
        parts.append((head, 0, MAIN, lanes, main_marks, None, main_probs))
        parts.append((head, MAIN, 2 * SLOT, lanes, slot_marks, valid, slot_probs))
    scores = []
    for head, first, rows, lanes, (mark_query, mark_key), _, _ in parts:
        query = jnp.concatenate([qkv[0, first:first + rows, lanes], mark_query], axis=1)
        key = jnp.concatenate([qkv[1, first:first + rows, lanes], mark_key], axis=1)
        scores.append(dot(key, query, 1, 1))
    probs = []
    for score, (_, _, _, _, _, good, _) in zip(scores, parts):
        weights = jnp.exp2((score - jnp.max(score, axis=0, keepdims=True)) * EXPONENT)
        scale = 1.0 / jnp.sum(weights, axis=0, keepdims=True)
        probs.append(weights * (scale if good is None else jnp.where(good, scale, 0.0)))
    for prob, (head, first, rows, lanes, _, _, probs_ref) in zip(probs, parts):
        probs_ref[head] = prob
        result = dot(qkv[2, first:first + rows, lanes], prob.astype(jnp.bfloat16), 0, 0)
        attended[lanes, first:first + rows] = result.astype(jnp.bfloat16)


def forward(counts, qkv):
    _, rows, width = qkv.shape
    heads = width // HS
    return pl.pallas_call(
        forward_kernel,
        grid_spec=pltpu.PrefetchScalarGridSpec(
            num_scalar_prefetch=1,
            grid=(-(-heads // PAIR),),
            in_specs=[pl.BlockSpec((3, rows, PAIR * HS), lambda h, c: (0, 0, h))],
            out_specs=[
                pl.BlockSpec((PAIR * HS, rows), lambda h, c: (h, 0)),
                pl.BlockSpec((PAIR, MAIN, MAIN), lambda h, c: (h, 0, 0)),
                pl.BlockSpec((PAIR, 2 * SLOT, 2 * SLOT), lambda h, c: (h, 0, 0)),
            ],
        ),
        out_shape=[
            pltpu.HBM((width, rows), jnp.bfloat16),
            pltpu.HBM((heads, MAIN, MAIN), jnp.float32),
            pltpu.HBM((heads, 2 * SLOT, 2 * SLOT), jnp.float32),
        ],
        compiler_params=pltpu.CompilerParams(vmem_limit_bytes=VMEM_BYTES),
        cost_estimate=LONG,
        name="attention_forward",
    )(counts, in_hbm(qkv))


def backward_kernel(qkv, grad_mine, grad_other, main_probs, slot_probs, *rest):
    grads = rest[-1]
    parts = []
    for head in range(PAIR):
        lanes = slice(head * HS, (head + 1) * HS)
        for first, rows, probs_ref in ((0, MAIN, main_probs), (MAIN, 2 * SLOT, slot_probs)):
            parts.append((head, slice(first, first + rows), lanes, probs_ref))
    grad, dprobs, dscores = [], [], []
    for head, at, lanes, _ in parts:
        both = grad_mine[lanes, at] + grad_other[lanes, at].astype(jnp.float32)
        grad.append(both.astype(jnp.bfloat16))
    for g, (head, at, lanes, _) in zip(grad, parts):
        dprobs.append(dot(qkv[2, at, lanes], g, 1, 0))
    for g, (head, at, lanes, probs_ref) in zip(grad, parts):
        grads[2, at, lanes] = dot(probs_ref[head].astype(jnp.bfloat16), g, 1, 1).astype(jnp.bfloat16)
    for dprob, (head, at, lanes, probs_ref) in zip(dprobs, parts):
        probs = probs_ref[head]
        delta = jnp.sum(probs * dprob, axis=0, keepdims=True)
        dscores.append((probs * (dprob - delta) * FACTOR).astype(jnp.bfloat16))
    for dscore, (head, at, lanes, _) in zip(dscores, parts):
        grads[1, at, lanes] = dot(dscore, qkv[0, at, lanes], 1, 0).astype(jnp.bfloat16)
        grads[0, at, lanes] = dot(dscore, qkv[1, at, lanes], 0, 0).astype(jnp.bfloat16)


def backward(qkv, grad_mine, grad_other, main_probs, slot_probs, low, high, grads):
    _, rows, width = qkv.shape
    held = [] if grads is None else [grads]
    return pl.pallas_call(
        backward_kernel,
        grid=(high - low,),
        in_specs=[
            pl.BlockSpec((3, rows, PAIR * HS), lambda h: (0, 0, h + low)),
            pl.BlockSpec((PAIR * HS, rows), lambda h: (h + low, 0)),
            pl.BlockSpec((PAIR * HS, rows), lambda h: (h + low, 0)),
            pl.BlockSpec((PAIR, MAIN, MAIN), lambda h: (h + low, 0, 0)),
            pl.BlockSpec((PAIR, 2 * SLOT, 2 * SLOT), lambda h: (h + low, 0, 0)),
        ] + [pl.BlockSpec(memory_space=pl.ANY)] * len(held),
        out_specs=pl.BlockSpec((3, rows, PAIR * HS), lambda h: (0, 0, h + low)),
        out_shape=pltpu.HBM(qkv.shape, jnp.bfloat16),
        input_output_aliases={5: 0} if held else {},
        compiler_params=pltpu.CompilerParams(vmem_limit_bytes=VMEM_BYTES),
        cost_estimate=LONG,
        name="attention_backward",
    )(in_hbm(qkv), in_hbm(grad_mine), grad_other, in_hbm(main_probs), in_hbm(slot_probs), *map(in_hbm, held))


def grad_out_kernel(sizes, split, total, info, turned, turned_other, *refs):
    mine, other, columns, tall, mine_rows, other_rows, in_sems, out_sems = refs[-8:]
    count, depth, rows = mine_rows.shape
    core = info[0]
    at = pl.ds(pl.multiple_of(core * (total - split), LANE), split)
    loads = [
        pltpu.make_async_copy(source.at[at], columns.at[i], in_sems.at[i]) for i, source in enumerate((turned, turned_other))
    ]
    index = 0
    for j, size in enumerate(sizes):
        first = 0
        for piece in refs[index:index + size]:
            target = tall.at[j] if size == 1 else tall.at[j, pl.ds(first, piece.shape[0])]
            loads.append(pltpu.make_async_copy(piece, target, in_sems.at[len(loads)]))
            first += piece.shape[0]
        index += size
    for load in loads:
        load.start()
    for load in loads:
        load.wait()

    @pl.when(core == 1)
    def _():
        shared = 2 * split - total
        columns[:, :shared, :] = jnp.zeros((2, shared, columns.shape[2]), jnp.bfloat16)

    stores = []
    for i, (result, out) in enumerate(((mine_rows, mine), (other_rows, other))):
        if depth % 16 == 0:
            product = dot(tall[...].reshape(count * depth, split), columns[i], 1, 0)[:, :rows]
            result[...] = product.astype(result.dtype).reshape(count, depth, rows)
        else:
            for j in range(count):
                result[j] = dot(tall[j], columns[i], 1, 0)[:, :rows].astype(result.dtype)
        for j in range(count):
            stores.append(pltpu.make_async_copy(result.at[j], out.at[info[1 + j]], out_sems.at[i, j]))
            stores[-1].start()
    for store in stores:
        store.wait()


def grad_out_rows(info, turned, turned_other, rows, pieces, shards, held):
    total, lanes = turned.shape
    split = pieces[0][0].shape[1]
    depth = sum(p.shape[0] for p in pieces[0])
    sizes = [len(p) for p in pieces]
    arrays = [a for p in pieces for a in p]
    count = len(pieces)
    held = [] if held is None else list(held)
    return pl.pallas_call(
        functools.partial(grad_out_kernel, sizes, split, total),
        grid_spec=pltpu.PrefetchScalarGridSpec(
            num_scalar_prefetch=1,
            grid=(1,),
            in_specs=[pl.BlockSpec(memory_space=pl.ANY)] * (2 + len(arrays) + len(held)),
            out_specs=[pl.BlockSpec(memory_space=pl.ANY)] * 2,
            scratch_shapes=[
                pltpu.VMEM((2, split, lanes), jnp.bfloat16),
                pltpu.VMEM((count, depth, split), jnp.bfloat16),
                pltpu.VMEM((count, depth, rows), jnp.float32),
                pltpu.VMEM((count, depth, rows), jnp.bfloat16),
                pltpu.SemaphoreType.DMA((2 + len(arrays),)),
                pltpu.SemaphoreType.DMA((2, count)),
            ],
        ),
        out_shape=[
            pltpu.HBM((shards, depth, rows), jnp.float32),
            pltpu.HBM((shards, depth, rows), jnp.bfloat16),
        ],
        input_output_aliases={3 + len(arrays) + i: i for i in range(len(held))},
        compiler_params=pltpu.CompilerParams(vmem_limit_bytes=VMEM_BYTES),
        cost_estimate=LONG,
        name="grad_out_rows",
    )(info, turned, turned_other, *arrays, *map(in_hbm, held))


def half_kernel(starts, weight, out, sem):
    copy = pltpu.make_async_copy(weight.at[:, pl.ds(pl.multiple_of(starts[0], LANE), out.shape[1])], out, sem)
    copy.start()
    copy.wait()


def half_columns(start, weight, width):
    return pl.pallas_call(
        half_kernel,
        grid_spec=pltpu.PrefetchScalarGridSpec(
            num_scalar_prefetch=1,
            grid=(1,),
            in_specs=[pl.BlockSpec(memory_space=pl.ANY)],
            out_specs=pl.BlockSpec(memory_space=pl.ANY),
            scratch_shapes=[pltpu.SemaphoreType.DMA],
        ),
        out_shape=jax.ShapeDtypeStruct((weight.shape[0], width), weight.dtype),
        compiler_params=pltpu.CompilerParams(vmem_limit_bytes=VMEM_BYTES),
        cost_estimate=SHORT,
        name="own_half_of_weight",
    )(start, weight)


def finish_kernel(offsets, start, term, came_up, came_down, out):
    total = term[...] + came_up[...].astype(jnp.float32) + came_down[...].astype(jnp.float32)
    for offset in offsets:

        @pl.when(start[0] == offset)
        def _():
            out[...] = total[:, offset:offset + out.shape[1]]


def finish(start, term, came_up, came_down, owned, offsets):
    depth, window = term.shape
    block = pl.BlockSpec((depth, window), lambda i, s: (0, 0))
    return pl.pallas_call(
        functools.partial(finish_kernel, offsets),
        grid_spec=pltpu.PrefetchScalarGridSpec(
            num_scalar_prefetch=1,
            grid=(1,),
            in_specs=[block] * 3,
            out_specs=pl.BlockSpec((depth, owned), lambda i, s: (0, 0)),
        ),
        out_shape=jax.ShapeDtypeStruct((depth, owned), jnp.float32),
        compiler_params=pltpu.CompilerParams(vmem_limit_bytes=VMEM_BYTES),
        cost_estimate=SHORT,
        name="last_sum",
    )(start, term, came_up, came_down)


def partial_kernel(sources, count, window, order, starts, *refs):
    attended, columns = refs[:sources], refs[sources:2 * sources]
    outs, (chunks, held, sems) = refs[2 * sources:-3], refs[-3:]
    depth = chunks.shape[2]
    copies = []
    for i in range(sources):
        at = pl.ds(pl.multiple_of(starts[min(i // 2, 1)], LANE), window)
        some = [pltpu.make_async_copy(columns[i].at[:, at], held.at[i], sems.at[i, count])]
        for j in range(count):
            source = attended[i].at[order[j] if i < 2 else j]
            some.append(pltpu.make_async_copy(source, chunks.at[i, j], sems.at[i, j]))
        copies.append(some)
    for some in copies:
        for copy in some:
            copy.start()
    together = depth % 16 == 0
    for i, some in enumerate(copies):
        for copy in some:
            copy.wait()
        if together:
            product = dot(chunks[i].reshape(count * depth, chunks.shape[3]), held[i], 1, 0)
        for j, out in enumerate(outs):
            part = product[j * depth:(j + 1) * depth] if together else dot(chunks[i, j], held[i], 1, 0)
            if i == 0:
                out[...] = part
            else:
                out[...] += part


def partial_products(order, starts, attended, columns, window):
    _, depth, rows = attended[0].shape
    count, sources = order.shape[0], len(attended)
    return pl.pallas_call(
        functools.partial(partial_kernel, sources, count, window),
        grid_spec=pltpu.PrefetchScalarGridSpec(
            num_scalar_prefetch=2,
            grid=(1,),
            in_specs=[pl.BlockSpec(memory_space=pl.ANY)] * (2 * sources),
            out_specs=[pl.BlockSpec((depth, window), lambda j, o, s: (0, 0))] * count,
            scratch_shapes=[
                pltpu.VMEM((sources, count, depth, rows), jnp.bfloat16),
                pltpu.VMEM((sources, rows, window), jnp.bfloat16),
                pltpu.SemaphoreType.DMA((sources, count + 1)),
            ],
        ),
        out_shape=[jax.ShapeDtypeStruct((depth, window), jnp.float32)] * count,
        compiler_params=pltpu.CompilerParams(vmem_limit_bytes=VMEM_BYTES),
        cost_estimate=LONG,
        name="projection_partial",
    )(order, starts, *attended, *columns)


def windows_of(groups, owned, total):
    lows = [g * owned // LANE * LANE for g in range(groups)]
    width = max(-(-((g + 1) * owned) // LANE) * LANE - low for g, low in enumerate(lows))
    return width


def ring_of(count):
    return list(range(0, count, 2)) + list(range(count - 1, 0, -2))


def local(members, shards, query_key_value, cotangent, proj_weight, layer_scale, lengths):
    member = lax.axis_index("dp")
    shard = lax.axis_index("fsdp")
    core, chip, peers = member % 2, member // 2, members // 2
    ring = ring_of(shards)
    place = jnp.where(shard % 2 == 0, shard // 2, shards - 1 - shard // 2)
    ahead = [(ring[i], ring[(i + 1) % shards]) for i in range(shards)]
    behind = [(ring[i], ring[(i - 1) % shards]) for i in range(shards)]
    half = shards // 2
    depth, total = proj_weight.shape
    rows, width = query_key_value.shape[1:]
    owned = total // members
    counts = lax.dynamic_index_in_dim(lengths[:, 0, :], member, 0, keepdims=False)

    def swap(array, bit):
        return lax.ppermute(array, "dp", [(i, i ^ bit) for i in range(members)])

    def shard_at(offset):
        at = (place + offset + shards) % shards
        return jnp.where(at < half, 2 * at, 2 * (shards - 1 - at) + 1)

    def table(values):
        return jnp.stack([jnp.asarray(v) for v in values]).astype(jnp.int32)

    chip_width, window = windows_of(peers, 2 * owned, total), windows_of(members, owned, total)

    def chip_start(chip):
        return jnp.minimum(chip * 2 * owned // LANE * LANE, total - chip_width)

    my_start = jnp.minimum(member * owned // LANE * LANE, chip_start(chip) + chip_width - window)
    starts = table([my_start, my_start - chip_start(chip)])

    split = -(-(total // LANE) // 2) * LANE
    mine = half_columns(table([core * (total - split)]), proj_weight, split)
    cut = -(-depth // 32) * 16
    up, down = [mine], [mine]
    up.append(lax.ppermute(up[-1], "fsdp", ahead))
    down.append(lax.ppermute(down[-1], "fsdp", behind))

    mine, cotangent = lax.optimization_barrier((mine, cotangent))
    scaled, turned, *sent = prepare(
        table([chip_start(chip ^ k) for k in range(1, peers)] or [0]), cotangent, layer_scale, peers - 1, chip_width
    )
    columns = [scaled, swap(scaled, 1)]
    turned_other = swap(turned, 1)
    attended, main_probs, slot_probs = forward(counts, query_key_value)
    attended = attended.reshape(shards, depth, rows)
    near = [[o, -o] for o in range(half - 1, 0, -1)]
    groups = [[half] + near[0]] + near[1:-1] + [near[-1] + [0]]
    came_columns = [swap(sent[k - 1], 2 * k) for k in range(1, peers)]
    flat = table([shard_at(o) for group in groups for o in group])
    sizes = [len(group) for group in groups]
    orders = [flat[sum(sizes[:g]):sum(sizes[:g + 1])] for g in range(len(groups))]
    chunks = list(arrange(flat, attended, sizes))
    came = [[swap(chunks[0], 2 * k) for k in range(1, peers)]]

    def rows_of(some, held):
        info = table([core] + [shard_at(o) for _, o in some])
        return grad_out_rows(info, turned, turned_other, rows, [p for p, _ in some], shards, held)

    up[1], down[1], attended = lax.optimization_barrier((up[1], down[1], attended))
    both = [attended, swap(attended, 1)]
    for _ in range(half - 3):
        up.append(lax.ppermute(up[-1], "fsdp", ahead))
        down.append(lax.ppermute(down[-1], "fsdp", behind))
    up[-1], down[-1], columns[1], turned_other = lax.optimization_barrier((up[-1], down[-1], columns[1], turned_other))
    came_columns, near_up, near_down, chunks = lax.optimization_barrier((came_columns, up[-1], down[-1], chunks))
    came.append([swap(chunks[1], 2 * k) for k in range(1, peers)])
    pieces = [([mine], 0)]
    for step in range(1, half - 1):
        last = step == half - 2
        pieces += [([near_up if last else up[step]], -step), ([near_down if last else down[step]], step)]
    grad_out = rows_of(pieces, None)
    for c in came_columns:
        columns += [c, swap(c, 1)]
    up.append(lax.ppermute(up[-1], "fsdp", ahead))
    down.append(lax.ppermute(down[-1], "fsdp", behind))
    up[-1], down[-1], grad_out, both[1] = lax.optimization_barrier((up[-1], down[-1], grad_out, both[1]))
    came[0], near_up, near_down = lax.optimization_barrier((came[0], up[-1], down[-1]))
    far_up = lax.ppermute(up[-1][:cut], "fsdp", ahead)
    far_down = lax.ppermute(down[-1][cut:], "fsdp", behind)

    def products(index):
        taken = list(both)
        for c in came[index]:
            taken += [c, swap(c, 1)]
        result = partial_products(orders[index], starts, taken, columns, window)
        return {o: result[j] for j, o in enumerate(groups[index])}

    terms = products(0)
    first = terms[half].astype(jnp.bfloat16)
    far_up, far_down, terms, chunks = lax.optimization_barrier((far_up, far_down, terms, chunks))
    came += [[swap(some, 2 * k) for k in range(1, peers)] for some in chunks[2:]]
    going_up, going_down = first[:cut], first[cut:]
    came_up = lax.ppermute(going_up, "fsdp", ahead)
    came_down = lax.ppermute(going_down, "fsdp", behind)

    grad_out = rows_of([([near_up], 1 - half), ([near_down], half - 1), ([far_up, far_down], half)], grad_out)
    grad_mine = grad_out[0].reshape(width, rows)
    grad_other = swap(grad_out[1], 1).reshape(width, rows)
    pairs = -(-(width // HS) // PAIR)
    bounds = [0, 3, 5, pairs]

    def back(index, held):
        return backward(
            query_key_value, grad_mine, grad_other, main_probs, slot_probs, bounds[index], bounds[index + 1], held
        )

    grads = None
    for step in range(half, 1, -1):
        if step == half:
            came_up = jnp.pad(came_up, ((0, depth - cut), (0, 0)))
            came_down = jnp.pad(came_down, ((cut, 0), (0, 0)))
        else:
            terms.update(products(half - step))
        going_up = (terms[step - 1] + came_up.astype(jnp.float32)).astype(jnp.bfloat16)
        going_down = (terms[1 - step] + came_down.astype(jnp.float32)).astype(jnp.bfloat16)
        beside = []
        if step > 2:
            beside.append(came[half - step + 1])
        if step == 3:
            beside.append(grad_mine)
        if step == 2:
            grads = back(0, grads)
            beside.append(grads)
        going_up, going_down, *beside = lax.optimization_barrier((going_up, going_down, *beside))
        if step > 2:
            came[half - step + 1] = beside[0]
        if step == 3:
            grad_mine = beside[1]
        if step == 2:
            grads = beside[0]
        came_up = lax.ppermute(going_up, "fsdp", ahead)
        came_down = lax.ppermute(going_down, "fsdp", behind)
    grads = back(2, back(1, grads))
    came_up, came_down, grads = lax.optimization_barrier((came_up, came_down, grads))
    offsets = set()
    for m in range(members):
        low = min((m // 2) * 2 * owned // LANE * LANE, total - chip_width)
        offsets.add(m * owned - min(m * owned // LANE * LANE, low + chip_width - window))
    grad_proj = finish(table([member * owned - my_start]), terms[0], came_up, came_down, owned, sorted(offsets))
    return grads, grad_proj


def solution(mesh):
    members, shards = mesh.shape["dp"], mesh.shape["fsdp"]
    placed = (
        P(None, ("dp", "fsdp"), None),
        P(("dp", "fsdp"), None),
        P("fsdp", None),
        P(),
        P(None, "fsdp", None),
    )
    return jax.shard_map(
        functools.partial(local, members, shards),
        mesh=mesh,
        in_specs=placed,
        out_specs=(P(None, ("dp", "fsdp"), None), P("fsdp", "dp")),
        check_vma=False,
    )
```

```python
import functools

import jax
import jax.numpy as jnp
from jax import lax
from jax.experimental import pallas as pl
from jax.experimental.pallas import tpu as pltpu
from jax.sharding import PartitionSpec as P

HS = 128
MAIN = 256
SLOT = 96
LANE = 128
FACTOR = HS ** (-0.5)
VMEM_BYTES = 20 * 1024 * 1024


def lasting(microseconds):
    return pl.CostEstimate(flops=int(microseconds * 575000000), bytes_accessed=1000, transcendentals=0)


def dot(left, right, left_dim, right_dim):
    return lax.dot_general(left, right, (((left_dim,), (right_dim,)), ((), ())), preferred_element_type=jnp.float32)


def in_hbm(array):
    return pltpu.with_memory_space_constraint(array, pltpu.HBM)


def window_kernel(peers, starts, cotangent, layer_scale, *refs):
    windows, (held, sems) = refs[:-2], refs[-2:]
    parts = len(windows) // peers
    width = held.shape[2]
    copies = []
    for k in range(peers):
        at = pl.ds(pl.multiple_of(starts[k], LANE), width)
        first = 0
        for part in range(parts):
            rows = pl.ds(first, windows[part].shape[0])
            copies.append(pltpu.make_async_copy(cotangent.at[rows, at], held.at[k, rows], sems.at[k, part]))
            first += windows[part].shape[0]
    for copy in copies:
        copy.start()
    for k in range(peers):
        scale = layer_scale[:, pl.ds(pl.multiple_of(starts[k], LANE), width)]
        first = 0
        for part in range(parts):
            copies[k * parts + part].wait()
            window = windows[k * parts + part]
            values = held[k, first:first + window.shape[0], :].astype(jnp.float32)
            window[...] = (values * scale).astype(jnp.bfloat16)
            first += window.shape[0]


def peer_windows(starts, cotangent, layer_scale, peers, width):
    rows, total = cotangent.shape
    parts = (rows // 48 * 16 + 16, rows - rows // 48 * 16 - 16)
    arrays = pl.pallas_call(
        functools.partial(window_kernel, peers),
        grid_spec=pltpu.PrefetchScalarGridSpec(
            num_scalar_prefetch=1,
            grid=(1,),
            in_specs=[pl.BlockSpec(memory_space=pl.ANY), pl.BlockSpec((1, total), lambda i, s: (0, 0))],
            out_specs=[pl.BlockSpec((part, width), lambda i, s: (0, 0)) for part in parts] * peers,
            scratch_shapes=[
                pltpu.VMEM((peers, rows, width), jnp.bfloat16),
                pltpu.SemaphoreType.DMA((peers, len(parts))),
            ],
        ),
        out_shape=[pltpu.HBM((part, width), jnp.bfloat16) for part in parts] * peers,
        compiler_params=pltpu.CompilerParams(vmem_limit_bytes=VMEM_BYTES),
        cost_estimate=lasting(60),
        name="peer_windows",
    )(starts, in_hbm(cotangent), layer_scale)
    return [arrays[part::len(parts)] for part in range(len(parts))]


def prepare_kernel(cotangent, layer_scale, turned):
    values = (cotangent[...].astype(jnp.float32) * layer_scale[...]).astype(jnp.bfloat16)
    spare = jnp.zeros((turned.shape[1] - values.shape[0], values.shape[1]), jnp.bfloat16)
    turned[...] = jnp.concatenate([values, spare], axis=0).T


def prepare(cotangent, layer_scale):
    rows, total = cotangent.shape
    lanes = -(-rows // LANE) * LANE
    steps = 5
    block = total // steps
    return pl.pallas_call(
        prepare_kernel,
        grid=(steps,),
        in_specs=[pl.BlockSpec((rows, block), lambda i: (0, i)), pl.BlockSpec((1, block), lambda i: (0, i))],
        out_specs=pl.BlockSpec((block, lanes), lambda i: (i, 0)),
        out_shape=pltpu.HBM((total, lanes), jnp.bfloat16),
        compiler_params=pltpu.CompilerParams(vmem_limit_bytes=VMEM_BYTES),
        cost_estimate=lasting(60),
        name="scaled_cotangent",
    )(in_hbm(cotangent), layer_scale)


def arrange_kernel(sizes, order, attended, *refs):
    *outs, sems = refs
    copies = []
    for out, size in zip(outs, sizes):
        for j in range(size):
            n = len(copies)
            copies.append(pltpu.make_async_copy(attended.at[order[n]], out.at[j], sems.at[n]))
    for copy in copies:
        copy.start()
    for copy in copies:
        copy.wait()


def arrange(order, attended, sizes):
    _, depth, rows = attended.shape
    return pl.pallas_call(
        functools.partial(arrange_kernel, sizes),
        grid_spec=pltpu.PrefetchScalarGridSpec(
            num_scalar_prefetch=1,
            grid=(1,),
            in_specs=[pl.BlockSpec(memory_space=pl.ANY)],
            out_specs=[pl.BlockSpec((size, depth, rows), lambda i, o: (0, 0, 0)) for size in sizes],
            scratch_shapes=[pltpu.SemaphoreType.DMA((sum(sizes),))],
        ),
        out_shape=[jax.ShapeDtypeStruct((size, depth, rows), attended.dtype) for size in sizes],
        compiler_params=pltpu.CompilerParams(vmem_limit_bytes=VMEM_BYTES),
        cost_estimate=lasting(2),
        name="attended_chunks",
    )(order, in_hbm(attended))


def far_kernel(up, down, out_up, out_down, sems):
    cut = out_up.shape[0]
    copies = [
        pltpu.make_async_copy(up.at[pl.ds(0, cut)], out_up, sems.at[0]),
        pltpu.make_async_copy(down.at[pl.ds(cut, out_down.shape[0])], out_down, sems.at[1]),
    ]
    for copy in copies:
        copy.start()
    for copy in copies:
        copy.wait()


def far_parts(up, down, cut):
    depth, width = up.shape
    sizes = (cut, depth - cut)
    return pl.pallas_call(
        far_kernel,
        grid=(1,),
        in_specs=[pl.BlockSpec(memory_space=pl.ANY)] * 2,
        out_specs=[pl.BlockSpec((size, width), lambda i: (0, 0)) for size in sizes],
        out_shape=[jax.ShapeDtypeStruct((size, width), up.dtype) for size in sizes],
        scratch_shapes=[pltpu.SemaphoreType.DMA((2,))],
        compiler_params=pltpu.CompilerParams(vmem_limit_bytes=VMEM_BYTES),
        cost_estimate=lasting(1),
        name="far_parts",
    )(up, down)


PAIR = 2
EXPONENT = FACTOR * 1.4426950408889634


def forward_kernel(counts, qkv, attended, main_probs, slot_probs):
    def marks(image, ids):
        lane = lax.broadcasted_iota(jnp.int32, (image.shape[0], HS), 1)
        first = jnp.where(image == ids[0], 1.0, 0.0)
        second = jnp.where(image == ids[1], 1.0, 0.0)
        own = jnp.where(lane == 0, first, jnp.where(lane == 1, second, 0.0))
        other = jnp.where(lane == 0, 1.0 - first, jnp.where(lane == 1, 1.0 - second, 0.0)) * -1e30
        return own.astype(jnp.bfloat16), other.astype(jnp.bfloat16)

    main_at = lax.broadcasted_iota(jnp.int32, (MAIN, HS), 0)
    main_marks = marks(jnp.where(main_at >= counts[0], 1, 0), (0, 1))

    def image(at):
        first = jnp.where(at < counts[2], 2, -1)
        return jnp.where(at < SLOT, first, jnp.where(at - SLOT < counts[3], 3, -1))

    slot_marks = marks(image(lax.broadcasted_iota(jnp.int32, (2 * SLOT, HS), 0)), (2, 3))
    valid = image(lax.broadcasted_iota(jnp.int32, (1, 2 * SLOT), 1)) >= 0
    parts = []
    for head in range(PAIR):
        lanes = slice(head * HS, (head + 1) * HS)
        parts.append((head, 0, MAIN, lanes, main_marks, None, main_probs))
        parts.append((head, MAIN, 2 * SLOT, lanes, slot_marks, valid, slot_probs))
    scores = []
    for head, first, rows, lanes, (mark_query, mark_key), _, _ in parts:
        query = jnp.concatenate([qkv[0, first:first + rows, lanes], mark_query], axis=1)
        key = jnp.concatenate([qkv[1, first:first + rows, lanes], mark_key], axis=1)
        scores.append(dot(key, query, 1, 1))
    probs = []
    for score, (_, _, _, _, _, good, _) in zip(scores, parts):
        weights = jnp.exp2((score - jnp.max(score, axis=0, keepdims=True)) * EXPONENT)
        scale = 1.0 / jnp.sum(weights, axis=0, keepdims=True)
        probs.append(weights * (scale if good is None else jnp.where(good, scale, 0.0)))
    for prob, (head, first, rows, lanes, _, _, probs_ref) in zip(probs, parts):
        probs_ref[head] = prob
        result = dot(qkv[2, first:first + rows, lanes], prob.astype(jnp.bfloat16), 0, 0)
        attended[lanes, first:first + rows] = result.astype(jnp.bfloat16)


def forward(counts, qkv):
    _, rows, width = qkv.shape
    heads = width // HS
    return pl.pallas_call(
        forward_kernel,
        grid_spec=pltpu.PrefetchScalarGridSpec(
            num_scalar_prefetch=1,
            grid=(-(-heads // PAIR),),
            in_specs=[pl.BlockSpec((3, rows, PAIR * HS), lambda h, c: (0, 0, h))],
            out_specs=[
                pl.BlockSpec((PAIR * HS, rows), lambda h, c: (h, 0)),
                pl.BlockSpec((PAIR, MAIN, MAIN), lambda h, c: (h, 0, 0)),
                pl.BlockSpec((PAIR, 2 * SLOT, 2 * SLOT), lambda h, c: (h, 0, 0)),
            ],
        ),
        out_shape=[
            pltpu.HBM((width, rows), jnp.bfloat16),
            pltpu.HBM((heads, MAIN, MAIN), jnp.float32),
            pltpu.HBM((heads, 2 * SLOT, 2 * SLOT), jnp.float32),
        ],
        compiler_params=pltpu.CompilerParams(vmem_limit_bytes=VMEM_BYTES),
        cost_estimate=lasting(60),
        name="attention_forward",
    )(counts, qkv)


def backward_kernel(qkv, grad_mine, grad_other, main_probs, slot_probs, *rest):
    grads = rest[-1]
    parts = []
    for head in range(PAIR):
        lanes = slice(head * HS, (head + 1) * HS)
        for first, rows, probs_ref in ((0, MAIN, main_probs), (MAIN, 2 * SLOT, slot_probs)):
            parts.append((head, slice(first, first + rows), lanes, probs_ref))
    grad, dprobs, dscores = [], [], []
    for head, at, lanes, _ in parts:
        both = grad_mine[lanes, at] + grad_other[lanes, at].astype(jnp.float32)
        grad.append(both.astype(jnp.bfloat16))
    for g, (head, at, lanes, _) in zip(grad, parts):
        dprobs.append(dot(qkv[2, at, lanes], g, 1, 0))
    for g, (head, at, lanes, probs_ref) in zip(grad, parts):
        grads[2, at, lanes] = dot(probs_ref[head].astype(jnp.bfloat16), g, 1, 1).astype(jnp.bfloat16)
    for dprob, (head, at, lanes, probs_ref) in zip(dprobs, parts):
        probs = probs_ref[head]
        delta = jnp.sum(probs * dprob, axis=0, keepdims=True)
        dscores.append((probs * (dprob - delta) * FACTOR).astype(jnp.bfloat16))
    for dscore, (head, at, lanes, _) in zip(dscores, parts):
        grads[1, at, lanes] = dot(dscore, qkv[0, at, lanes], 1, 0).astype(jnp.bfloat16)
        grads[0, at, lanes] = dot(dscore, qkv[1, at, lanes], 0, 0).astype(jnp.bfloat16)


def backward(qkv, grad_mine, grad_other, main_probs, slot_probs, low, high, grads):
    _, rows, width = qkv.shape
    held = [] if grads is None else [grads]
    return pl.pallas_call(
        backward_kernel,
        grid=(high - low,),
        in_specs=[
            pl.BlockSpec((3, rows, PAIR * HS), lambda h: (0, 0, h + low)),
            pl.BlockSpec((PAIR * HS, rows), lambda h: (h + low, 0)),
            pl.BlockSpec((PAIR * HS, rows), lambda h: (h + low, 0)),
            pl.BlockSpec((PAIR, MAIN, MAIN), lambda h: (h + low, 0, 0)),
            pl.BlockSpec((PAIR, 2 * SLOT, 2 * SLOT), lambda h: (h + low, 0, 0)),
        ] + [pl.BlockSpec(memory_space=pl.ANY)] * len(held),
        out_specs=pl.BlockSpec((3, rows, PAIR * HS), lambda h: (0, 0, h + low)),
        out_shape=pltpu.HBM(qkv.shape, jnp.bfloat16),
        input_output_aliases={5: 0} if held else {},
        compiler_params=pltpu.CompilerParams(vmem_limit_bytes=VMEM_BYTES),
        cost_estimate=lasting(2 * (high - low)),
        name="attention_backward",
    )(qkv, grad_mine, grad_other, main_probs, slot_probs, *map(in_hbm, held))


def grad_out_kernel(sizes, split, total, info, turned, turned_other, *refs):
    mine, other, columns, tall, mine_rows, other_rows, in_sems, out_sems = refs[-8:]
    count, depth, rows = mine_rows.shape
    core = info[0]
    at = pl.ds(pl.multiple_of(core * (total - split), LANE), split)
    loads = [
        pltpu.make_async_copy(source.at[at], columns.at[i], in_sems.at[i]) for i, source in enumerate((turned, turned_other))
    ]
    index = 0
    for j, size in enumerate(sizes):
        first = 0
        for piece in refs[index:index + size]:
            target = tall.at[j] if size == 1 else tall.at[j, pl.ds(first, piece.shape[0])]
            loads.append(pltpu.make_async_copy(piece, target, in_sems.at[len(loads)]))
            first += piece.shape[0]
        index += size
    for load in loads:
        load.start()
    for load in loads:
        load.wait()

    @pl.when(core == 1)
    def _():
        shared = 2 * split - total
        columns[:, :shared, :] = jnp.zeros((2, shared, columns.shape[2]), jnp.bfloat16)

    stores = []
    for i, (result, out) in enumerate(((mine_rows, mine), (other_rows, other))):
        if depth % 16 == 0:
            product = dot(tall[...].reshape(count * depth, split), columns[i], 1, 0)[:, :rows]
            result[...] = product.astype(result.dtype).reshape(count, depth, rows)
        else:
            for j in range(count):
                result[j] = dot(tall[j], columns[i], 1, 0)[:, :rows].astype(result.dtype)
        for j in range(count):
            stores.append(pltpu.make_async_copy(result.at[j], out.at[info[1 + j]], out_sems.at[i, j]))
            stores[-1].start()
    for store in stores:
        store.wait()


def grad_out_rows(info, turned, turned_other, rows, pieces, shards, held, after=()):
    total, lanes = turned.shape
    split = pieces[0][0].shape[1]
    depth = sum(p.shape[0] for p in pieces[0])
    sizes = [len(p) for p in pieces]
    arrays = [a for p in pieces for a in p]
    count = len(pieces)
    held = [] if held is None else list(held)
    return pl.pallas_call(
        functools.partial(grad_out_kernel, sizes, split, total),
        grid_spec=pltpu.PrefetchScalarGridSpec(
            num_scalar_prefetch=1,
            grid=(1,),
            in_specs=[pl.BlockSpec(memory_space=pl.ANY)] * (2 + len(arrays) + len(held) + len(after)),
            out_specs=[pl.BlockSpec(memory_space=pl.ANY)] * 2,
            scratch_shapes=[
                pltpu.VMEM((2, split, lanes), jnp.bfloat16),
                pltpu.VMEM((count, depth, split), jnp.bfloat16),
                pltpu.VMEM((count, depth, rows), jnp.float32),
                pltpu.VMEM((count, depth, rows), jnp.bfloat16),
                pltpu.SemaphoreType.DMA((2 + len(arrays),)),
                pltpu.SemaphoreType.DMA((2, count)),
            ],
        ),
        out_shape=[
            pltpu.HBM((shards, depth, rows), jnp.float32),
            pltpu.HBM((shards, depth, rows), jnp.bfloat16),
        ],
        input_output_aliases={3 + len(arrays) + i: i for i in range(len(held))},
        compiler_params=pltpu.CompilerParams(vmem_limit_bytes=VMEM_BYTES),
        cost_estimate=lasting(0.2 if held else 1.5 * len(pieces)),
        name="grad_out_rows",
    )(info, in_hbm(turned), turned_other, *arrays, *map(in_hbm, held), *after)


def half_kernel(starts, weight, out, sem):
    copy = pltpu.make_async_copy(weight.at[:, pl.ds(pl.multiple_of(starts[0], LANE), out.shape[1])], out, sem)
    copy.start()
    copy.wait()


def half_columns(start, weight, width):
    return pl.pallas_call(
        half_kernel,
        grid_spec=pltpu.PrefetchScalarGridSpec(
            num_scalar_prefetch=1,
            grid=(1,),
            in_specs=[pl.BlockSpec(memory_space=pl.ANY)],
            out_specs=pl.BlockSpec(memory_space=pl.ANY),
            scratch_shapes=[pltpu.SemaphoreType.DMA],
        ),
        out_shape=jax.ShapeDtypeStruct((weight.shape[0], width), weight.dtype),
        compiler_params=pltpu.CompilerParams(vmem_limit_bytes=VMEM_BYTES),
        cost_estimate=lasting(1),
        name="own_half_of_weight",
    )(start, in_hbm(weight))


def finish_kernel(offsets, start, term, came_up, came_down, out):
    total = term[...] + came_up[...].astype(jnp.float32) + came_down[...].astype(jnp.float32)
    for offset in offsets:

        @pl.when(start[0] == offset)
        def _():
            out[...] = total[:, offset:offset + out.shape[1]]


def finish(start, term, came_up, came_down, owned, offsets):
    depth, window = term.shape
    block = pl.BlockSpec((depth, window), lambda i, s: (0, 0))
    return pl.pallas_call(
        functools.partial(finish_kernel, offsets),
        grid_spec=pltpu.PrefetchScalarGridSpec(
            num_scalar_prefetch=1,
            grid=(1,),
            in_specs=[block] * 3,
            out_specs=pl.BlockSpec((depth, owned), lambda i, s: (0, 0)),
        ),
        out_shape=jax.ShapeDtypeStruct((depth, owned), jnp.float32),
        compiler_params=pltpu.CompilerParams(vmem_limit_bytes=VMEM_BYTES),
        cost_estimate=lasting(2),
        name="last_sum",
    )(start, term, came_up, came_down)


def partial_kernel(chosen, sources, parts, count, window, order, start, *refs):
    attended, columns = refs[:sources], refs[sources:sources * (1 + parts)]
    chunks, held, sems = refs[-3:]
    bases = refs[sources * (1 + parts):-3 - count]
    outs = refs[-3 - count:-3]
    depth, rows = chunks.shape[2:]
    at = pl.ds(pl.multiple_of(start[0], LANE), window)
    copies = []
    for i in range(sources):
        some, first = [], 0
        for part in range(parts):
            source = columns[i * parts + part]
            if chosen:
                some.append(pltpu.make_async_copy(source.at[at], held.at[i], sems.at[i, count + part]))
            else:
                target = held.at[i, pl.ds(first, source.shape[0])]
                some.append(pltpu.make_async_copy(source.at[:, at], target, sems.at[i, count + part]))
            first += source.shape[0]
        for j in range(count):
            source = attended[i].at[order[j] if chosen else j]
            some.append(pltpu.make_async_copy(source, chunks.at[i, j], sems.at[i, j]))
        copies.append(some)
    for some in copies:
        for copy in some:
            copy.start()
    together = depth % 16 == 0
    for i, some in enumerate(copies):
        for copy in some:
            copy.wait()
        if together:
            tall = chunks[i].reshape(count * depth, rows)
            product = dot(tall, held[i][:, :rows], 1, 1) if chosen else dot(tall, held[i], 1, 0)
        for j, out in enumerate(outs):
            if together:
                part = product[j * depth:(j + 1) * depth]
            else:
                part = dot(chunks[i, j], held[i][:, :rows], 1, 1) if chosen else dot(chunks[i, j], held[i], 1, 0)
            if i == 0:
                out[...] = bases[j][...] + part if bases else part
            else:
                out[...] += part


def partial_products(order, start, attended, columns, window, bases=()):
    _, depth, rows = attended[0].shape
    parts = len(columns) // len(attended)
    count, sources = order.shape[0], len(attended)
    block = pl.BlockSpec((depth, window), lambda j, o, s: (0, 0))
    return pl.pallas_call(
        functools.partial(partial_kernel, not bases, sources, parts, count, window),
        grid_spec=pltpu.PrefetchScalarGridSpec(
            num_scalar_prefetch=2,
            grid=(1,),
            in_specs=[pl.BlockSpec(memory_space=pl.ANY)] * (sources * (1 + parts)) + [block] * len(bases),
            out_specs=[block] * count,
            scratch_shapes=[
                pltpu.VMEM((sources, count, depth, rows), jnp.bfloat16),
                pltpu.VMEM((sources, rows, window) if bases else (sources, window, columns[0].shape[1]), jnp.bfloat16),
                pltpu.SemaphoreType.DMA((sources, count + parts)),
            ],
        ),
        out_shape=[(jax.ShapeDtypeStruct if bases else pltpu.HBM)((depth, window), jnp.float32)] * count,
        compiler_params=pltpu.CompilerParams(vmem_limit_bytes=VMEM_BYTES),
        cost_estimate=lasting(0.2 if bases else 6),
        name="projection_peers" if bases else "projection_chip",
    )(order, start, *attended, *columns, *map(in_hbm, bases))


def windows_of(groups, owned, total):
    lows = [g * owned // LANE * LANE for g in range(groups)]
    width = max(-(-((g + 1) * owned) // LANE) * LANE - low for g, low in enumerate(lows))
    return width


def ring_of(count):
    return list(range(0, count, 2)) + list(range(count - 1, 0, -2))


def local(members, shards, query_key_value, cotangent, proj_weight, layer_scale, lengths):
    member = lax.axis_index("dp")
    shard = lax.axis_index("fsdp")
    core, chip, peers = member % 2, member // 2, members // 2
    ring = ring_of(shards)
    place = jnp.where(shard % 2 == 0, shard // 2, shards - 1 - shard // 2)
    ahead = [(ring[i], ring[(i + 1) % shards]) for i in range(shards)]
    behind = [(ring[i], ring[(i - 1) % shards]) for i in range(shards)]
    half = shards // 2
    depth, total = proj_weight.shape
    rows, width = query_key_value.shape[1:]
    owned = total // members
    counts = lax.dynamic_index_in_dim(lengths[:, 0, :], member, 0, keepdims=False)

    def swap(array, bit):
        return lax.ppermute(array, "dp", [(i, i ^ bit) for i in range(members)])

    def shard_at(offset):
        at = (place + offset + shards) % shards
        return jnp.where(at < half, 2 * at, 2 * (shards - 1 - at) + 1)

    def table(values):
        return jnp.stack([jnp.asarray(v) for v in values]).astype(jnp.int32)

    chip_width, window = windows_of(peers, 2 * owned, total), windows_of(members, owned, total)

    def chip_start(chip):
        return jnp.minimum(chip * 2 * owned // LANE * LANE, total - chip_width)

    my_start = jnp.minimum(member * owned // LANE * LANE, chip_start(chip) + chip_width - window)
    starts = table([my_start, my_start - chip_start(chip)])

    split = -(-(total // LANE) // 2) * LANE
    mine = half_columns(table([core * (total - split)]), proj_weight, split)
    cut = -(-depth // 32) * 16
    up, down = [mine], [mine]
    up.append(lax.ppermute(up[-1], "fsdp", ahead))
    down.append(lax.ppermute(down[-1], "fsdp", behind))

    mine, cotangent = lax.optimization_barrier((mine, cotangent))
    scales = layer_scale.reshape(1, total)
    sent = peer_windows(
        table([chip_start(chip ^ k) for k in range(1, peers)] or [0]), cotangent, scales, peers - 1, chip_width
    )
    sent, cotangent = lax.optimization_barrier((sent, cotangent))
    came_columns = [[swap(array, 2 * k) for k, array in enumerate(part, 1)] for part in sent]
    turned = prepare(cotangent, scales)
    attended, main_probs, slot_probs = forward(counts, query_key_value)
    attended = attended.reshape(shards, depth, rows)
    near = [[o, -o] for o in range(half - 1, 0, -1)]
    groups = [[half] + near[0]] + near[1:-1] + [near[-1] + [0]]
    flat = table([shard_at(o) for group in groups for o in group])
    sizes = [len(group) for group in groups]
    orders = [flat[sum(sizes[:g]):sum(sizes[:g + 1])] for g in range(len(groups))]

    def rows_of(some, held, after=()):
        info = table([core] + [shard_at(o) for _, o in some])
        return grad_out_rows(info, turned, turned_other, rows, [p for p, _ in some], shards, held, after)

    up[1], down[1], attended, came_columns[0], turned = lax.optimization_barrier(
        (up[1], down[1], attended, came_columns[0], turned)
    )
    turned_other = swap(turned, 1)
    other_columns = [[swap(array, 1) for array in came_columns[0]]]
    attended_other = swap(attended, 1)
    chunks = list(arrange(flat, attended, sizes))
    for _ in range(half - 3):
        up.append(lax.ppermute(up[-1], "fsdp", ahead))
        down.append(lax.ppermute(down[-1], "fsdp", behind))
    up[-1], down[-1], turned_other, attended_other = lax.optimization_barrier(
        (up[-1], down[-1], turned_other, attended_other)
    )

    bases = partial_products(
        flat, starts[:1], [in_hbm(attended), attended_other], [in_hbm(turned), turned_other], window
    )
    late, chunks, *bases = lax.optimization_barrier((came_columns[1], chunks, *bases))
    came = [[swap(chunks[0], 2 * k) for k in range(1, peers)]]
    other_columns.append([swap(array, 1) for array in late])
    came_columns[1] = late
    came.append([swap(chunks[1], 2 * k) for k in range(1, peers)])
    columns = []
    for k in range(peers - 1):
        for arrays in (came_columns, other_columns):
            columns += [part[k] for part in arrays]
    pieces = [([mine], 0)]
    for step in range(1, half - 1):
        pieces += [([up[step]], -step), ([down[step]], step)]
    grad_out = rows_of(pieces, None)
    up.append(lax.ppermute(up[-1], "fsdp", ahead))
    down.append(lax.ppermute(down[-1], "fsdp", behind))
    up[-1], down[-1], grad_out, *bases = lax.optimization_barrier((up[-1], down[-1], grad_out, *bases))
    bases = dict(zip([o for group in groups for o in group], bases))
    if depth % 16 == 0:
        far_up, far_down = far_parts(up[-1], down[-1], cut)
    else:
        far_up, far_down = up[-1][:cut], down[-1][cut:]
    came[0], near_up, near_down, sent_up = lax.optimization_barrier((came[0], up[-1], down[-1], far_up))
    far_up = lax.ppermute(far_up, "fsdp", ahead)
    far_down = lax.ppermute(far_down, "fsdp", behind)

    def both_cores(arrays):
        return [a for c in arrays for a in (c, swap(c, 1))]

    def products(index, taken):
        group = groups[index]
        if not taken:
            return {o: bases[o] for o in group}
        result = partial_products(orders[index], starts[1:], taken, columns, window, [bases[o] for o in group])
        return dict(zip(group, result))

    terms = products(0, both_cores(came[0]))
    first = terms[half].astype(jnp.bfloat16)
    going_up, going_down, came[1], chunks, far_up, far_down = lax.optimization_barrier(
        (first[:cut], first[cut:], came[1], chunks, far_up, far_down)
    )
    came += [[swap(some, 2 * k) for k in range(1, peers)] for some in chunks[2:]]
    taken = both_cores(came[1])
    came_up = lax.ppermute(going_up, "fsdp", ahead)
    came_down = lax.ppermute(going_down, "fsdp", behind)

    bounds = [0, 3, 5, -(-(width // HS) // PAIR)]
    grads = None
    for step in range(half, 1, -1):
        if step == half:
            came_up = jnp.pad(came_up, ((0, depth - cut), (0, 0)))
            came_down = jnp.pad(came_down, ((cut, 0), (0, 0)))
        else:
            terms.update(products(half - step, taken))
        going_up = (terms[step - 1] + came_up.astype(jnp.float32)).astype(jnp.bfloat16)
        going_down = (terms[1 - step] + came_down.astype(jnp.float32)).astype(jnp.bfloat16)
        if step == half:
            going_up, going_down, near_up = lax.optimization_barrier((going_up, going_down, near_up))
            grad_out = rows_of([([near_up], 1 - half), ([near_down], half - 1), ([far_up, far_down], half)], grad_out, [sent_up])
            grad_mine = grad_out[0].reshape(width, rows)
            grad_other = swap(grad_out[1], 1).reshape(width, rows)
        elif step > 2:
            arrived = came[half - step + 1]
            going_up, going_down, arrived, grad_mine = lax.optimization_barrier((going_up, going_down, arrived, grad_mine))
            taken = both_cores(arrived)
        else:
            grads = backward(query_key_value, grad_mine, grad_other, main_probs, slot_probs, bounds[0], bounds[1], grads)
            going_up, going_down, grads = lax.optimization_barrier((going_up, going_down, grads))
        came_up = lax.ppermute(going_up, "fsdp", ahead)
        came_down = lax.ppermute(going_down, "fsdp", behind)
    for low, high in zip(bounds[1:], bounds[2:]):
        grads = backward(query_key_value, grad_mine, grad_other, main_probs, slot_probs, low, high, grads)
    came_up, came_down, grads = lax.optimization_barrier((came_up, came_down, grads))
    offsets = set()
    for m in range(members):
        low = min((m // 2) * 2 * owned // LANE * LANE, total - chip_width)
        offsets.add(m * owned - min(m * owned // LANE * LANE, low + chip_width - window))
    grad_proj = finish(table([member * owned - my_start]), terms[0], came_up, came_down, owned, sorted(offsets))
    return grads, grad_proj


def solution(mesh):
    members, shards = mesh.shape["dp"], mesh.shape["fsdp"]
    placed = (
        P(None, ("dp", "fsdp"), None),
        P(("dp", "fsdp"), None),
        P("fsdp", None),
        P(),
        P(None, "fsdp", None),
    )
    return jax.shard_map(
        functools.partial(local, members, shards),
        mesh=mesh,
        in_specs=placed,
        out_specs=(P(None, ("dp", "fsdp"), None), P("fsdp", "dp")),
        check_vma=False,
    )
```

```python
import functools

import jax
import jax.numpy as jnp
from jax import lax
from jax.experimental import pallas as pl
from jax.experimental.pallas import tpu as pltpu
from jax.sharding import PartitionSpec as P

HS = 128
MAIN = 256
SLOT = 96
LANE = 128
FACTOR = HS ** (-0.5)
VMEM_BYTES = 20 * 1024 * 1024


def lasting(microseconds):
    return pl.CostEstimate(flops=int(microseconds * 575000000), bytes_accessed=1000, transcendentals=0)


def dot(left, right, left_dim, right_dim):
    return lax.dot_general(left, right, (((left_dim,), (right_dim,)), ((), ())), preferred_element_type=jnp.float32)


def in_hbm(array):
    return pltpu.with_memory_space_constraint(array, pltpu.HBM)


def window_kernel(peers, starts, cotangent, layer_scale, *refs):
    windows, (held, sems) = refs[:-2], refs[-2:]
    parts = len(windows) // peers
    width = held.shape[2]
    copies = []
    for k in range(peers):
        at = pl.ds(pl.multiple_of(starts[k], LANE), width)
        first = 0
        for part in range(parts):
            rows = pl.ds(first, windows[part].shape[0])
            copies.append(pltpu.make_async_copy(cotangent.at[rows, at], held.at[k, rows], sems.at[k, part]))
            first += windows[part].shape[0]
    for copy in copies:
        copy.start()
    for k in range(peers):
        scale = layer_scale[:, pl.ds(pl.multiple_of(starts[k], LANE), width)]
        first = 0
        for part in range(parts):
            copies[k * parts + part].wait()
            window = windows[k * parts + part]
            values = held[k, first:first + window.shape[0], :].astype(jnp.float32)
            window[...] = (values * scale).astype(jnp.bfloat16)
            first += window.shape[0]


def peer_windows(starts, cotangent, layer_scale, peers, width):
    rows, total = cotangent.shape
    parts = (rows // 48 * 16 + 16, rows - rows // 48 * 16 - 16)
    arrays = pl.pallas_call(
        functools.partial(window_kernel, peers),
        grid_spec=pltpu.PrefetchScalarGridSpec(
            num_scalar_prefetch=1,
            grid=(1,),
            in_specs=[pl.BlockSpec(memory_space=pl.ANY), pl.BlockSpec((1, total), lambda i, s: (0, 0))],
            out_specs=[pl.BlockSpec((part, width), lambda i, s: (0, 0)) for part in parts] * peers,
            scratch_shapes=[
                pltpu.VMEM((peers, rows, width), jnp.bfloat16),
                pltpu.SemaphoreType.DMA((peers, len(parts))),
            ],
        ),
        out_shape=[pltpu.HBM((part, width), jnp.bfloat16) for part in parts] * peers,
        compiler_params=pltpu.CompilerParams(vmem_limit_bytes=VMEM_BYTES),
        cost_estimate=lasting(60),
        name="peer_windows",
    )(starts, in_hbm(cotangent), layer_scale)
    return [arrays[part::len(parts)] for part in range(len(parts))]


def prepare_kernel(cotangent, layer_scale, turned):
    values = (cotangent[...].astype(jnp.float32) * layer_scale[...]).astype(jnp.bfloat16)
    spare = jnp.zeros((turned.shape[1] - values.shape[0], values.shape[1]), jnp.bfloat16)
    turned[...] = jnp.concatenate([values, spare], axis=0).T


def prepare(cotangent, layer_scale):
    rows, total = cotangent.shape
    lanes = -(-rows // LANE) * LANE
    steps = 5
    block = total // steps
    return pl.pallas_call(
        prepare_kernel,
        grid=(steps,),
        in_specs=[pl.BlockSpec((rows, block), lambda i: (0, i)), pl.BlockSpec((1, block), lambda i: (0, i))],
        out_specs=pl.BlockSpec((block, lanes), lambda i: (i, 0)),
        out_shape=pltpu.HBM((total, lanes), jnp.bfloat16),
        compiler_params=pltpu.CompilerParams(vmem_limit_bytes=VMEM_BYTES),
        cost_estimate=lasting(60),
        name="scaled_cotangent",
    )(in_hbm(cotangent), layer_scale)


def arrange_kernel(sizes, order, attended, *refs):
    *outs, sems = refs
    copies = []
    for out, size in zip(outs, sizes):
        for j in range(size):
            n = len(copies)
            copies.append(pltpu.make_async_copy(attended.at[order[n]], out.at[j], sems.at[n]))
    for copy in copies:
        copy.start()
    for copy in copies:
        copy.wait()


def arrange(order, attended, sizes):
    _, depth, rows = attended.shape
    return pl.pallas_call(
        functools.partial(arrange_kernel, sizes),
        grid_spec=pltpu.PrefetchScalarGridSpec(
            num_scalar_prefetch=1,
            grid=(1,),
            in_specs=[pl.BlockSpec(memory_space=pl.ANY)],
            out_specs=[pl.BlockSpec((size, depth, rows), lambda i, o: (0, 0, 0)) for size in sizes],
            scratch_shapes=[pltpu.SemaphoreType.DMA((sum(sizes),))],
        ),
        out_shape=[jax.ShapeDtypeStruct((size, depth, rows), attended.dtype) for size in sizes],
        compiler_params=pltpu.CompilerParams(vmem_limit_bytes=VMEM_BYTES),
        cost_estimate=lasting(2),
        name="attended_chunks",
    )(order, in_hbm(attended))


def far_kernel(up, down, out_up, out_down, sems):
    cut = out_up.shape[0]
    copies = [
        pltpu.make_async_copy(up.at[pl.ds(0, cut)], out_up, sems.at[0]),
        pltpu.make_async_copy(down.at[pl.ds(cut, out_down.shape[0])], out_down, sems.at[1]),
    ]
    for copy in copies:
        copy.start()
    for copy in copies:
        copy.wait()


def far_parts(up, down, cut):
    depth, width = up.shape
    sizes = (cut, depth - cut)
    return pl.pallas_call(
        far_kernel,
        grid=(1,),
        in_specs=[pl.BlockSpec(memory_space=pl.ANY)] * 2,
        out_specs=[pl.BlockSpec((size, width), lambda i: (0, 0)) for size in sizes],
        out_shape=[jax.ShapeDtypeStruct((size, width), up.dtype) for size in sizes],
        scratch_shapes=[pltpu.SemaphoreType.DMA((2,))],
        compiler_params=pltpu.CompilerParams(vmem_limit_bytes=VMEM_BYTES),
        cost_estimate=lasting(1),
        name="far_parts",
    )(up, down)


PAIR = 2
EXPONENT = FACTOR * 1.4426950408889634


def forward_kernel(counts, qkv, attended, main_probs, slot_probs):
    def marks(image, ids):
        lane = lax.broadcasted_iota(jnp.int32, (image.shape[0], HS), 1)
        first = jnp.where(image == ids[0], 1.0, 0.0)
        second = jnp.where(image == ids[1], 1.0, 0.0)
        own = jnp.where(lane == 0, first, jnp.where(lane == 1, second, 0.0))
        other = jnp.where(lane == 0, 1.0 - first, jnp.where(lane == 1, 1.0 - second, 0.0)) * -1e30
        return own.astype(jnp.bfloat16), other.astype(jnp.bfloat16)

    main_at = lax.broadcasted_iota(jnp.int32, (MAIN, HS), 0)
    main_marks = marks(jnp.where(main_at >= counts[0], 1, 0), (0, 1))

    def image(at):
        first = jnp.where(at < counts[2], 2, -1)
        return jnp.where(at < SLOT, first, jnp.where(at - SLOT < counts[3], 3, -1))

    slot_marks = marks(image(lax.broadcasted_iota(jnp.int32, (2 * SLOT, HS), 0)), (2, 3))
    valid = image(lax.broadcasted_iota(jnp.int32, (1, 2 * SLOT), 1)) >= 0
    parts = []
    for head in range(PAIR):
        lanes = slice(head * HS, (head + 1) * HS)
        parts.append((head, 0, MAIN, lanes, main_marks, None, main_probs))
        parts.append((head, MAIN, 2 * SLOT, lanes, slot_marks, valid, slot_probs))
    scores = []
    for head, first, rows, lanes, (mark_query, mark_key), _, _ in parts:
        query = jnp.concatenate([qkv[0, first:first + rows, lanes], mark_query], axis=1)
        key = jnp.concatenate([qkv[1, first:first + rows, lanes], mark_key], axis=1)
        scores.append(dot(key, query, 1, 1))
    probs = []
    for score, (_, _, _, _, _, good, _) in zip(scores, parts):
        weights = jnp.exp2((score - jnp.max(score, axis=0, keepdims=True)) * EXPONENT)
        scale = 1.0 / jnp.sum(weights, axis=0, keepdims=True)
        probs.append(weights * (scale if good is None else jnp.where(good, scale, 0.0)))
    for prob, (head, first, rows, lanes, _, _, probs_ref) in zip(probs, parts):
        probs_ref[head] = prob
        result = dot(qkv[2, first:first + rows, lanes], prob.astype(jnp.bfloat16), 0, 0)
        attended[lanes, first:first + rows] = result.astype(jnp.bfloat16)


def forward(counts, qkv):
    _, rows, width = qkv.shape
    heads = width // HS
    return pl.pallas_call(
        forward_kernel,
        grid_spec=pltpu.PrefetchScalarGridSpec(
            num_scalar_prefetch=1,
            grid=(-(-heads // PAIR),),
            in_specs=[pl.BlockSpec((3, rows, PAIR * HS), lambda h, c: (0, 0, h))],
            out_specs=[
                pl.BlockSpec((PAIR * HS, rows), lambda h, c: (h, 0)),
                pl.BlockSpec((PAIR, MAIN, MAIN), lambda h, c: (h, 0, 0)),
                pl.BlockSpec((PAIR, 2 * SLOT, 2 * SLOT), lambda h, c: (h, 0, 0)),
            ],
        ),
        out_shape=[
            pltpu.HBM((width, rows), jnp.bfloat16),
            pltpu.HBM((heads, MAIN, MAIN), jnp.float32),
            pltpu.HBM((heads, 2 * SLOT, 2 * SLOT), jnp.float32),
        ],
        compiler_params=pltpu.CompilerParams(vmem_limit_bytes=VMEM_BYTES),
        cost_estimate=lasting(60),
        name="attention_forward",
    )(counts, qkv)


def backward_kernel(qkv, grad_mine, grad_other, main_probs, slot_probs, *rest):
    grads = rest[-1]
    parts = []
    for head in range(PAIR):
        lanes = slice(head * HS, (head + 1) * HS)
        for first, rows, probs_ref in ((0, MAIN, main_probs), (MAIN, 2 * SLOT, slot_probs)):
            parts.append((head, slice(first, first + rows), lanes, probs_ref))
    grad, dprobs, dscores = [], [], []
    for head, at, lanes, _ in parts:
        both = grad_mine[lanes, at] + grad_other[lanes, at].astype(jnp.float32)
        grad.append(both.astype(jnp.bfloat16))
    for g, (head, at, lanes, _) in zip(grad, parts):
        dprobs.append(dot(qkv[2, at, lanes], g, 1, 0))
    for g, (head, at, lanes, probs_ref) in zip(grad, parts):
        grads[2, at, lanes] = dot(probs_ref[head].astype(jnp.bfloat16), g, 1, 1).astype(jnp.bfloat16)
    for dprob, (head, at, lanes, probs_ref) in zip(dprobs, parts):
        probs = probs_ref[head]
        delta = jnp.sum(probs * dprob, axis=0, keepdims=True)
        dscores.append((probs * (dprob - delta) * FACTOR).astype(jnp.bfloat16))
    for dscore, (head, at, lanes, _) in zip(dscores, parts):
        grads[1, at, lanes] = dot(dscore, qkv[0, at, lanes], 1, 0).astype(jnp.bfloat16)
        grads[0, at, lanes] = dot(dscore, qkv[1, at, lanes], 0, 0).astype(jnp.bfloat16)


def backward(qkv, grad_mine, grad_other, main_probs, slot_probs, low, high, grads):
    _, rows, width = qkv.shape
    held = [] if grads is None else [grads]
    return pl.pallas_call(
        backward_kernel,
        grid=(high - low,),
        in_specs=[
            pl.BlockSpec((3, rows, PAIR * HS), lambda h: (0, 0, h + low)),
            pl.BlockSpec((PAIR * HS, rows), lambda h: (h + low, 0)),
            pl.BlockSpec((PAIR * HS, rows), lambda h: (h + low, 0)),
            pl.BlockSpec((PAIR, MAIN, MAIN), lambda h: (h + low, 0, 0)),
            pl.BlockSpec((PAIR, 2 * SLOT, 2 * SLOT), lambda h: (h + low, 0, 0)),
        ] + [pl.BlockSpec(memory_space=pl.ANY)] * len(held),
        out_specs=pl.BlockSpec((3, rows, PAIR * HS), lambda h: (0, 0, h + low)),
        out_shape=pltpu.HBM(qkv.shape, jnp.bfloat16),
        input_output_aliases={5: 0} if held else {},
        compiler_params=pltpu.CompilerParams(vmem_limit_bytes=VMEM_BYTES),
        cost_estimate=lasting(2 * (high - low)),
        name="attention_backward",
    )(qkv, grad_mine, grad_other, main_probs, slot_probs, *map(in_hbm, held))


def grad_out_kernel(sizes, split, total, info, turned, turned_other, *refs):
    mine, other, columns, tall, mine_rows, other_rows, in_sems, out_sems = refs[-8:]
    count, depth, rows = mine_rows.shape
    core = info[0]
    at = pl.ds(pl.multiple_of(core * (total - split), LANE), split)
    loads = [
        pltpu.make_async_copy(source.at[at], columns.at[i], in_sems.at[i]) for i, source in enumerate((turned, turned_other))
    ]
    index = 0
    for j, size in enumerate(sizes):
        first = 0
        for piece in refs[index:index + size]:
            target = tall.at[j] if size == 1 else tall.at[j, pl.ds(first, piece.shape[0])]
            loads.append(pltpu.make_async_copy(piece, target, in_sems.at[len(loads)]))
            first += piece.shape[0]
        index += size
    for load in loads:
        load.start()
    for load in loads:
        load.wait()

    @pl.when(core == 1)
    def _():
        shared = 2 * split - total
        columns[:, :shared, :] = jnp.zeros((2, shared, columns.shape[2]), jnp.bfloat16)

    stores = []
    for i, (result, out) in enumerate(((mine_rows, mine), (other_rows, other))):
        if depth % 16 == 0:
            product = dot(tall[...].reshape(count * depth, split), columns[i], 1, 0)[:, :rows]
            result[...] = product.astype(result.dtype).reshape(count, depth, rows)
        else:
            for j in range(count):
                result[j] = dot(tall[j], columns[i], 1, 0)[:, :rows].astype(result.dtype)
        for j in range(count):
            stores.append(pltpu.make_async_copy(result.at[j], out.at[info[1 + j]], out_sems.at[i, j]))
            stores[-1].start()
    for store in stores:
        store.wait()


def grad_out_rows(info, turned, turned_other, rows, pieces, shards, held, after=()):
    total, lanes = turned.shape
    split = pieces[0][0].shape[1]
    depth = sum(p.shape[0] for p in pieces[0])
    sizes = [len(p) for p in pieces]
    arrays = [a for p in pieces for a in p]
    count = len(pieces)
    held = [] if held is None else list(held)
    return pl.pallas_call(
        functools.partial(grad_out_kernel, sizes, split, total),
        grid_spec=pltpu.PrefetchScalarGridSpec(
            num_scalar_prefetch=1,
            grid=(1,),
            in_specs=[pl.BlockSpec(memory_space=pl.ANY)] * (2 + len(arrays) + len(held) + len(after)),
            out_specs=[pl.BlockSpec(memory_space=pl.ANY)] * 2,
            scratch_shapes=[
                pltpu.VMEM((2, split, lanes), jnp.bfloat16),
                pltpu.VMEM((count, depth, split), jnp.bfloat16),
                pltpu.VMEM((count, depth, rows), jnp.float32),
                pltpu.VMEM((count, depth, rows), jnp.bfloat16),
                pltpu.SemaphoreType.DMA((2 + len(arrays),)),
                pltpu.SemaphoreType.DMA((2, count)),
            ],
        ),
        out_shape=[
            pltpu.HBM((shards, depth, rows), jnp.float32),
            pltpu.HBM((shards, depth, rows), jnp.bfloat16),
        ],
        input_output_aliases={3 + len(arrays) + i: i for i in range(len(held))},
        compiler_params=pltpu.CompilerParams(vmem_limit_bytes=VMEM_BYTES),
        cost_estimate=lasting(0.2 if held else 1.5 * len(pieces)),
        name="grad_out_rows",
    )(info, in_hbm(turned), turned_other, *arrays, *map(in_hbm, held), *after)


def half_kernel(starts, weight, out, sem):
    copy = pltpu.make_async_copy(weight.at[:, pl.ds(pl.multiple_of(starts[0], LANE), out.shape[1])], out, sem)
    copy.start()
    copy.wait()


def half_columns(start, weight, width):
    return pl.pallas_call(
        half_kernel,
        grid_spec=pltpu.PrefetchScalarGridSpec(
            num_scalar_prefetch=1,
            grid=(1,),
            in_specs=[pl.BlockSpec(memory_space=pl.ANY)],
            out_specs=pl.BlockSpec(memory_space=pl.ANY),
            scratch_shapes=[pltpu.SemaphoreType.DMA],
        ),
        out_shape=jax.ShapeDtypeStruct((weight.shape[0], width), weight.dtype),
        compiler_params=pltpu.CompilerParams(vmem_limit_bytes=VMEM_BYTES),
        cost_estimate=lasting(1),
        name="own_half_of_weight",
    )(start, in_hbm(weight))


def finish_kernel(offsets, start, term, came_up, came_down, out):
    total = term[...] + came_up[...].astype(jnp.float32) + came_down[...].astype(jnp.float32)
    for offset in offsets:

        @pl.when(start[0] == offset)
        def _():
            out[...] = total[:, offset:offset + out.shape[1]]


def finish(start, term, came_up, came_down, owned, offsets):
    depth, window = term.shape
    block = pl.BlockSpec((depth, window), lambda i, s: (0, 0))
    return pl.pallas_call(
        functools.partial(finish_kernel, offsets),
        grid_spec=pltpu.PrefetchScalarGridSpec(
            num_scalar_prefetch=1,
            grid=(1,),
            in_specs=[block] * 3,
            out_specs=pl.BlockSpec((depth, owned), lambda i, s: (0, 0)),
        ),
        out_shape=jax.ShapeDtypeStruct((depth, owned), jnp.float32),
        compiler_params=pltpu.CompilerParams(vmem_limit_bytes=VMEM_BYTES),
        cost_estimate=lasting(2),
        name="last_sum",
    )(start, term, came_up, came_down)


def partial_kernel(chosen, sources, parts, count, window, order, start, *refs):
    attended, columns = refs[:sources], refs[sources:sources * (1 + parts)]
    chunks, held, sems = refs[-3:]
    bases = refs[sources * (1 + parts):-3 - count]
    outs = refs[-3 - count:-3]
    depth, rows = chunks.shape[2:]
    at = pl.ds(pl.multiple_of(start[0], LANE), window)
    copies = []
    for i in range(sources):
        some, first = [], 0
        for part in range(parts):
            source = columns[i * parts + part]
            if chosen:
                some.append(pltpu.make_async_copy(source.at[at], held.at[i], sems.at[i, count + part]))
            else:
                target = held.at[i, pl.ds(first, source.shape[0])]
                some.append(pltpu.make_async_copy(source.at[:, at], target, sems.at[i, count + part]))
            first += source.shape[0]
        for j in range(count):
            source = attended[i].at[order[j] if chosen else j]
            some.append(pltpu.make_async_copy(source, chunks.at[i, j], sems.at[i, j]))
        copies.append(some)
    for some in copies:
        for copy in some:
            copy.start()
    together = depth % 16 == 0
    for i, some in enumerate(copies):
        for copy in some:
            copy.wait()
        if together:
            tall = chunks[i].reshape(count * depth, rows)
            product = dot(tall, held[i][:, :rows], 1, 1) if chosen else dot(tall, held[i], 1, 0)
        for j, out in enumerate(outs):
            if together:
                part = product[j * depth:(j + 1) * depth]
            else:
                part = dot(chunks[i, j], held[i][:, :rows], 1, 1) if chosen else dot(chunks[i, j], held[i], 1, 0)
            if i == 0:
                out[...] = bases[j][...] + part if bases else part
            else:
                out[...] += part


def partial_products(order, start, attended, columns, window, bases=()):
    _, depth, rows = attended[0].shape
    parts = len(columns) // len(attended)
    count, sources = order.shape[0], len(attended)
    block = pl.BlockSpec((depth, window), lambda j, o, s: (0, 0))
    return pl.pallas_call(
        functools.partial(partial_kernel, not bases, sources, parts, count, window),
        grid_spec=pltpu.PrefetchScalarGridSpec(
            num_scalar_prefetch=2,
            grid=(1,),
            in_specs=[pl.BlockSpec(memory_space=pl.ANY)] * (sources * (1 + parts)) + [block] * len(bases),
            out_specs=[block] * count,
            scratch_shapes=[
                pltpu.VMEM((sources, count, depth, rows), jnp.bfloat16),
                pltpu.VMEM((sources, rows, window) if bases else (sources, window, columns[0].shape[1]), jnp.bfloat16),
                pltpu.SemaphoreType.DMA((sources, count + parts)),
            ],
        ),
        out_shape=[(jax.ShapeDtypeStruct if bases else pltpu.HBM)((depth, window), jnp.float32)] * count,
        compiler_params=pltpu.CompilerParams(vmem_limit_bytes=VMEM_BYTES),
        cost_estimate=lasting(3 if bases else 6),
        name="projection_peers" if bases else "projection_chip",
    )(order, start, *attended, *columns, *map(in_hbm, bases))


def windows_of(groups, owned, total):
    lows = [g * owned // LANE * LANE for g in range(groups)]
    width = max(-(-((g + 1) * owned) // LANE) * LANE - low for g, low in enumerate(lows))
    return width


def ring_of(count):
    return list(range(0, count, 2)) + list(range(count - 1, 0, -2))


def local(members, shards, query_key_value, cotangent, proj_weight, layer_scale, lengths):
    member = lax.axis_index("dp")
    shard = lax.axis_index("fsdp")
    core, chip, peers = member % 2, member // 2, members // 2
    ring = ring_of(shards)
    place = jnp.where(shard % 2 == 0, shard // 2, shards - 1 - shard // 2)
    ahead = [(ring[i], ring[(i + 1) % shards]) for i in range(shards)]
    behind = [(ring[i], ring[(i - 1) % shards]) for i in range(shards)]
    half = shards // 2
    depth, total = proj_weight.shape
    rows, width = query_key_value.shape[1:]
    owned = total // members
    counts = lax.dynamic_index_in_dim(lengths[:, 0, :], member, 0, keepdims=False)

    def swap(array, bit):
        return lax.ppermute(array, "dp", [(i, i ^ bit) for i in range(members)])

    def shard_at(offset):
        at = (place + offset + shards) % shards
        return jnp.where(at < half, 2 * at, 2 * (shards - 1 - at) + 1)

    def table(values):
        return jnp.stack([jnp.asarray(v) for v in values]).astype(jnp.int32)

    chip_width, window = windows_of(peers, 2 * owned, total), windows_of(members, owned, total)

    def chip_start(chip):
        return jnp.minimum(chip * 2 * owned // LANE * LANE, total - chip_width)

    my_start = jnp.minimum(member * owned // LANE * LANE, chip_start(chip) + chip_width - window)
    starts = table([my_start, my_start - chip_start(chip)])

    split = -(-(total // LANE) // 2) * LANE
    mine = half_columns(table([core * (total - split)]), proj_weight, split)
    cut = -(-depth // 32) * 16
    up, down = [mine], [mine]
    up.append(lax.ppermute(up[-1], "fsdp", ahead))
    down.append(lax.ppermute(down[-1], "fsdp", behind))

    mine, cotangent = lax.optimization_barrier((mine, cotangent))
    scales = layer_scale.reshape(1, total)
    sent = peer_windows(
        table([chip_start(chip ^ k) for k in range(1, peers)] or [0]), cotangent, scales, peers - 1, chip_width
    )
    sent, cotangent = lax.optimization_barrier((sent, cotangent))
    came_columns = [[swap(array, 2 * k) for k, array in enumerate(part, 1)] for part in sent]
    turned = prepare(cotangent, scales)
    attended, main_probs, slot_probs = forward(counts, query_key_value)
    attended = attended.reshape(shards, depth, rows)
    near = [[o, -o] for o in range(half - 1, 0, -1)]
    groups = [[half] + near[0]] + near[1:-1] + [near[-1] + [0]]
    flat = table([shard_at(o) for group in groups for o in group])
    sizes = [len(group) for group in groups]
    orders = [flat[sum(sizes[:g]):sum(sizes[:g + 1])] for g in range(len(groups))]

    def rows_of(some, held, after=()):
        info = table([core] + [shard_at(o) for _, o in some])
        return grad_out_rows(info, turned, turned_other, rows, [p for p, _ in some], shards, held, after)

    up[1], down[1], attended, came_columns[0], turned = lax.optimization_barrier(
        (up[1], down[1], attended, came_columns[0], turned)
    )
    turned_other = swap(turned, 1)
    other_columns = [[swap(array, 1) for array in came_columns[0]]]
    attended_other = swap(attended, 1)
    chunks = list(arrange(flat, attended, sizes))
    for _ in range(half - 3):
        up.append(lax.ppermute(up[-1], "fsdp", ahead))
        down.append(lax.ppermute(down[-1], "fsdp", behind))
    bases = partial_products(
        flat, starts[:1], [in_hbm(attended), attended_other], [in_hbm(turned), turned_other], window
    )
    up[-1], down[-1], turned_other, attended_other, *bases = lax.optimization_barrier(
        (up[-1], down[-1], turned_other, attended_other, *bases)
    )
    bases = dict(zip([o for group in groups for o in group], bases))

    late, chunks = lax.optimization_barrier((came_columns[1], chunks))
    came = [[swap(chunks[0], 2 * k) for k in range(1, peers)]]
    other_columns.append([swap(array, 1) for array in late])
    came_columns[1] = late
    came.append([swap(chunks[1], 2 * k) for k in range(1, peers)])
    columns = []
    for k in range(peers - 1):
        for arrays in (came_columns, other_columns):
            columns += [part[k] for part in arrays]
    pieces = [([mine], 0)]
    for step in range(1, half - 1):
        pieces += [([up[step]], -step), ([down[step]], step)]
    grad_out = rows_of(pieces, None)
    up.append(lax.ppermute(up[-1], "fsdp", ahead))
    down.append(lax.ppermute(down[-1], "fsdp", behind))
    up[-1], down[-1], grad_out = lax.optimization_barrier((up[-1], down[-1], grad_out))
    if depth % 16 == 0:
        far_up, far_down = far_parts(up[-1], down[-1], cut)
    else:
        far_up, far_down = up[-1][:cut], down[-1][cut:]
    came[0], near_up, near_down, sent_up = lax.optimization_barrier((came[0], up[-1], down[-1], far_up))
    far_up = lax.ppermute(far_up, "fsdp", ahead)
    far_down = lax.ppermute(far_down, "fsdp", behind)

    def both_cores(arrays):
        return [a for c in arrays for a in (c, swap(c, 1))]

    def products(index, taken):
        group = groups[index]
        if not taken:
            return {o: bases[o] for o in group}
        result = partial_products(orders[index], starts[1:], taken, columns, window, [bases[o] for o in group])
        return dict(zip(group, result))

    terms = products(0, both_cores(came[0]))
    first = terms[half].astype(jnp.bfloat16)
    going_up, going_down, came[1], chunks, far_up, far_down = lax.optimization_barrier(
        (first[:cut], first[cut:], came[1], chunks, far_up, far_down)
    )
    came += [[swap(some, 2 * k) for k in range(1, peers)] for some in chunks[2:]]
    taken = both_cores(came[1])
    came_up = lax.ppermute(going_up, "fsdp", ahead)
    came_down = lax.ppermute(going_down, "fsdp", behind)

    bounds = [0, 3, 5, -(-(width // HS) // PAIR)]
    grads = None
    for step in range(half, 1, -1):
        if step == half:
            came_up, came_down, following = lax.optimization_barrier((came_up, came_down, products(1, taken)))
            terms.update(following)
            came_up = jnp.pad(came_up, ((0, depth - cut), (0, 0)))
            came_down = jnp.pad(came_down, ((cut, 0), (0, 0)))
        going_up = (terms[step - 1] + came_up.astype(jnp.float32)).astype(jnp.bfloat16)
        going_down = (terms[1 - step] + came_down.astype(jnp.float32)).astype(jnp.bfloat16)
        if step == half:
            going_up, going_down, near_up = lax.optimization_barrier((going_up, going_down, near_up))
            grad_out = rows_of([([near_up], 1 - half), ([near_down], half - 1), ([far_up, far_down], half)], grad_out, [sent_up])
            grad_mine = grad_out[0].reshape(width, rows)
            grad_other = swap(grad_out[1], 1).reshape(width, rows)
        elif step > 2:
            arrived = came[half - step + 1]
            going_up, going_down, arrived, grad_mine = lax.optimization_barrier((going_up, going_down, arrived, grad_mine))
            terms.update(products(half - step + 1, both_cores(arrived)))
        else:
            going_up, going_down = lax.optimization_barrier((going_up, going_down))
        came_up = lax.ppermute(going_up, "fsdp", ahead)
        came_down = lax.ppermute(going_down, "fsdp", behind)
    for low, high in zip(bounds, bounds[1:]):
        grads = backward(query_key_value, grad_mine, grad_other, main_probs, slot_probs, low, high, grads)
    came_up, came_down, grads = lax.optimization_barrier((came_up, came_down, grads))
    offsets = set()
    for m in range(members):
        low = min((m // 2) * 2 * owned // LANE * LANE, total - chip_width)
        offsets.add(m * owned - min(m * owned // LANE * LANE, low + chip_width - window))
    grad_proj = finish(table([member * owned - my_start]), terms[0], came_up, came_down, owned, sorted(offsets))
    return grads, grad_proj


def solution(mesh):
    members, shards = mesh.shape["dp"], mesh.shape["fsdp"]
    placed = (
        P(None, ("dp", "fsdp"), None),
        P(("dp", "fsdp"), None),
        P("fsdp", None),
        P(),
        P(None, "fsdp", None),
    )
    return jax.shard_map(
        functools.partial(local, members, shards),
        mesh=mesh,
        in_specs=placed,
        out_specs=(P(None, ("dp", "fsdp"), None), P("fsdp", "dp")),
        check_vma=False,
    )
```

```python
import functools

import jax
import jax.numpy as jnp
from jax import lax
from jax.experimental import pallas as pl
from jax.experimental.pallas import tpu as pltpu
from jax.sharding import PartitionSpec as P

HS = 128
MAIN = 256
SLOT = 96
LANE = 128
FACTOR = HS ** (-0.5)
VMEM_BYTES = 20 * 1024 * 1024


def lasting(microseconds):
    return pl.CostEstimate(flops=int(microseconds * 575000000), bytes_accessed=1000, transcendentals=0)


def dot(left, right, left_dim, right_dim):
    return lax.dot_general(left, right, (((left_dim,), (right_dim,)), ((), ())), preferred_element_type=jnp.float32)


def in_hbm(array):
    return pltpu.with_memory_space_constraint(array, pltpu.HBM)


def window_kernel(peers, starts, cotangent, layer_scale, *refs):
    windows, (held, sems) = refs[:-2], refs[-2:]
    parts = len(windows) // peers
    width = held.shape[2]
    copies = []
    for k in range(peers):
        at = pl.ds(pl.multiple_of(starts[k], LANE), width)
        first = 0
        for part in range(parts):
            rows = pl.ds(first, windows[part].shape[0])
            copies.append(pltpu.make_async_copy(cotangent.at[rows, at], held.at[k, rows], sems.at[k, part]))
            first += windows[part].shape[0]
    for copy in copies:
        copy.start()
    for k in range(peers):
        scale = layer_scale[:, pl.ds(pl.multiple_of(starts[k], LANE), width)]
        first = 0
        for part in range(parts):
            copies[k * parts + part].wait()
            window = windows[k * parts + part]
            values = held[k, first:first + window.shape[0], :].astype(jnp.float32)
            window[...] = (values * scale).astype(jnp.bfloat16)
            first += window.shape[0]


def peer_windows(starts, cotangent, layer_scale, peers, width):
    rows, total = cotangent.shape
    parts = (rows // 48 * 16 + 16, rows - rows // 48 * 16 - 16)
    arrays = pl.pallas_call(
        functools.partial(window_kernel, peers),
        grid_spec=pltpu.PrefetchScalarGridSpec(
            num_scalar_prefetch=1,
            grid=(1,),
            in_specs=[pl.BlockSpec(memory_space=pl.ANY), pl.BlockSpec((1, total), lambda i, s: (0, 0))],
            out_specs=[pl.BlockSpec((part, width), lambda i, s: (0, 0)) for part in parts] * peers,
            scratch_shapes=[
                pltpu.VMEM((peers, rows, width), jnp.bfloat16),
                pltpu.SemaphoreType.DMA((peers, len(parts))),
            ],
        ),
        out_shape=[pltpu.HBM((part, width), jnp.bfloat16) for part in parts] * peers,
        compiler_params=pltpu.CompilerParams(vmem_limit_bytes=VMEM_BYTES),
        cost_estimate=lasting(60),
        name="peer_windows",
    )(starts, in_hbm(cotangent), layer_scale)
    return [arrays[part::len(parts)] for part in range(len(parts))]


def prepare_kernel(cotangent, layer_scale, turned):
    values = (cotangent[...].astype(jnp.float32) * layer_scale[...]).astype(jnp.bfloat16)
    spare = jnp.zeros((turned.shape[1] - values.shape[0], values.shape[1]), jnp.bfloat16)
    turned[...] = jnp.concatenate([values, spare], axis=0).T


def prepare(cotangent, layer_scale):
    rows, total = cotangent.shape
    lanes = -(-rows // LANE) * LANE
    steps = 5
    block = total // steps
    return pl.pallas_call(
        prepare_kernel,
        grid=(steps,),
        in_specs=[pl.BlockSpec((rows, block), lambda i: (0, i)), pl.BlockSpec((1, block), lambda i: (0, i))],
        out_specs=pl.BlockSpec((block, lanes), lambda i: (i, 0)),
        out_shape=pltpu.HBM((total, lanes), jnp.bfloat16),
        compiler_params=pltpu.CompilerParams(vmem_limit_bytes=VMEM_BYTES),
        cost_estimate=lasting(60),
        name="scaled_cotangent",
    )(in_hbm(cotangent), layer_scale)


def arrange_kernel(sizes, order, attended, *refs):
    *outs, sems = refs
    copies = []
    for out, size in zip(outs, sizes):
        for j in range(size):
            n = len(copies)
            copies.append(pltpu.make_async_copy(attended.at[order[n]], out.at[j], sems.at[n]))
    for copy in copies:
        copy.start()
    for copy in copies:
        copy.wait()


def arrange(order, attended, sizes):
    _, depth, rows = attended.shape
    return pl.pallas_call(
        functools.partial(arrange_kernel, sizes),
        grid_spec=pltpu.PrefetchScalarGridSpec(
            num_scalar_prefetch=1,
            grid=(1,),
            in_specs=[pl.BlockSpec(memory_space=pl.ANY)],
            out_specs=[pl.BlockSpec((size, depth, rows), lambda i, o: (0, 0, 0)) for size in sizes],
            scratch_shapes=[pltpu.SemaphoreType.DMA((sum(sizes),))],
        ),
        out_shape=[jax.ShapeDtypeStruct((size, depth, rows), attended.dtype) for size in sizes],
        compiler_params=pltpu.CompilerParams(vmem_limit_bytes=VMEM_BYTES),
        cost_estimate=lasting(2),
        name="attended_chunks",
    )(order, in_hbm(attended))


def far_kernel(up, down, out_up, out_down, sems):
    cut = out_up.shape[0]
    copies = [
        pltpu.make_async_copy(up.at[pl.ds(0, cut)], out_up, sems.at[0]),
        pltpu.make_async_copy(down.at[pl.ds(cut, out_down.shape[0])], out_down, sems.at[1]),
    ]
    for copy in copies:
        copy.start()
    for copy in copies:
        copy.wait()


def far_parts(up, down, cut):
    depth, width = up.shape
    sizes = (cut, depth - cut)
    return pl.pallas_call(
        far_kernel,
        grid=(1,),
        in_specs=[pl.BlockSpec(memory_space=pl.ANY)] * 2,
        out_specs=[pl.BlockSpec((size, width), lambda i: (0, 0)) for size in sizes],
        out_shape=[jax.ShapeDtypeStruct((size, width), up.dtype) for size in sizes],
        scratch_shapes=[pltpu.SemaphoreType.DMA((2,))],
        compiler_params=pltpu.CompilerParams(vmem_limit_bytes=VMEM_BYTES),
        cost_estimate=lasting(1),
        name="far_parts",
    )(up, down)


PAIR = 2
EXPONENT = FACTOR * 1.4426950408889634


def forward_kernel(counts, qkv, attended, main_probs, slot_probs):
    def marks(image, ids):
        lane = lax.broadcasted_iota(jnp.int32, (image.shape[0], HS), 1)
        first = jnp.where(image == ids[0], 1.0, 0.0)
        second = jnp.where(image == ids[1], 1.0, 0.0)
        own = jnp.where(lane == 0, first, jnp.where(lane == 1, second, 0.0))
        other = jnp.where(lane == 0, 1.0 - first, jnp.where(lane == 1, 1.0 - second, 0.0)) * -1e30
        return own.astype(jnp.bfloat16), other.astype(jnp.bfloat16)

    main_at = lax.broadcasted_iota(jnp.int32, (MAIN, HS), 0)
    main_marks = marks(jnp.where(main_at >= counts[0], 1, 0), (0, 1))

    def image(at):
        first = jnp.where(at < counts[2], 2, -1)
        return jnp.where(at < SLOT, first, jnp.where(at - SLOT < counts[3], 3, -1))

    slot_marks = marks(image(lax.broadcasted_iota(jnp.int32, (2 * SLOT, HS), 0)), (2, 3))
    valid = image(lax.broadcasted_iota(jnp.int32, (1, 2 * SLOT), 1)) >= 0
    parts = []
    for head in range(PAIR):
        lanes = slice(head * HS, (head + 1) * HS)
        parts.append((head, 0, MAIN, lanes, main_marks, None, main_probs))
        parts.append((head, MAIN, 2 * SLOT, lanes, slot_marks, valid, slot_probs))
    scores = []
    for head, first, rows, lanes, (mark_query, mark_key), _, _ in parts:
        query = jnp.concatenate([qkv[0, first:first + rows, lanes], mark_query], axis=1)
        key = jnp.concatenate([qkv[1, first:first + rows, lanes], mark_key], axis=1)
        scores.append(dot(key, query, 1, 1))
    probs = []
    for score, (_, _, _, _, _, good, _) in zip(scores, parts):
        weights = jnp.exp2((score - jnp.max(score, axis=0, keepdims=True)) * EXPONENT)
        scale = 1.0 / jnp.sum(weights, axis=0, keepdims=True)
        probs.append(weights * (scale if good is None else jnp.where(good, scale, 0.0)))
    for prob, (head, first, rows, lanes, _, _, probs_ref) in zip(probs, parts):
        probs_ref[head] = prob
        result = dot(qkv[2, first:first + rows, lanes], prob.astype(jnp.bfloat16), 0, 0)
        attended[lanes, first:first + rows] = result.astype(jnp.bfloat16)


def forward(counts, qkv):
    _, rows, width = qkv.shape
    heads = width // HS
    return pl.pallas_call(
        forward_kernel,
        grid_spec=pltpu.PrefetchScalarGridSpec(
            num_scalar_prefetch=1,
            grid=(-(-heads // PAIR),),
            in_specs=[pl.BlockSpec((3, rows, PAIR * HS), lambda h, c: (0, 0, h))],
            out_specs=[
                pl.BlockSpec((PAIR * HS, rows), lambda h, c: (h, 0)),
                pl.BlockSpec((PAIR, MAIN, MAIN), lambda h, c: (h, 0, 0)),
                pl.BlockSpec((PAIR, 2 * SLOT, 2 * SLOT), lambda h, c: (h, 0, 0)),
            ],
        ),
        out_shape=[
            pltpu.HBM((width, rows), jnp.bfloat16),
            pltpu.HBM((heads, MAIN, MAIN), jnp.float32),
            pltpu.HBM((heads, 2 * SLOT, 2 * SLOT), jnp.float32),
        ],
        compiler_params=pltpu.CompilerParams(vmem_limit_bytes=VMEM_BYTES),
        cost_estimate=lasting(60),
        name="attention_forward",
    )(counts, qkv)


def backward_kernel(qkv, grad_mine, grad_other, main_probs, slot_probs, *rest):
    grads = rest[-1]
    parts = []
    for head in range(PAIR):
        lanes = slice(head * HS, (head + 1) * HS)
        for first, rows, probs_ref in ((0, MAIN, main_probs), (MAIN, 2 * SLOT, slot_probs)):
            parts.append((head, slice(first, first + rows), lanes, probs_ref))
    grad, dprobs, dscores = [], [], []
    for head, at, lanes, _ in parts:
        both = grad_mine[lanes, at] + grad_other[lanes, at].astype(jnp.float32)
        grad.append(both.astype(jnp.bfloat16))
    for g, (head, at, lanes, _) in zip(grad, parts):
        dprobs.append(dot(qkv[2, at, lanes], g, 1, 0))
    for g, (head, at, lanes, probs_ref) in zip(grad, parts):
        grads[2, at, lanes] = dot(probs_ref[head].astype(jnp.bfloat16), g, 1, 1).astype(jnp.bfloat16)
    for dprob, (head, at, lanes, probs_ref) in zip(dprobs, parts):
        probs = probs_ref[head]
        delta = jnp.sum(probs * dprob, axis=0, keepdims=True)
        dscores.append((probs * (dprob - delta) * FACTOR).astype(jnp.bfloat16))
    for dscore, (head, at, lanes, _) in zip(dscores, parts):
        grads[1, at, lanes] = dot(dscore, qkv[0, at, lanes], 1, 0).astype(jnp.bfloat16)
        grads[0, at, lanes] = dot(dscore, qkv[1, at, lanes], 0, 0).astype(jnp.bfloat16)


def backward(qkv, grad_mine, grad_other, main_probs, slot_probs, low, high, grads):
    _, rows, width = qkv.shape
    held = [] if grads is None else [grads]
    return pl.pallas_call(
        backward_kernel,
        grid=(high - low,),
        in_specs=[
            pl.BlockSpec((3, rows, PAIR * HS), lambda h: (0, 0, h + low)),
            pl.BlockSpec((PAIR * HS, rows), lambda h: (h + low, 0)),
            pl.BlockSpec((PAIR * HS, rows), lambda h: (h + low, 0)),
            pl.BlockSpec((PAIR, MAIN, MAIN), lambda h: (h + low, 0, 0)),
            pl.BlockSpec((PAIR, 2 * SLOT, 2 * SLOT), lambda h: (h + low, 0, 0)),
        ] + [pl.BlockSpec(memory_space=pl.ANY)] * len(held),
        out_specs=pl.BlockSpec((3, rows, PAIR * HS), lambda h: (0, 0, h + low)),
        out_shape=pltpu.HBM(qkv.shape, jnp.bfloat16),
        input_output_aliases={5: 0} if held else {},
        compiler_params=pltpu.CompilerParams(vmem_limit_bytes=VMEM_BYTES),
        cost_estimate=lasting(2 * (high - low)),
        name="attention_backward",
    )(qkv, grad_mine, grad_other, main_probs, slot_probs, *map(in_hbm, held))


def grad_out_kernel(sizes, split, total, info, turned, turned_other, *refs):
    mine, other, columns, tall, mine_rows, other_rows, in_sems, out_sems = refs[-8:]
    count, depth, rows = mine_rows.shape
    core = info[0]
    at = pl.ds(pl.multiple_of(core * (total - split), LANE), split)
    loads = [
        pltpu.make_async_copy(source.at[at], columns.at[i], in_sems.at[i]) for i, source in enumerate((turned, turned_other))
    ]
    index = 0
    for j, size in enumerate(sizes):
        first = 0
        for piece in refs[index:index + size]:
            target = tall.at[j] if size == 1 else tall.at[j, pl.ds(first, piece.shape[0])]
            loads.append(pltpu.make_async_copy(piece, target, in_sems.at[len(loads)]))
            first += piece.shape[0]
        index += size
    for load in loads:
        load.start()
    for load in loads:
        load.wait()

    @pl.when(core == 1)
    def _():
        shared = 2 * split - total
        columns[:, :shared, :] = jnp.zeros((2, shared, columns.shape[2]), jnp.bfloat16)

    stores = []
    for i, (result, out) in enumerate(((mine_rows, mine), (other_rows, other))):
        if depth % 16 == 0:
            product = dot(tall[...].reshape(count * depth, split), columns[i], 1, 0)[:, :rows]
            result[...] = product.astype(result.dtype).reshape(count, depth, rows)
        else:
            for j in range(count):
                result[j] = dot(tall[j], columns[i], 1, 0)[:, :rows].astype(result.dtype)
        for j in range(count):
            stores.append(pltpu.make_async_copy(result.at[j], out.at[info[1 + j]], out_sems.at[i, j]))
            stores[-1].start()
    for store in stores:
        store.wait()


def grad_out_rows(info, turned, turned_other, rows, pieces, shards, held, after=()):
    total, lanes = turned.shape
    split = pieces[0][0].shape[1]
    depth = sum(p.shape[0] for p in pieces[0])
    sizes = [len(p) for p in pieces]
    arrays = [a for p in pieces for a in p]
    count = len(pieces)
    held = [] if held is None else list(held)
    return pl.pallas_call(
        functools.partial(grad_out_kernel, sizes, split, total),
        grid_spec=pltpu.PrefetchScalarGridSpec(
            num_scalar_prefetch=1,
            grid=(1,),
            in_specs=[pl.BlockSpec(memory_space=pl.ANY)] * (2 + len(arrays) + len(held) + len(after)),
            out_specs=[pl.BlockSpec(memory_space=pl.ANY)] * 2,
            scratch_shapes=[
                pltpu.VMEM((2, split, lanes), jnp.bfloat16),
                pltpu.VMEM((count, depth, split), jnp.bfloat16),
                pltpu.VMEM((count, depth, rows), jnp.float32),
                pltpu.VMEM((count, depth, rows), jnp.bfloat16),
                pltpu.SemaphoreType.DMA((2 + len(arrays),)),
                pltpu.SemaphoreType.DMA((2, count)),
            ],
        ),
        out_shape=[
            pltpu.HBM((shards, depth, rows), jnp.float32),
            pltpu.HBM((shards, depth, rows), jnp.bfloat16),
        ],
        input_output_aliases={3 + len(arrays) + i: i for i in range(len(held))},
        compiler_params=pltpu.CompilerParams(vmem_limit_bytes=VMEM_BYTES),
        cost_estimate=lasting(0.2 if held else 1.5 * len(pieces)),
        name="grad_out_rows",
    )(info, in_hbm(turned), turned_other, *arrays, *map(in_hbm, held), *after)


def half_kernel(starts, weight, out, sem):
    copy = pltpu.make_async_copy(weight.at[:, pl.ds(pl.multiple_of(starts[0], LANE), out.shape[1])], out, sem)
    copy.start()
    copy.wait()


def half_columns(start, weight, width):
    return pl.pallas_call(
        half_kernel,
        grid_spec=pltpu.PrefetchScalarGridSpec(
            num_scalar_prefetch=1,
            grid=(1,),
            in_specs=[pl.BlockSpec(memory_space=pl.ANY)],
            out_specs=pl.BlockSpec(memory_space=pl.ANY),
            scratch_shapes=[pltpu.SemaphoreType.DMA],
        ),
        out_shape=jax.ShapeDtypeStruct((weight.shape[0], width), weight.dtype),
        compiler_params=pltpu.CompilerParams(vmem_limit_bytes=VMEM_BYTES),
        cost_estimate=lasting(1),
        name="own_half_of_weight",
    )(start, in_hbm(weight))


def finish_kernel(offsets, start, term, came_up, came_down, out):
    total = term[...] + came_up[...].astype(jnp.float32) + came_down[...].astype(jnp.float32)
    for offset in offsets:

        @pl.when(start[0] == offset)
        def _():
            out[...] = total[:, offset:offset + out.shape[1]]


def finish(start, term, came_up, came_down, owned, offsets):
    depth, window = term.shape
    block = pl.BlockSpec((depth, window), lambda i, s: (0, 0))
    return pl.pallas_call(
        functools.partial(finish_kernel, offsets),
        grid_spec=pltpu.PrefetchScalarGridSpec(
            num_scalar_prefetch=1,
            grid=(1,),
            in_specs=[block] * 3,
            out_specs=pl.BlockSpec((depth, owned), lambda i, s: (0, 0)),
        ),
        out_shape=jax.ShapeDtypeStruct((depth, owned), jnp.float32),
        compiler_params=pltpu.CompilerParams(vmem_limit_bytes=VMEM_BYTES),
        cost_estimate=lasting(2),
        name="last_sum",
    )(start, term, came_up, came_down)


def partial_kernel(chosen, sources, parts, count, window, order, start, *refs):
    attended, columns = refs[:sources], refs[sources:sources * (1 + parts)]
    chunks, held, sums, sems = refs[-4:]
    bases = refs[sources * (1 + parts):-4 - count]
    outs = refs[-4 - count:-4]
    depth, rows = chunks.shape[2:]
    at = pl.ds(pl.multiple_of(start[0], LANE), window)
    copies = []
    for i in range(sources):
        some, first = [], 0
        for part in range(parts):
            source = columns[i * parts + part]
            if chosen:
                some.append(pltpu.make_async_copy(source.at[at], held.at[i], sems.at[i, count + part]))
            else:
                target = held.at[i, pl.ds(first, source.shape[0])]
                some.append(pltpu.make_async_copy(source.at[:, at], target, sems.at[i, count + part]))
            first += source.shape[0]
        for j in range(count):
            source = attended[i].at[order[j] if chosen else j]
            some.append(pltpu.make_async_copy(source, chunks.at[i, j], sems.at[i, j]))
        copies.append(some)
    for some in copies:
        for copy in some:
            copy.start()
    together = depth % 16 == 0
    for i, some in enumerate(copies):
        for copy in some:
            copy.wait()
        if together:
            tall = chunks[i].reshape(count * depth, rows)
            product = dot(tall, held[i][:, :rows], 1, 1) if chosen else dot(tall, held[i], 1, 0)
        for j, out in enumerate(outs):
            if together:
                part = product[j * depth:(j + 1) * depth]
            else:
                part = dot(chunks[i, j], held[i][:, :rows], 1, 1) if chosen else dot(chunks[i, j], held[i], 1, 0)
            if i == 0:
                total = bases[j][...].astype(jnp.float32) + part if bases else part
            else:
                total = sums[j] + part
            if i < sources - 1:
                sums[j] = total
            else:
                out[...] = total.astype(out.dtype)


def partial_products(order, start, attended, columns, window, bases=()):
    _, depth, rows = attended[0].shape
    parts = len(columns) // len(attended)
    count, sources = order.shape[0], len(attended)
    block = pl.BlockSpec((depth, window), lambda j, o, s: (0, 0))
    return pl.pallas_call(
        functools.partial(partial_kernel, not bases, sources, parts, count, window),
        grid_spec=pltpu.PrefetchScalarGridSpec(
            num_scalar_prefetch=2,
            grid=(1,),
            in_specs=[pl.BlockSpec(memory_space=pl.ANY)] * (sources * (1 + parts)) + [block] * len(bases),
            out_specs=[block] * count,
            scratch_shapes=[
                pltpu.VMEM((sources, count, depth, rows), jnp.bfloat16),
                pltpu.VMEM((sources, rows, window) if bases else (sources, window, columns[0].shape[1]), jnp.bfloat16),
                pltpu.VMEM((count, depth, window), jnp.float32),
                pltpu.SemaphoreType.DMA((sources, count + parts)),
            ],
        ),
        out_shape=[
            jax.ShapeDtypeStruct((depth, window), jnp.float32) if bases else pltpu.HBM((depth, window), jnp.bfloat16)
        ] * count,
        compiler_params=pltpu.CompilerParams(vmem_limit_bytes=VMEM_BYTES),
        cost_estimate=lasting(3 if bases else 6),
        name="projection_peers" if bases else "projection_chip",
    )(order, start, *attended, *columns, *map(in_hbm, bases))


def windows_of(groups, owned, total):
    lows = [g * owned // LANE * LANE for g in range(groups)]
    width = max(-(-((g + 1) * owned) // LANE) * LANE - low for g, low in enumerate(lows))
    return width


def ring_of(count):
    return list(range(0, count, 2)) + list(range(count - 1, 0, -2))


def local(members, shards, query_key_value, cotangent, proj_weight, layer_scale, lengths):
    member = lax.axis_index("dp")
    shard = lax.axis_index("fsdp")
    core, chip, peers = member % 2, member // 2, members // 2
    ring = ring_of(shards)
    place = jnp.where(shard % 2 == 0, shard // 2, shards - 1 - shard // 2)
    ahead = [(ring[i], ring[(i + 1) % shards]) for i in range(shards)]
    behind = [(ring[i], ring[(i - 1) % shards]) for i in range(shards)]
    half = shards // 2
    depth, total = proj_weight.shape
    rows, width = query_key_value.shape[1:]
    owned = total // members
    counts = lax.dynamic_index_in_dim(lengths[:, 0, :], member, 0, keepdims=False)

    def swap(array, bit):
        return lax.ppermute(array, "dp", [(i, i ^ bit) for i in range(members)])

    def shard_at(offset):
        at = (place + offset + shards) % shards
        return jnp.where(at < half, 2 * at, 2 * (shards - 1 - at) + 1)

    def table(values):
        return jnp.stack([jnp.asarray(v) for v in values]).astype(jnp.int32)

    chip_width, window = windows_of(peers, 2 * owned, total), windows_of(members, owned, total)

    def chip_start(chip):
        return jnp.minimum(chip * 2 * owned // LANE * LANE, total - chip_width)

    my_start = jnp.minimum(member * owned // LANE * LANE, chip_start(chip) + chip_width - window)
    starts = table([my_start, my_start - chip_start(chip)])

    split = -(-(total // LANE) // 2) * LANE
    mine = half_columns(table([core * (total - split)]), proj_weight, split)
    cut = -(-depth // 32) * 16
    up, down = [mine], [mine]
    up.append(lax.ppermute(up[-1], "fsdp", ahead))
    down.append(lax.ppermute(down[-1], "fsdp", behind))

    mine, cotangent = lax.optimization_barrier((mine, cotangent))
    scales = layer_scale.reshape(1, total)
    sent = peer_windows(
        table([chip_start(chip ^ k) for k in range(1, peers)] or [0]), cotangent, scales, peers - 1, chip_width
    )
    sent, cotangent = lax.optimization_barrier((sent, cotangent))
    came_columns = [[swap(array, 2 * k) for k, array in enumerate(part, 1)] for part in sent]
    turned = prepare(cotangent, scales)
    attended, main_probs, slot_probs = forward(counts, query_key_value)
    attended = attended.reshape(shards, depth, rows)
    near = [[o, -o] for o in range(half - 1, 0, -1)]
    groups = [[half] + near[0]] + near[1:-1] + [near[-1] + [0]]
    flat = table([shard_at(o) for group in groups for o in group])
    sizes = [len(group) for group in groups]
    orders = [flat[sum(sizes[:g]):sum(sizes[:g + 1])] for g in range(len(groups))]

    def rows_of(some, held, after=()):
        info = table([core] + [shard_at(o) for _, o in some])
        return grad_out_rows(info, turned, turned_other, rows, [p for p, _ in some], shards, held, after)

    up[1], down[1], attended, came_columns[0], turned = lax.optimization_barrier(
        (up[1], down[1], attended, came_columns[0], turned)
    )
    turned_other = swap(turned, 1)
    other_columns = [[swap(array, 1) for array in came_columns[0]]]
    attended_other = swap(attended, 1)
    chunks = list(arrange(flat, attended, sizes))
    attended_other, chunks = lax.optimization_barrier((attended_other, chunks))
    for _ in range(half - 3):
        up.append(lax.ppermute(up[-1], "fsdp", ahead))
        down.append(lax.ppermute(down[-1], "fsdp", behind))
    bases = partial_products(
        flat, starts[:1], [in_hbm(attended), attended_other], [in_hbm(turned), turned_other], window
    )
    up[-1], down[-1], turned_other, attended_other, *bases = lax.optimization_barrier(
        (up[-1], down[-1], turned_other, attended_other, *bases)
    )
    bases = dict(zip([o for group in groups for o in group], bases))

    late, chunks = lax.optimization_barrier((came_columns[1], chunks))
    came = [[swap(chunks[0], 2 * k) for k in range(1, peers)]]
    other_columns.append([swap(array, 1) for array in late])
    came_columns[1] = late
    came.append([swap(chunks[1], 2 * k) for k in range(1, peers)])
    columns = []
    for k in range(peers - 1):
        for arrays in (came_columns, other_columns):
            columns += [part[k] for part in arrays]
    pieces = [([mine], 0)]
    for step in range(1, half - 1):
        pieces += [([up[step]], -step), ([down[step]], step)]
    grad_out = rows_of(pieces, None)
    up.append(lax.ppermute(up[-1], "fsdp", ahead))
    down.append(lax.ppermute(down[-1], "fsdp", behind))
    up[-1], down[-1], grad_out = lax.optimization_barrier((up[-1], down[-1], grad_out))
    if depth % 16 == 0:
        far_up, far_down = far_parts(up[-1], down[-1], cut)
    else:
        far_up, far_down = up[-1][:cut], down[-1][cut:]
    came[0], near_up, near_down, sent_up = lax.optimization_barrier((came[0], up[-1], down[-1], far_up))
    far_up = lax.ppermute(far_up, "fsdp", ahead)
    far_down = lax.ppermute(far_down, "fsdp", behind)

    def both_cores(arrays):
        return [a for c in arrays for a in (c, swap(c, 1))]

    def products(index, taken):
        group = groups[index]
        if not taken:
            return {o: bases[o] for o in group}
        result = partial_products(orders[index], starts[1:], taken, columns, window, [bases[o] for o in group])
        return dict(zip(group, result))

    terms = products(0, both_cores(came[0]))
    first = terms[half].astype(jnp.bfloat16)
    going_up, going_down, came[1], chunks, far_up, far_down = lax.optimization_barrier(
        (first[:cut], first[cut:], came[1], chunks, far_up, far_down)
    )
    came += [[swap(some, 2 * k) for k in range(1, peers)] for some in chunks[2:]]
    taken = both_cores(came[1])
    came_up = lax.ppermute(going_up, "fsdp", ahead)
    came_down = lax.ppermute(going_down, "fsdp", behind)

    bounds = [0, 3, 5, -(-(width // HS) // PAIR)]
    grads = None
    for step in range(half, 1, -1):
        if step == half:
            came_up, came_down, following = lax.optimization_barrier((came_up, came_down, products(1, taken)))
            terms.update(following)
            came_up = jnp.pad(came_up, ((0, depth - cut), (0, 0)))
            came_down = jnp.pad(came_down, ((cut, 0), (0, 0)))
        going_up = (terms[step - 1] + came_up.astype(jnp.float32)).astype(jnp.bfloat16)
        going_down = (terms[1 - step] + came_down.astype(jnp.float32)).astype(jnp.bfloat16)
        if step == half:
            going_up, going_down, near_up = lax.optimization_barrier((going_up, going_down, near_up))
            grad_out = rows_of([([near_up], 1 - half), ([near_down], half - 1), ([far_up, far_down], half)], grad_out, [sent_up])
            grad_mine = grad_out[0].reshape(width, rows)
            came[2], grad_other = lax.optimization_barrier((came[2], grad_out[1]))
            grad_other = swap(grad_other, 1).reshape(width, rows)
        elif step > 2:
            arrived = came[half - step + 1]
            going_up, going_down, arrived, grad_mine = lax.optimization_barrier((going_up, going_down, arrived, grad_mine))
            terms.update(products(half - step + 1, both_cores(arrived)))
        else:
            going_up, going_down = lax.optimization_barrier((going_up, going_down))
        came_up = lax.ppermute(going_up, "fsdp", ahead)
        came_down = lax.ppermute(going_down, "fsdp", behind)
    for low, high in zip(bounds, bounds[1:]):
        grads = backward(query_key_value, grad_mine, grad_other, main_probs, slot_probs, low, high, grads)
    came_up, came_down, grads = lax.optimization_barrier((came_up, came_down, grads))
    offsets = set()
    for m in range(members):
        low = min((m // 2) * 2 * owned // LANE * LANE, total - chip_width)
        offsets.add(m * owned - min(m * owned // LANE * LANE, low + chip_width - window))
    grad_proj = finish(table([member * owned - my_start]), terms[0], came_up, came_down, owned, sorted(offsets))
    return grads, grad_proj


def solution(mesh):
    members, shards = mesh.shape["dp"], mesh.shape["fsdp"]
    placed = (
        P(None, ("dp", "fsdp"), None),
        P(("dp", "fsdp"), None),
        P("fsdp", None),
        P(),
        P(None, "fsdp", None),
    )
    return jax.shard_map(
        functools.partial(local, members, shards),
        mesh=mesh,
        in_specs=placed,
        out_specs=(P(None, ("dp", "fsdp"), None), P("fsdp", "dp")),
        check_vma=False,
    )
```

```python
import functools

import jax
import jax.numpy as jnp
from jax import lax
from jax.experimental import pallas as pl
from jax.experimental.pallas import tpu as pltpu
from jax.sharding import PartitionSpec as P

HS = 128
MAIN = 256
SLOT = 96
LANE = 128
FACTOR = HS ** (-0.5)
MIB = 1024 * 1024


def lasting(microseconds):
    return pl.CostEstimate(flops=int(microseconds * 575000000), bytes_accessed=1000, transcendentals=0)


def dot(left, right, left_dim, right_dim):
    return lax.dot_general(left, right, (((left_dim,), (right_dim,)), ((), ())), preferred_element_type=jnp.float32)


def in_hbm(array):
    return pltpu.with_memory_space_constraint(array, pltpu.HBM)


def window_kernel(peers, starts, cotangent, layer_scale, *refs):
    windows, (held, sems) = refs[:-2], refs[-2:]
    parts = len(windows) // peers
    width = held.shape[2]
    copies = []
    for k in range(peers):
        at = pl.ds(pl.multiple_of(starts[k], LANE), width)
        first = 0
        for part in range(parts):
            rows = pl.ds(first, windows[part].shape[0])
            copies.append(pltpu.make_async_copy(cotangent.at[rows, at], held.at[k, rows], sems.at[k, part]))
            first += windows[part].shape[0]
    for copy in copies:
        copy.start()
    for k in range(peers):
        scale = layer_scale[:, pl.ds(pl.multiple_of(starts[k], LANE), width)]
        first = 0
        for part in range(parts):
            copies[k * parts + part].wait()
            window = windows[k * parts + part]
            values = held[k, first:first + window.shape[0], :].astype(jnp.float32)
            window[...] = (values * scale).astype(jnp.bfloat16)
            first += window.shape[0]


def peer_windows(starts, cotangent, layer_scale, peers, width):
    rows, total = cotangent.shape
    parts = (rows // 48 * 16 + 16, rows - rows // 48 * 16 - 16)
    arrays = pl.pallas_call(
        functools.partial(window_kernel, peers),
        grid_spec=pltpu.PrefetchScalarGridSpec(
            num_scalar_prefetch=1,
            grid=(1,),
            in_specs=[pl.BlockSpec(memory_space=pl.ANY), pl.BlockSpec((1, total), lambda i, s: (0, 0))],
            out_specs=[pl.BlockSpec((part, width), lambda i, s: (0, 0)) for part in parts] * peers,
            scratch_shapes=[
                pltpu.VMEM((peers, rows, width), jnp.bfloat16),
                pltpu.SemaphoreType.DMA((peers, len(parts))),
            ],
        ),
        out_shape=[pltpu.HBM((part, width), jnp.bfloat16) for part in parts] * peers,
        compiler_params=pltpu.CompilerParams(vmem_limit_bytes=8 * MIB),
        cost_estimate=lasting(60),
        name="peer_windows",
    )(starts, in_hbm(cotangent), layer_scale)
    return [arrays[part::len(parts)] for part in range(len(parts))]


def prepare_kernel(cotangent, layer_scale, turned):
    values = (cotangent[...].astype(jnp.float32) * layer_scale[...]).astype(jnp.bfloat16)
    spare = jnp.zeros((turned.shape[1] - values.shape[0], values.shape[1]), jnp.bfloat16)
    turned[...] = jnp.concatenate([values, spare], axis=0).T


def prepare(cotangent, layer_scale):
    rows, total = cotangent.shape
    lanes = -(-rows // LANE) * LANE
    steps = 5
    block = total // steps
    return pl.pallas_call(
        prepare_kernel,
        grid=(steps,),
        in_specs=[pl.BlockSpec((rows, block), lambda i: (0, i)), pl.BlockSpec((1, block), lambda i: (0, i))],
        out_specs=pl.BlockSpec((block, lanes), lambda i: (i, 0)),
        out_shape=pltpu.HBM((total, lanes), jnp.bfloat16),
        compiler_params=pltpu.CompilerParams(vmem_limit_bytes=8 * MIB),
        cost_estimate=lasting(60),
        name="scaled_cotangent",
    )(in_hbm(cotangent), layer_scale)


def arrange_kernel(sizes, order, attended, *refs):
    *outs, sems = refs
    copies = []
    for out, size in zip(outs, sizes):
        for j in range(size):
            n = len(copies)
            copies.append(pltpu.make_async_copy(attended.at[order[n]], out.at[j], sems.at[n]))
    for copy in copies:
        copy.start()
    for copy in copies:
        copy.wait()


def arrange(order, attended, sizes):
    _, depth, rows = attended.shape
    return pl.pallas_call(
        functools.partial(arrange_kernel, sizes),
        grid_spec=pltpu.PrefetchScalarGridSpec(
            num_scalar_prefetch=1,
            grid=(1,),
            in_specs=[pl.BlockSpec(memory_space=pl.ANY)],
            out_specs=[pl.BlockSpec((size, depth, rows), lambda i, o: (0, 0, 0)) for size in sizes],
            scratch_shapes=[pltpu.SemaphoreType.DMA((sum(sizes),))],
        ),
        out_shape=[jax.ShapeDtypeStruct((size, depth, rows), attended.dtype) for size in sizes],
        compiler_params=pltpu.CompilerParams(vmem_limit_bytes=6 * MIB),
        cost_estimate=lasting(2),
        name="attended_chunks",
    )(order, in_hbm(attended))


def far_kernel(up, down, out_up, out_down, sems):
    cut = out_up.shape[0]
    copies = [
        pltpu.make_async_copy(up.at[pl.ds(0, cut)], out_up, sems.at[0]),
        pltpu.make_async_copy(down.at[pl.ds(cut, out_down.shape[0])], out_down, sems.at[1]),
    ]
    for copy in copies:
        copy.start()
    for copy in copies:
        copy.wait()


def far_parts(up, down, cut):
    depth, width = up.shape
    sizes = (cut, depth - cut)
    return pl.pallas_call(
        far_kernel,
        grid=(1,),
        in_specs=[pl.BlockSpec(memory_space=pl.ANY)] * 2,
        out_specs=[pl.BlockSpec((size, width), lambda i: (0, 0)) for size in sizes],
        out_shape=[jax.ShapeDtypeStruct((size, width), up.dtype) for size in sizes],
        scratch_shapes=[pltpu.SemaphoreType.DMA((2,))],
        compiler_params=pltpu.CompilerParams(vmem_limit_bytes=4 * MIB),
        cost_estimate=lasting(1),
        name="far_parts",
    )(up, down)


PAIR = 2
EXPONENT = FACTOR * 1.4426950408889634


def forward_kernel(counts, qkv, attended, main_probs, slot_probs):
    def marks(image, ids):
        lane = lax.broadcasted_iota(jnp.int32, (image.shape[0], HS), 1)
        first = jnp.where(image == ids[0], 1.0, 0.0)
        second = jnp.where(image == ids[1], 1.0, 0.0)
        own = jnp.where(lane == 0, first, jnp.where(lane == 1, second, 0.0))
        other = jnp.where(lane == 0, 1.0 - first, jnp.where(lane == 1, 1.0 - second, 0.0)) * -1e30
        return own.astype(jnp.bfloat16), other.astype(jnp.bfloat16)

    main_at = lax.broadcasted_iota(jnp.int32, (MAIN, HS), 0)
    main_marks = marks(jnp.where(main_at >= counts[0], 1, 0), (0, 1))

    def image(at):
        first = jnp.where(at < counts[2], 2, -1)
        return jnp.where(at < SLOT, first, jnp.where(at - SLOT < counts[3], 3, -1))

    slot_marks = marks(image(lax.broadcasted_iota(jnp.int32, (2 * SLOT, HS), 0)), (2, 3))
    valid = image(lax.broadcasted_iota(jnp.int32, (1, 2 * SLOT), 1)) >= 0
    parts = []
    for head in range(PAIR):
        lanes = slice(head * HS, (head + 1) * HS)
        parts.append((head, 0, MAIN, lanes, main_marks, None, main_probs))
        parts.append((head, MAIN, 2 * SLOT, lanes, slot_marks, valid, slot_probs))
    scores = []
    for head, first, rows, lanes, (mark_query, mark_key), _, _ in parts:
        query = jnp.concatenate([qkv[0, first:first + rows, lanes], mark_query], axis=1)
        key = jnp.concatenate([qkv[1, first:first + rows, lanes], mark_key], axis=1)
        scores.append(dot(key, query, 1, 1))
    probs = []
    for score, (_, _, _, _, _, good, _) in zip(scores, parts):
        weights = jnp.exp2((score - jnp.max(score, axis=0, keepdims=True)) * EXPONENT)
        scale = 1.0 / jnp.sum(weights, axis=0, keepdims=True)
        probs.append(weights * (scale if good is None else jnp.where(good, scale, 0.0)))
    for prob, (head, first, rows, lanes, _, _, probs_ref) in zip(probs, parts):
        probs_ref[head] = prob
        result = dot(qkv[2, first:first + rows, lanes], prob.astype(jnp.bfloat16), 0, 0)
        attended[lanes, first:first + rows] = result.astype(jnp.bfloat16)


def forward(counts, qkv):
    _, rows, width = qkv.shape
    heads = width // HS
    return pl.pallas_call(
        forward_kernel,
        grid_spec=pltpu.PrefetchScalarGridSpec(
            num_scalar_prefetch=1,
            grid=(-(-heads // PAIR),),
            in_specs=[pl.BlockSpec((3, rows, PAIR * HS), lambda h, c: (0, 0, h))],
            out_specs=[
                pl.BlockSpec((PAIR * HS, rows), lambda h, c: (h, 0)),
                pl.BlockSpec((PAIR, MAIN, MAIN), lambda h, c: (h, 0, 0)),
                pl.BlockSpec((PAIR, 2 * SLOT, 2 * SLOT), lambda h, c: (h, 0, 0)),
            ],
        ),
        out_shape=[
            pltpu.HBM((width, rows), jnp.bfloat16),
            pltpu.HBM((heads, MAIN, MAIN), jnp.float32),
            pltpu.HBM((heads, 2 * SLOT, 2 * SLOT), jnp.float32),
        ],
        compiler_params=pltpu.CompilerParams(vmem_limit_bytes=12 * MIB),
        cost_estimate=lasting(60),
        name="attention_forward",
    )(counts, qkv)


def backward_kernel(qkv, grad_mine, grad_other, main_probs, slot_probs, *rest):
    grads = rest[-1]
    parts = []
    for head in range(PAIR):
        lanes = slice(head * HS, (head + 1) * HS)
        for first, rows, probs_ref in ((0, MAIN, main_probs), (MAIN, 2 * SLOT, slot_probs)):
            parts.append((head, slice(first, first + rows), lanes, probs_ref))
    grad, dprobs, dscores = [], [], []
    for head, at, lanes, _ in parts:
        both = grad_mine[lanes, at] + grad_other[lanes, at].astype(jnp.float32)
        grad.append(both.astype(jnp.bfloat16))
    for g, (head, at, lanes, _) in zip(grad, parts):
        dprobs.append(dot(qkv[2, at, lanes], g, 1, 0))
    for g, (head, at, lanes, probs_ref) in zip(grad, parts):
        grads[2, at, lanes] = dot(probs_ref[head].astype(jnp.bfloat16), g, 1, 1).astype(jnp.bfloat16)
    for dprob, (head, at, lanes, probs_ref) in zip(dprobs, parts):
        probs = probs_ref[head]
        delta = jnp.sum(probs * dprob, axis=0, keepdims=True)
        dscores.append((probs * (dprob - delta) * FACTOR).astype(jnp.bfloat16))
    for dscore, (head, at, lanes, _) in zip(dscores, parts):
        grads[1, at, lanes] = dot(dscore, qkv[0, at, lanes], 1, 0).astype(jnp.bfloat16)
        grads[0, at, lanes] = dot(dscore, qkv[1, at, lanes], 0, 0).astype(jnp.bfloat16)


def backward(qkv, grad_mine, grad_other, main_probs, slot_probs, low, high, grads):
    _, rows, width = qkv.shape
    held = [] if grads is None else [grads]
    return pl.pallas_call(
        backward_kernel,
        grid=(high - low,),
        in_specs=[
            pl.BlockSpec((3, rows, PAIR * HS), lambda h: (0, 0, h + low)),
            pl.BlockSpec((PAIR * HS, rows), lambda h: (h + low, 0)),
            pl.BlockSpec((PAIR * HS, rows), lambda h: (h + low, 0)),
            pl.BlockSpec((PAIR, MAIN, MAIN), lambda h: (h + low, 0, 0)),
            pl.BlockSpec((PAIR, 2 * SLOT, 2 * SLOT), lambda h: (h + low, 0, 0)),
        ] + [pl.BlockSpec(memory_space=pl.ANY)] * len(held),
        out_specs=pl.BlockSpec((3, rows, PAIR * HS), lambda h: (0, 0, h + low)),
        out_shape=pltpu.HBM(qkv.shape, jnp.bfloat16),
        input_output_aliases={5: 0} if held else {},
        compiler_params=pltpu.CompilerParams(vmem_limit_bytes=14 * MIB),
        cost_estimate=lasting(2 * (high - low)),
        name="attention_backward",
    )(qkv, grad_mine, grad_other, main_probs, slot_probs, *map(in_hbm, held))


def grad_out_kernel(sizes, split, total, info, turned, turned_other, *refs):
    mine, other, columns, tall, mine_rows, other_rows, in_sems, out_sems = refs[-8:]
    count, depth, rows = mine_rows.shape
    core = info[0]
    at = pl.ds(pl.multiple_of(core * (total - split), LANE), split)
    loads = [
        pltpu.make_async_copy(source.at[at], columns.at[i], in_sems.at[i]) for i, source in enumerate((turned, turned_other))
    ]
    index = 0
    for j, size in enumerate(sizes):
        first = 0
        for piece in refs[index:index + size]:
            target = tall.at[j] if size == 1 else tall.at[j, pl.ds(first, piece.shape[0])]
            loads.append(pltpu.make_async_copy(piece, target, in_sems.at[len(loads)]))
            first += piece.shape[0]
        index += size
    for load in loads:
        load.start()
    for load in loads:
        load.wait()

    @pl.when(core == 1)
    def _():
        shared = 2 * split - total
        columns[:, :shared, :] = jnp.zeros((2, shared, columns.shape[2]), jnp.bfloat16)

    stores = []
    for i, (result, out) in enumerate(((mine_rows, mine), (other_rows, other))):
        if depth % 16 == 0:
            product = dot(tall[...].reshape(count * depth, split), columns[i], 1, 0)[:, :rows]
            result[...] = product.astype(result.dtype).reshape(count, depth, rows)
        else:
            for j in range(count):
                result[j] = dot(tall[j], columns[i], 1, 0)[:, :rows].astype(result.dtype)
        for j in range(count):
            stores.append(pltpu.make_async_copy(result.at[j], out.at[info[1 + j]], out_sems.at[i, j]))
            stores[-1].start()
    for store in stores:
        store.wait()


def grad_out_rows(info, turned, turned_other, rows, pieces, shards, held, after=()):
    total, lanes = turned.shape
    split = pieces[0][0].shape[1]
    depth = sum(p.shape[0] for p in pieces[0])
    sizes = [len(p) for p in pieces]
    arrays = [a for p in pieces for a in p]
    count = len(pieces)
    held = [] if held is None else list(held)
    return pl.pallas_call(
        functools.partial(grad_out_kernel, sizes, split, total),
        grid_spec=pltpu.PrefetchScalarGridSpec(
            num_scalar_prefetch=1,
            grid=(1,),
            in_specs=[pl.BlockSpec(memory_space=pl.ANY)] * (2 + len(arrays) + len(held) + len(after)),
            out_specs=[pl.BlockSpec(memory_space=pl.ANY)] * 2,
            scratch_shapes=[
                pltpu.VMEM((2, split, lanes), jnp.bfloat16),
                pltpu.VMEM((count, depth, split), jnp.bfloat16),
                pltpu.VMEM((count, depth, rows), jnp.float32),
                pltpu.VMEM((count, depth, rows), jnp.bfloat16),
                pltpu.SemaphoreType.DMA((2 + len(arrays),)),
                pltpu.SemaphoreType.DMA((2, count)),
            ],
        ),
        out_shape=[
            pltpu.HBM((shards, depth, rows), jnp.float32),
            pltpu.HBM((shards, depth, rows), jnp.bfloat16),
        ],
        input_output_aliases={3 + len(arrays) + i: i for i in range(len(held))},
        compiler_params=pltpu.CompilerParams(vmem_limit_bytes=16 * MIB),
        cost_estimate=lasting(0.2 if held else 1.5 * len(pieces)),
        name="grad_out_rows",
    )(info, in_hbm(turned), turned_other, *arrays, *map(in_hbm, held), *after)


def half_kernel(starts, weight, out, sem):
    copy = pltpu.make_async_copy(weight.at[:, pl.ds(pl.multiple_of(starts[0], LANE), out.shape[1])], out, sem)
    copy.start()
    copy.wait()


def half_columns(start, weight, width):
    return pl.pallas_call(
        half_kernel,
        grid_spec=pltpu.PrefetchScalarGridSpec(
            num_scalar_prefetch=1,
            grid=(1,),
            in_specs=[pl.BlockSpec(memory_space=pl.ANY)],
            out_specs=pl.BlockSpec(memory_space=pl.ANY),
            scratch_shapes=[pltpu.SemaphoreType.DMA],
        ),
        out_shape=jax.ShapeDtypeStruct((weight.shape[0], width), weight.dtype),
        compiler_params=pltpu.CompilerParams(vmem_limit_bytes=2 * MIB),
        cost_estimate=lasting(1),
        name="own_half_of_weight",
    )(start, in_hbm(weight))


def finish_kernel(offsets, start, term, came_up, came_down, out):
    total = term[...] + came_up[...].astype(jnp.float32) + came_down[...].astype(jnp.float32)
    for offset in offsets:

        @pl.when(start[0] == offset)
        def _():
            out[...] = total[:, offset:offset + out.shape[1]]


def finish(start, term, came_up, came_down, owned, offsets):
    depth, window = term.shape
    block = pl.BlockSpec((depth, window), lambda i, s: (0, 0))
    return pl.pallas_call(
        functools.partial(finish_kernel, offsets),
        grid_spec=pltpu.PrefetchScalarGridSpec(
            num_scalar_prefetch=1,
            grid=(1,),
            in_specs=[block] * 3,
            out_specs=pl.BlockSpec((depth, owned), lambda i, s: (0, 0)),
        ),
        out_shape=jax.ShapeDtypeStruct((depth, owned), jnp.float32),
        compiler_params=pltpu.CompilerParams(vmem_limit_bytes=8 * MIB),
        cost_estimate=lasting(2),
        name="last_sum",
    )(start, term, came_up, came_down)


def partial_kernel(chosen, sources, parts, count, window, order, start, *refs):
    attended, columns = refs[:sources], refs[sources:sources * (1 + parts)]
    chunks, held, sems = refs[-3:]
    bases = refs[sources * (1 + parts):-3 - count]
    outs = refs[-3 - count:-3]
    depth, rows = chunks.shape[2:]
    at = pl.ds(pl.multiple_of(start[0], LANE), window)
    copies = []
    for i in range(sources):
        some, first = [], 0
        for part in range(parts):
            source = columns[i * parts + part]
            if chosen:
                some.append(pltpu.make_async_copy(source.at[at], held.at[i], sems.at[i, count + part]))
            else:
                target = held.at[i, pl.ds(first, source.shape[0])]
                some.append(pltpu.make_async_copy(source.at[:, at], target, sems.at[i, count + part]))
            first += source.shape[0]
        for j in range(count):
            source = attended[i].at[order[j] if chosen else j]
            some.append(pltpu.make_async_copy(source, chunks.at[i, j], sems.at[i, j]))
        copies.append(some)
    for some in copies:
        for copy in some:
            copy.start()
    most = 4 if depth % 16 == 0 else 1
    for first in range(0, count, most):
        some = min(most, count - first)
        total = None
        for i in range(sources):
            if first == 0:
                for copy in copies[i]:
                    copy.wait()
            tall = chunks[i, first:first + some].reshape(some * depth, rows) if some > 1 else chunks[i, first]
            part = dot(tall, held[i][:, :rows], 1, 1) if chosen else dot(tall, held[i], 1, 0)
            total = part if total is None else total + part
        for j in range(some):
            result = total[j * depth:(j + 1) * depth]
            if bases:
                result += bases[first + j][...].astype(jnp.float32)
            outs[first + j][...] = result.astype(outs[first + j].dtype)


def partial_products(order, start, attended, columns, window, bases=()):
    _, depth, rows = attended[0].shape
    parts = len(columns) // len(attended)
    count, sources = order.shape[0], len(attended)
    block = pl.BlockSpec((depth, window), lambda j, o, s: (0, 0))
    return pl.pallas_call(
        functools.partial(partial_kernel, not bases, sources, parts, count, window),
        grid_spec=pltpu.PrefetchScalarGridSpec(
            num_scalar_prefetch=2,
            grid=(1,),
            in_specs=[pl.BlockSpec(memory_space=pl.ANY)] * (sources * (1 + parts)) + [block] * len(bases),
            out_specs=[block] * count,
            scratch_shapes=[
                pltpu.VMEM((sources, count, depth, rows), jnp.bfloat16),
                pltpu.VMEM((sources, rows, window) if bases else (sources, window, columns[0].shape[1]), jnp.bfloat16),
                pltpu.SemaphoreType.DMA((sources, count + parts)),
            ],
        ),
        out_shape=[
            jax.ShapeDtypeStruct((depth, window), jnp.float32) if bases else pltpu.HBM((depth, window), jnp.bfloat16)
        ] * count,
        compiler_params=pltpu.CompilerParams(vmem_limit_bytes=(16 if bases else 18) * MIB),
        cost_estimate=lasting(3 if bases else 6),
        name="projection_peers" if bases else "projection_chip",
    )(order, start, *attended, *columns, *map(in_hbm, bases))


def windows_of(groups, owned, total):
    lows = [g * owned // LANE * LANE for g in range(groups)]
    width = max(-(-((g + 1) * owned) // LANE) * LANE - low for g, low in enumerate(lows))
    return width


def ring_of(count):
    return list(range(0, count, 2)) + list(range(count - 1, 0, -2))


def local(members, shards, query_key_value, cotangent, proj_weight, layer_scale, lengths):
    member = lax.axis_index("dp")
    shard = lax.axis_index("fsdp")
    core, chip, peers = member % 2, member // 2, members // 2
    ring = ring_of(shards)
    place = jnp.where(shard % 2 == 0, shard // 2, shards - 1 - shard // 2)
    ahead = [(ring[i], ring[(i + 1) % shards]) for i in range(shards)]
    behind = [(ring[i], ring[(i - 1) % shards]) for i in range(shards)]
    half = shards // 2
    depth, total = proj_weight.shape
    rows, width = query_key_value.shape[1:]
    owned = total // members
    counts = lax.dynamic_index_in_dim(lengths[:, 0, :], member, 0, keepdims=False)

    def swap(array, bit):
        return lax.ppermute(array, "dp", [(i, i ^ bit) for i in range(members)])

    def shard_at(offset):
        at = (place + offset + shards) % shards
        return jnp.where(at < half, 2 * at, 2 * (shards - 1 - at) + 1)

    def table(values):
        return jnp.stack([jnp.asarray(v) for v in values]).astype(jnp.int32)

    chip_width, window = windows_of(peers, 2 * owned, total), windows_of(members, owned, total)

    def chip_start(chip):
        return jnp.minimum(chip * 2 * owned // LANE * LANE, total - chip_width)

    my_start = jnp.minimum(member * owned // LANE * LANE, chip_start(chip) + chip_width - window)
    starts = table([my_start, my_start - chip_start(chip)])

    split = -(-(total // LANE) // 2) * LANE
    mine = half_columns(table([core * (total - split)]), proj_weight, split)
    cut = -(-depth // 32) * 16
    up, down = [mine], [mine]
    up.append(lax.ppermute(up[-1], "fsdp", ahead))
    down.append(lax.ppermute(down[-1], "fsdp", behind))

    mine, cotangent = lax.optimization_barrier((mine, cotangent))
    scales = layer_scale.reshape(1, total)
    sent = peer_windows(
        table([chip_start(chip ^ k) for k in range(1, peers)] or [0]), cotangent, scales, peers - 1, chip_width
    )
    sent, cotangent = lax.optimization_barrier((sent, cotangent))
    came_columns = [[swap(array, 2 * k) for k, array in enumerate(part, 1)] for part in sent]
    turned = prepare(cotangent, scales)
    attended, main_probs, slot_probs = forward(counts, query_key_value)
    attended = attended.reshape(shards, depth, rows)
    near = [[o, -o] for o in range(half - 1, 0, -1)]
    groups = [[half] + near[0]] + near[1:-1] + [near[-1] + [0]]
    flat = table([shard_at(o) for group in groups for o in group])
    sizes = [len(group) for group in groups]
    orders = [flat[sum(sizes[:g]):sum(sizes[:g + 1])] for g in range(len(groups))]

    def rows_of(some, held, after=()):
        info = table([core] + [shard_at(o) for _, o in some])
        return grad_out_rows(info, turned, turned_other, rows, [p for p, _ in some], shards, held, after)

    up[1], down[1], attended, came_columns[0], turned = lax.optimization_barrier(
        (up[1], down[1], attended, came_columns[0], turned)
    )
    turned_other = swap(turned, 1)
    other_columns = [[swap(array, 1) for array in came_columns[0]]]
    attended_other = swap(attended, 1)
    chunks = list(arrange(flat, attended, sizes))
    attended_other, chunks = lax.optimization_barrier((attended_other, chunks))
    for _ in range(half - 3):
        up.append(lax.ppermute(up[-1], "fsdp", ahead))
        down.append(lax.ppermute(down[-1], "fsdp", behind))
    bases = partial_products(
        flat, starts[:1], [in_hbm(attended), attended_other], [in_hbm(turned), turned_other], window
    )
    up[-1], down[-1], turned_other, attended_other, *bases = lax.optimization_barrier(
        (up[-1], down[-1], turned_other, attended_other, *bases)
    )
    bases = dict(zip([o for group in groups for o in group], bases))

    late, chunks = lax.optimization_barrier((came_columns[1], chunks))
    came = [[swap(chunks[0], 2 * k) for k in range(1, peers)]]
    other_columns.append([swap(array, 1) for array in late])
    came_columns[1] = late
    came.append([swap(chunks[1], 2 * k) for k in range(1, peers)])
    columns = []
    for k in range(peers - 1):
        for arrays in (came_columns, other_columns):
            columns += [part[k] for part in arrays]
    pieces = [([mine], 0)]
    for step in range(1, half - 1):
        pieces += [([up[step]], -step), ([down[step]], step)]
    grad_out = rows_of(pieces, None)
    up.append(lax.ppermute(up[-1], "fsdp", ahead))
    down.append(lax.ppermute(down[-1], "fsdp", behind))
    up[-1], down[-1], grad_out = lax.optimization_barrier((up[-1], down[-1], grad_out))
    if depth % 16 == 0:
        far_up, far_down = far_parts(up[-1], down[-1], cut)
    else:
        far_up, far_down = up[-1][:cut], down[-1][cut:]
    came[0], near_up, near_down, sent_up = lax.optimization_barrier((came[0], up[-1], down[-1], far_up))
    far_up = lax.ppermute(far_up, "fsdp", ahead)
    far_down = lax.ppermute(far_down, "fsdp", behind)

    def both_cores(arrays):
        return [a for c in arrays for a in (c, swap(c, 1))]

    def products(index, taken):
        group = groups[index]
        if not taken:
            return {o: bases[o] for o in group}
        result = partial_products(orders[index], starts[1:], taken, columns, window, [bases[o] for o in group])
        return dict(zip(group, result))

    terms = products(0, both_cores(came[0]))
    first = terms[half].astype(jnp.bfloat16)
    going_up, going_down, came[1], chunks, far_up, far_down = lax.optimization_barrier(
        (first[:cut], first[cut:], came[1], chunks, far_up, far_down)
    )
    came += [[swap(some, 2 * k) for k in range(1, peers)] for some in chunks[2:]]
    taken = both_cores(came[1])
    came_up = lax.ppermute(going_up, "fsdp", ahead)
    came_down = lax.ppermute(going_down, "fsdp", behind)

    bounds = [0, 3, 5, -(-(width // HS) // PAIR)]
    grads = None
    for step in range(half, 1, -1):
        if step == half:
            came_up, came_down, following = lax.optimization_barrier((came_up, came_down, products(1, taken)))
            terms.update(following)
            came_up = jnp.pad(came_up, ((0, depth - cut), (0, 0)))
            came_down = jnp.pad(came_down, ((cut, 0), (0, 0)))
        going_up = (terms[step - 1] + came_up.astype(jnp.float32)).astype(jnp.bfloat16)
        going_down = (terms[1 - step] + came_down.astype(jnp.float32)).astype(jnp.bfloat16)
        if step == half:
            going_up, going_down, near_up = lax.optimization_barrier((going_up, going_down, near_up))
            grad_out = rows_of([([near_up], 1 - half), ([near_down], half - 1), ([far_up, far_down], half)], grad_out, [sent_up])
            grad_mine = grad_out[0].reshape(width, rows)
            came[2], grad_other = lax.optimization_barrier((came[2], grad_out[1]))
            grad_other = swap(grad_other, 1).reshape(width, rows)
        elif step > 2:
            arrived = came[half - step + 1]
            going_up, going_down, arrived, grad_mine = lax.optimization_barrier((going_up, going_down, arrived, grad_mine))
            terms.update(products(half - step + 1, both_cores(arrived)))
        else:
            going_up, going_down = lax.optimization_barrier((going_up, going_down))
        came_up = lax.ppermute(going_up, "fsdp", ahead)
        came_down = lax.ppermute(going_down, "fsdp", behind)
    for low, high in zip(bounds, bounds[1:]):
        grads = backward(query_key_value, grad_mine, grad_other, main_probs, slot_probs, low, high, grads)
    came_up, came_down, grads = lax.optimization_barrier((came_up, came_down, grads))
    offsets = set()
    for m in range(members):
        low = min((m // 2) * 2 * owned // LANE * LANE, total - chip_width)
        offsets.add(m * owned - min(m * owned // LANE * LANE, low + chip_width - window))
    grad_proj = finish(table([member * owned - my_start]), terms[0], came_up, came_down, owned, sorted(offsets))
    return grads, grad_proj


def solution(mesh):
    members, shards = mesh.shape["dp"], mesh.shape["fsdp"]
    placed = (
        P(None, ("dp", "fsdp"), None),
        P(("dp", "fsdp"), None),
        P("fsdp", None),
        P(),
        P(None, "fsdp", None),
    )
    return jax.shard_map(
        functools.partial(local, members, shards),
        mesh=mesh,
        in_specs=placed,
        out_specs=(P(None, ("dp", "fsdp"), None), P("fsdp", "dp")),
        check_vma=False,
    )
```

```python
import functools

import jax
import jax.numpy as jnp
from jax import lax
from jax.experimental import pallas as pl
from jax.experimental.pallas import tpu as pltpu
from jax.sharding import PartitionSpec as P

HS = 128
MAIN = 256
SLOT = 96
LANE = 128
FACTOR = HS ** (-0.5)
MIB = 1024 * 1024


def lasting(microseconds):
    return pl.CostEstimate(flops=int(microseconds * 575000000), bytes_accessed=1000, transcendentals=0)


def dot(left, right, left_dim, right_dim):
    return lax.dot_general(left, right, (((left_dim,), (right_dim,)), ((), ())), preferred_element_type=jnp.float32)


def in_hbm(array):
    return pltpu.with_memory_space_constraint(array, pltpu.HBM)


def window_kernel(peers, starts, cotangent, layer_scale, *refs):
    windows, (held, sems) = refs[:-2], refs[-2:]
    parts = len(windows) // peers
    width = held.shape[2]
    copies = []
    for k in range(peers):
        at = pl.ds(pl.multiple_of(starts[k], LANE), width)
        first = 0
        for part in range(parts):
            rows = pl.ds(first, windows[part].shape[0])
            copies.append(pltpu.make_async_copy(cotangent.at[rows, at], held.at[k, rows], sems.at[k, part]))
            first += windows[part].shape[0]
    for copy in copies:
        copy.start()
    for k in range(peers):
        scale = layer_scale[:, pl.ds(pl.multiple_of(starts[k], LANE), width)]
        first = 0
        for part in range(parts):
            copies[k * parts + part].wait()
            window = windows[k * parts + part]
            values = held[k, first:first + window.shape[0], :].astype(jnp.float32)
            window[...] = (values * scale).astype(jnp.bfloat16)
            first += window.shape[0]


def peer_windows(starts, cotangent, layer_scale, peers, width):
    rows, total = cotangent.shape
    parts = (rows // 48 * 16 + 16, rows - rows // 48 * 16 - 16)
    arrays = pl.pallas_call(
        functools.partial(window_kernel, peers),
        grid_spec=pltpu.PrefetchScalarGridSpec(
            num_scalar_prefetch=1,
            grid=(1,),
            in_specs=[pl.BlockSpec(memory_space=pl.ANY), pl.BlockSpec((1, total), lambda i, s: (0, 0))],
            out_specs=[pl.BlockSpec((part, width), lambda i, s: (0, 0)) for part in parts] * peers,
            scratch_shapes=[
                pltpu.VMEM((peers, rows, width), jnp.bfloat16),
                pltpu.SemaphoreType.DMA((peers, len(parts))),
            ],
        ),
        out_shape=[pltpu.HBM((part, width), jnp.bfloat16) for part in parts] * peers,
        compiler_params=pltpu.CompilerParams(vmem_limit_bytes=8 * MIB),
        cost_estimate=lasting(60),
        name="peer_windows",
    )(starts, in_hbm(cotangent), layer_scale)
    return [arrays[part::len(parts)] for part in range(len(parts))]


def prepare_kernel(cotangent, layer_scale, turned):
    values = (cotangent[...].astype(jnp.float32) * layer_scale[...]).astype(jnp.bfloat16)
    spare = jnp.zeros((turned.shape[1] - values.shape[0], values.shape[1]), jnp.bfloat16)
    turned[...] = jnp.concatenate([values, spare], axis=0).T


def prepare(cotangent, layer_scale):
    rows, total = cotangent.shape
    lanes = -(-rows // LANE) * LANE
    steps = 5
    block = total // steps
    return pl.pallas_call(
        prepare_kernel,
        grid=(steps,),
        in_specs=[pl.BlockSpec((rows, block), lambda i: (0, i)), pl.BlockSpec((1, block), lambda i: (0, i))],
        out_specs=pl.BlockSpec((block, lanes), lambda i: (i, 0)),
        out_shape=pltpu.HBM((total, lanes), jnp.bfloat16),
        compiler_params=pltpu.CompilerParams(vmem_limit_bytes=8 * MIB),
        cost_estimate=lasting(60),
        name="scaled_cotangent",
    )(in_hbm(cotangent), layer_scale)


def arrange_kernel(sizes, order, attended, *refs):
    *outs, sems = refs
    copies = []
    for out, size in zip(outs, sizes):
        for j in range(size):
            n = len(copies)
            copies.append(pltpu.make_async_copy(attended.at[order[n]], out.at[j], sems.at[n]))
    for copy in copies:
        copy.start()
    for copy in copies:
        copy.wait()


def arrange(order, attended, sizes):
    _, depth, rows = attended.shape
    return pl.pallas_call(
        functools.partial(arrange_kernel, sizes),
        grid_spec=pltpu.PrefetchScalarGridSpec(
            num_scalar_prefetch=1,
            grid=(1,),
            in_specs=[pl.BlockSpec(memory_space=pl.ANY)],
            out_specs=[pl.BlockSpec((size, depth, rows), lambda i, o: (0, 0, 0)) for size in sizes],
            scratch_shapes=[pltpu.SemaphoreType.DMA((sum(sizes),))],
        ),
        out_shape=[jax.ShapeDtypeStruct((size, depth, rows), attended.dtype) for size in sizes],
        compiler_params=pltpu.CompilerParams(vmem_limit_bytes=6 * MIB),
        cost_estimate=lasting(2),
        name="attended_chunks",
    )(order, in_hbm(attended))


def far_kernel(up, down, out_up, out_down, sems):
    cut = out_up.shape[0]
    copies = [
        pltpu.make_async_copy(up.at[pl.ds(0, cut)], out_up, sems.at[0]),
        pltpu.make_async_copy(down.at[pl.ds(cut, out_down.shape[0])], out_down, sems.at[1]),
    ]
    for copy in copies:
        copy.start()
    for copy in copies:
        copy.wait()


def far_parts(up, down, cut):
    depth, width = up.shape
    sizes = (cut, depth - cut)
    return pl.pallas_call(
        far_kernel,
        grid=(1,),
        in_specs=[pl.BlockSpec(memory_space=pl.ANY)] * 2,
        out_specs=[pl.BlockSpec((size, width), lambda i: (0, 0)) for size in sizes],
        out_shape=[jax.ShapeDtypeStruct((size, width), up.dtype) for size in sizes],
        scratch_shapes=[pltpu.SemaphoreType.DMA((2,))],
        compiler_params=pltpu.CompilerParams(vmem_limit_bytes=4 * MIB),
        cost_estimate=lasting(1),
        name="far_parts",
    )(up, down)


PAIR = 2
EXPONENT = FACTOR * 1.4426950408889634


def forward_kernel(counts, qkv, attended, main_probs, slot_probs):
    def marks(image, ids):
        lane = lax.broadcasted_iota(jnp.int32, (image.shape[0], HS), 1)
        first = jnp.where(image == ids[0], 1.0, 0.0)
        second = jnp.where(image == ids[1], 1.0, 0.0)
        own = jnp.where(lane == 0, first, jnp.where(lane == 1, second, 0.0))
        other = jnp.where(lane == 0, 1.0 - first, jnp.where(lane == 1, 1.0 - second, 0.0)) * -1e30
        return own.astype(jnp.bfloat16), other.astype(jnp.bfloat16)

    main_at = lax.broadcasted_iota(jnp.int32, (MAIN, HS), 0)
    main_marks = marks(jnp.where(main_at >= counts[0], 1, 0), (0, 1))

    def image(at):
        first = jnp.where(at < counts[2], 2, -1)
        return jnp.where(at < SLOT, first, jnp.where(at - SLOT < counts[3], 3, -1))

    slot_marks = marks(image(lax.broadcasted_iota(jnp.int32, (2 * SLOT, HS), 0)), (2, 3))
    valid = image(lax.broadcasted_iota(jnp.int32, (1, 2 * SLOT), 1)) >= 0
    parts = []
    for head in range(PAIR):
        lanes = slice(head * HS, (head + 1) * HS)
        parts.append((head, 0, MAIN, lanes, main_marks, None, main_probs))
        parts.append((head, MAIN, 2 * SLOT, lanes, slot_marks, valid, slot_probs))
    scores = []
    for head, first, rows, lanes, (mark_query, mark_key), _, _ in parts:
        query = jnp.concatenate([qkv[0, first:first + rows, lanes], mark_query], axis=1)
        key = jnp.concatenate([qkv[1, first:first + rows, lanes], mark_key], axis=1)
        scores.append(dot(key, query, 1, 1))
    probs = []
    for score, (_, _, _, _, _, good, _) in zip(scores, parts):
        weights = jnp.exp2((score - jnp.max(score, axis=0, keepdims=True)) * EXPONENT)
        scale = 1.0 / jnp.sum(weights, axis=0, keepdims=True)
        probs.append(weights * (scale if good is None else jnp.where(good, scale, 0.0)))
    for prob, (head, first, rows, lanes, _, _, probs_ref) in zip(probs, parts):
        probs_ref[head] = prob
        result = dot(qkv[2, first:first + rows, lanes], prob.astype(jnp.bfloat16), 0, 0)
        attended[lanes, first:first + rows] = result.astype(jnp.bfloat16)


def forward(counts, qkv):
    _, rows, width = qkv.shape
    heads = width // HS
    return pl.pallas_call(
        forward_kernel,
        grid_spec=pltpu.PrefetchScalarGridSpec(
            num_scalar_prefetch=1,
            grid=(-(-heads // PAIR),),
            in_specs=[pl.BlockSpec((3, rows, PAIR * HS), lambda h, c: (0, 0, h))],
            out_specs=[
                pl.BlockSpec((PAIR * HS, rows), lambda h, c: (h, 0)),
                pl.BlockSpec((PAIR, MAIN, MAIN), lambda h, c: (h, 0, 0)),
                pl.BlockSpec((PAIR, 2 * SLOT, 2 * SLOT), lambda h, c: (h, 0, 0)),
            ],
        ),
        out_shape=[
            pltpu.HBM((width, rows), jnp.bfloat16),
            pltpu.HBM((heads, MAIN, MAIN), jnp.float32),
            pltpu.HBM((heads, 2 * SLOT, 2 * SLOT), jnp.float32),
        ],
        compiler_params=pltpu.CompilerParams(vmem_limit_bytes=12 * MIB),
        cost_estimate=lasting(60),
        name="attention_forward",
    )(counts, qkv)


def backward_kernel(qkv, grad_mine, grad_other, main_probs, slot_probs, *rest):
    grads = rest[-1]
    parts = []
    for head in range(PAIR):
        lanes = slice(head * HS, (head + 1) * HS)
        for first, rows, probs_ref in ((0, MAIN, main_probs), (MAIN, 2 * SLOT, slot_probs)):
            parts.append((head, slice(first, first + rows), lanes, probs_ref))
    grad, dprobs, dscores = [], [], []
    for head, at, lanes, _ in parts:
        both = grad_mine[lanes, at] + grad_other[lanes, at].astype(jnp.float32)
        grad.append(both.astype(jnp.bfloat16))
    for g, (head, at, lanes, _) in zip(grad, parts):
        dprobs.append(dot(qkv[2, at, lanes], g, 1, 0))
    for g, (head, at, lanes, probs_ref) in zip(grad, parts):
        grads[2, at, lanes] = dot(probs_ref[head].astype(jnp.bfloat16), g, 1, 1).astype(jnp.bfloat16)
    for dprob, (head, at, lanes, probs_ref) in zip(dprobs, parts):
        probs = probs_ref[head]
        delta = jnp.sum(probs * dprob, axis=0, keepdims=True)
        dscores.append((probs * (dprob - delta) * FACTOR).astype(jnp.bfloat16))
    for dscore, (head, at, lanes, _) in zip(dscores, parts):
        grads[1, at, lanes] = dot(dscore, qkv[0, at, lanes], 1, 0).astype(jnp.bfloat16)
        grads[0, at, lanes] = dot(dscore, qkv[1, at, lanes], 0, 0).astype(jnp.bfloat16)


def backward(qkv, grad_mine, grad_other, main_probs, slot_probs, low, high, grads):
    _, rows, width = qkv.shape
    held = [] if grads is None else [grads]
    return pl.pallas_call(
        backward_kernel,
        grid=(high - low,),
        in_specs=[
            pl.BlockSpec((3, rows, PAIR * HS), lambda h: (0, 0, h + low)),
            pl.BlockSpec((PAIR * HS, rows), lambda h: (h + low, 0)),
            pl.BlockSpec((PAIR * HS, rows), lambda h: (h + low, 0)),
            pl.BlockSpec((PAIR, MAIN, MAIN), lambda h: (h + low, 0, 0)),
            pl.BlockSpec((PAIR, 2 * SLOT, 2 * SLOT), lambda h: (h + low, 0, 0)),
        ] + [pl.BlockSpec(memory_space=pl.ANY)] * len(held),
        out_specs=pl.BlockSpec((3, rows, PAIR * HS), lambda h: (0, 0, h + low)),
        out_shape=pltpu.HBM(qkv.shape, jnp.bfloat16),
        input_output_aliases={5: 0} if held else {},
        compiler_params=pltpu.CompilerParams(vmem_limit_bytes=14 * MIB),
        cost_estimate=lasting(2 * (high - low)),
        name="attention_backward",
    )(qkv, grad_mine, grad_other, main_probs, slot_probs, *map(in_hbm, held))


def grad_out_kernel(sizes, split, total, info, turned, turned_other, *refs):
    mine, other, columns, tall, mine_rows, other_rows, in_sems, out_sems = refs[-8:]
    count, depth, rows = mine_rows.shape
    core = info[0]
    at = pl.ds(pl.multiple_of(core * (total - split), LANE), split)
    loads = [
        pltpu.make_async_copy(source.at[at], columns.at[i], in_sems.at[i]) for i, source in enumerate((turned, turned_other))
    ]
    index = 0
    for j, size in enumerate(sizes):
        first = 0
        for piece in refs[index:index + size]:
            target = tall.at[j] if size == 1 else tall.at[j, pl.ds(first, piece.shape[0])]
            loads.append(pltpu.make_async_copy(piece, target, in_sems.at[len(loads)]))
            first += piece.shape[0]
        index += size
    for load in loads:
        load.start()
    for load in loads:
        load.wait()

    @pl.when(core == 1)
    def _():
        shared = 2 * split - total
        columns[:, :shared, :] = jnp.zeros((2, shared, columns.shape[2]), jnp.bfloat16)

    stores = []
    for i, (result, out) in enumerate(((mine_rows, mine), (other_rows, other))):
        if depth % 16 == 0:
            product = dot(tall[...].reshape(count * depth, split), columns[i], 1, 0)[:, :rows]
            result[...] = product.astype(result.dtype).reshape(count, depth, rows)
        else:
            for j in range(count):
                result[j] = dot(tall[j], columns[i], 1, 0)[:, :rows].astype(result.dtype)
        for j in range(count):
            stores.append(pltpu.make_async_copy(result.at[j], out.at[info[1 + j]], out_sems.at[i, j]))
            stores[-1].start()
    for store in stores:
        store.wait()


def grad_out_rows(info, turned, turned_other, rows, pieces, shards, held, after=()):
    total, lanes = turned.shape
    split = pieces[0][0].shape[1]
    depth = sum(p.shape[0] for p in pieces[0])
    sizes = [len(p) for p in pieces]
    arrays = [a for p in pieces for a in p]
    count = len(pieces)
    held = [] if held is None else list(held)
    return pl.pallas_call(
        functools.partial(grad_out_kernel, sizes, split, total),
        grid_spec=pltpu.PrefetchScalarGridSpec(
            num_scalar_prefetch=1,
            grid=(1,),
            in_specs=[pl.BlockSpec(memory_space=pl.ANY)] * (2 + len(arrays) + len(held) + len(after)),
            out_specs=[pl.BlockSpec(memory_space=pl.ANY)] * 2,
            scratch_shapes=[
                pltpu.VMEM((2, split, lanes), jnp.bfloat16),
                pltpu.VMEM((count, depth, split), jnp.bfloat16),
                pltpu.VMEM((count, depth, rows), jnp.float32),
                pltpu.VMEM((count, depth, rows), jnp.bfloat16),
                pltpu.SemaphoreType.DMA((2 + len(arrays),)),
                pltpu.SemaphoreType.DMA((2, count)),
            ],
        ),
        out_shape=[
            pltpu.HBM((shards, depth, rows), jnp.float32),
            pltpu.HBM((shards, depth, rows), jnp.bfloat16),
        ],
        input_output_aliases={3 + len(arrays) + i: i for i in range(len(held))},
        compiler_params=pltpu.CompilerParams(vmem_limit_bytes=16 * MIB),
        cost_estimate=lasting(0.2 if held else 1.5 * len(pieces)),
        name="grad_out_rows",
    )(info, in_hbm(turned), turned_other, *arrays, *map(in_hbm, held), *after)


def half_kernel(starts, weight, out, sem):
    copy = pltpu.make_async_copy(weight.at[:, pl.ds(pl.multiple_of(starts[0], LANE), out.shape[1])], out, sem)
    copy.start()
    copy.wait()


def half_columns(start, weight, width):
    return pl.pallas_call(
        half_kernel,
        grid_spec=pltpu.PrefetchScalarGridSpec(
            num_scalar_prefetch=1,
            grid=(1,),
            in_specs=[pl.BlockSpec(memory_space=pl.ANY)],
            out_specs=pl.BlockSpec(memory_space=pl.ANY),
            scratch_shapes=[pltpu.SemaphoreType.DMA],
        ),
        out_shape=jax.ShapeDtypeStruct((weight.shape[0], width), weight.dtype),
        compiler_params=pltpu.CompilerParams(vmem_limit_bytes=2 * MIB),
        cost_estimate=lasting(1),
        name="own_half_of_weight",
    )(start, in_hbm(weight))


def finish_kernel(offsets, start, term, came_up, came_down, out):
    total = term[...] + came_up[...].astype(jnp.float32) + came_down[...].astype(jnp.float32)
    for offset in offsets:

        @pl.when(start[0] == offset)
        def _():
            out[...] = total[:, offset:offset + out.shape[1]]


def finish(start, term, came_up, came_down, owned, offsets):
    depth, window = term.shape
    block = pl.BlockSpec((depth, window), lambda i, s: (0, 0))
    return pl.pallas_call(
        functools.partial(finish_kernel, offsets),
        grid_spec=pltpu.PrefetchScalarGridSpec(
            num_scalar_prefetch=1,
            grid=(1,),
            in_specs=[block] * 3,
            out_specs=pl.BlockSpec((depth, owned), lambda i, s: (0, 0)),
        ),
        out_shape=jax.ShapeDtypeStruct((depth, owned), jnp.float32),
        compiler_params=pltpu.CompilerParams(vmem_limit_bytes=8 * MIB),
        cost_estimate=lasting(2),
        name="last_sum",
    )(start, term, came_up, came_down)


def partial_kernel(chosen, sources, parts, count, window, order, start, *refs):
    attended, columns = refs[:sources], refs[sources:sources * (1 + parts)]
    chunks, held, sems = refs[-3:]
    bases = refs[sources * (1 + parts):-3 - count]
    outs = refs[-3 - count:-3]
    depth, rows = chunks.shape[2:]
    at = pl.ds(pl.multiple_of(start[0], LANE), window)
    copies = []
    for i in range(sources):
        some, first = [], 0
        for part in range(parts):
            source = columns[i * parts + part]
            if chosen:
                some.append(pltpu.make_async_copy(source.at[at], held.at[i], sems.at[i, count + part]))
            else:
                target = held.at[i, pl.ds(first, source.shape[0])]
                some.append(pltpu.make_async_copy(source.at[:, at], target, sems.at[i, count + part]))
            first += source.shape[0]
        for j in range(count):
            source = attended[i].at[order[j] if chosen else j]
            some.append(pltpu.make_async_copy(source, chunks.at[i, j], sems.at[i, j]))
        copies.append(some)
    for some in copies:
        for copy in some:
            copy.start()
    most = 4 if depth % 16 == 0 else 1
    for first in range(0, count, most):
        some = min(most, count - first)
        total = None
        for i in range(sources):
            if first == 0:
                for copy in copies[i]:
                    copy.wait()
            tall = chunks[i, first:first + some].reshape(some * depth, rows) if some > 1 else chunks[i, first]
            part = dot(tall, held[i][:, :rows], 1, 1) if chosen else dot(tall, held[i], 1, 0)
            total = part if total is None else total + part
        for j in range(some):
            result = total[j * depth:(j + 1) * depth]
            if bases:
                result += bases[first + j][...].astype(jnp.float32)
            outs[first + j][...] = result.astype(outs[first + j].dtype)


def partial_products(order, start, attended, columns, window, bases=()):
    _, depth, rows = attended[0].shape
    parts = len(columns) // len(attended)
    count, sources = order.shape[0], len(attended)
    block = pl.BlockSpec((depth, window), lambda j, o, s: (0, 0))
    return pl.pallas_call(
        functools.partial(partial_kernel, not bases, sources, parts, count, window),
        grid_spec=pltpu.PrefetchScalarGridSpec(
            num_scalar_prefetch=2,
            grid=(1,),
            in_specs=[pl.BlockSpec(memory_space=pl.ANY)] * (sources * (1 + parts)) + [block] * len(bases),
            out_specs=[block] * count,
            scratch_shapes=[
                pltpu.VMEM((sources, count, depth, rows), jnp.bfloat16),
                pltpu.VMEM((sources, rows, window) if bases else (sources, window, columns[0].shape[1]), jnp.bfloat16),
                pltpu.SemaphoreType.DMA((sources, count + parts)),
            ],
        ),
        out_shape=[
            jax.ShapeDtypeStruct((depth, window), jnp.float32) if bases else pltpu.HBM((depth, window), jnp.bfloat16)
        ] * count,
        compiler_params=pltpu.CompilerParams(vmem_limit_bytes=(16 if bases else 18) * MIB),
        cost_estimate=lasting(3 if bases else 6),
        name="projection_peers" if bases else "projection_chip",
    )(order, start, *attended, *columns, *map(in_hbm, bases))


def windows_of(groups, owned, total):
    lows = [g * owned // LANE * LANE for g in range(groups)]
    width = max(-(-((g + 1) * owned) // LANE) * LANE - low for g, low in enumerate(lows))
    return width


def ring_of(count):
    return list(range(0, count, 2)) + list(range(count - 1, 0, -2))


def local(members, shards, query_key_value, cotangent, proj_weight, layer_scale, lengths):
    member = lax.axis_index("dp")
    shard = lax.axis_index("fsdp")
    core, chip, peers = member % 2, member // 2, members // 2
    ring = ring_of(shards)
    place = jnp.where(shard % 2 == 0, shard // 2, shards - 1 - shard // 2)
    ahead = [(ring[i], ring[(i + 1) % shards]) for i in range(shards)]
    behind = [(ring[i], ring[(i - 1) % shards]) for i in range(shards)]
    half = shards // 2
    depth, total = proj_weight.shape
    rows, width = query_key_value.shape[1:]
    owned = total // members
    counts = lax.dynamic_index_in_dim(lengths[:, 0, :], member, 0, keepdims=False)

    def swap(array, bit):
        return lax.ppermute(array, "dp", [(i, i ^ bit) for i in range(members)])

    def shard_at(offset):
        at = (place + offset + shards) % shards
        return jnp.where(at < half, 2 * at, 2 * (shards - 1 - at) + 1)

    def table(values):
        return jnp.stack([jnp.asarray(v) for v in values]).astype(jnp.int32)

    chip_width, window = windows_of(peers, 2 * owned, total), windows_of(members, owned, total)

    def chip_start(chip):
        return jnp.minimum(chip * 2 * owned // LANE * LANE, total - chip_width)

    my_start = jnp.minimum(member * owned // LANE * LANE, chip_start(chip) + chip_width - window)
    starts = table([my_start, my_start - chip_start(chip)])

    split = -(-(total // LANE) // 2) * LANE
    mine = half_columns(table([core * (total - split)]), proj_weight, split)
    cut = -(-depth // 32) * 16
    up, down = [mine], [mine]
    up.append(lax.ppermute(up[-1], "fsdp", ahead))
    down.append(lax.ppermute(down[-1], "fsdp", behind))

    mine, cotangent = lax.optimization_barrier((mine, cotangent))
    scales = layer_scale.reshape(1, total)
    sent = peer_windows(
        table([chip_start(chip ^ k) for k in range(1, peers)] or [0]), cotangent, scales, peers - 1, chip_width
    )
    sent, cotangent = lax.optimization_barrier((sent, cotangent))
    came_columns = [[swap(array, 2 * k) for k, array in enumerate(part, 1)] for part in sent]
    turned = prepare(cotangent, scales)
    attended, main_probs, slot_probs = forward(counts, query_key_value)
    attended = attended.reshape(shards, depth, rows)
    near = [[o, -o] for o in range(half - 1, 0, -1)]
    groups = [[half] + near[0]] + near[1:-1] + [near[-1] + [0]]
    flat = table([shard_at(o) for group in groups for o in group])
    sizes = [len(group) for group in groups]
    orders = [flat[sum(sizes[:g]):sum(sizes[:g + 1])] for g in range(len(groups))]

    def rows_of(some, held, after=()):
        info = table([core] + [shard_at(o) for _, o in some])
        return grad_out_rows(info, turned, turned_other, rows, [p for p, _ in some], shards, held, after)

    up[1], down[1], attended, came_columns[0], turned = lax.optimization_barrier(
        (up[1], down[1], attended, came_columns[0], turned)
    )
    turned_other = swap(turned, 1)
    other_columns = [[swap(array, 1) for array in came_columns[0]]]
    attended_other = swap(attended, 1)
    chunks = list(arrange(flat, attended, sizes))
    attended_other, chunks = lax.optimization_barrier((attended_other, chunks))
    for _ in range(half - 3):
        up.append(lax.ppermute(up[-1], "fsdp", ahead))
        down.append(lax.ppermute(down[-1], "fsdp", behind))
    bases = partial_products(
        flat, starts[:1], [in_hbm(attended), attended_other], [in_hbm(turned), turned_other], window
    )
    up[-1], down[-1], turned_other, attended_other, *bases = lax.optimization_barrier(
        (up[-1], down[-1], turned_other, attended_other, *bases)
    )
    bases = dict(zip([o for group in groups for o in group], bases))

    late, chunks = lax.optimization_barrier((came_columns[1], chunks))
    came = [[swap(chunks[0], 2 * k) for k in range(1, peers)]]
    other_columns.append([swap(array, 1) for array in late])
    came_columns[1] = late
    came.append([swap(chunks[1], 2 * k) for k in range(1, peers)])
    columns = []
    for k in range(peers - 1):
        for arrays in (came_columns, other_columns):
            columns += [in_hbm(part[k]) for part in arrays]
    pieces = [([mine], 0)]
    for step in range(1, half - 1):
        pieces += [([up[step]], -step), ([down[step]], step)]
    pieces[:-2] = [([in_hbm(array) for array in arrays], o) for arrays, o in pieces[:-2]]
    grad_out = rows_of(pieces, None)
    up.append(lax.ppermute(up[-1], "fsdp", ahead))
    down.append(lax.ppermute(down[-1], "fsdp", behind))
    up[-1], down[-1], grad_out = lax.optimization_barrier((up[-1], down[-1], grad_out))
    if depth % 16 == 0:
        far_up, far_down = far_parts(up[-1], down[-1], cut)
    else:
        far_up, far_down = up[-1][:cut], down[-1][cut:]
    came[0], near_up, near_down, sent_up = lax.optimization_barrier((came[0], up[-1], down[-1], far_up))
    far_up = lax.ppermute(far_up, "fsdp", ahead)
    far_down = lax.ppermute(far_down, "fsdp", behind)

    def both_cores(arrays):
        return [a for c in arrays for a in (c, swap(c, 1))]

    def products(index, taken):
        group = groups[index]
        if not taken:
            return {o: bases[o] for o in group}
        result = partial_products(orders[index], starts[1:], taken, columns, window, [bases[o] for o in group])
        return dict(zip(group, result))

    terms = products(0, both_cores(came[0]))
    first = terms[half].astype(jnp.bfloat16)
    going_up, going_down, came[1], chunks, far_up, far_down = lax.optimization_barrier(
        (first[:cut], first[cut:], came[1], chunks, far_up, far_down)
    )
    came += [[swap(some, 2 * k) for k in range(1, peers)] for some in chunks[2:]]
    taken = both_cores(came[1])
    came_up = lax.ppermute(going_up, "fsdp", ahead)
    came_down = lax.ppermute(going_down, "fsdp", behind)

    bounds = [0, 3, 5, -(-(width // HS) // PAIR)]
    grads = None
    for step in range(half, 1, -1):
        if step == half:
            came_up, came_down, following = lax.optimization_barrier((came_up, came_down, products(1, taken)))
            terms.update(following)
            came_up = jnp.pad(came_up, ((0, depth - cut), (0, 0)))
            came_down = jnp.pad(came_down, ((cut, 0), (0, 0)))
        going_up = (terms[step - 1] + came_up.astype(jnp.float32)).astype(jnp.bfloat16)
        going_down = (terms[1 - step] + came_down.astype(jnp.float32)).astype(jnp.bfloat16)
        if step == half:
            going_up, going_down, near_up = lax.optimization_barrier((going_up, going_down, near_up))
            grad_out = rows_of([([near_up], 1 - half), ([near_down], half - 1), ([far_up, far_down], half)], grad_out, [sent_up])
            grad_mine = grad_out[0].reshape(width, rows)
            came[2], grad_other = lax.optimization_barrier((came[2], grad_out[1]))
            grad_other = swap(grad_other, 1).reshape(width, rows)
        elif step > 2:
            arrived = came[half - step + 1]
            going_up, going_down, arrived, grad_mine = lax.optimization_barrier((going_up, going_down, arrived, grad_mine))
            terms.update(products(half - step + 1, [in_hbm(array) for array in both_cores(arrived)]))
        else:
            going_up, going_down = lax.optimization_barrier((going_up, going_down))
        came_up = lax.ppermute(going_up, "fsdp", ahead)
        came_down = lax.ppermute(going_down, "fsdp", behind)
    for low, high in zip(bounds, bounds[1:]):
        grads = backward(query_key_value, grad_mine, grad_other, main_probs, slot_probs, low, high, grads)
    came_up, came_down, grads = lax.optimization_barrier((came_up, came_down, grads))
    offsets = set()
    for m in range(members):
        low = min((m // 2) * 2 * owned // LANE * LANE, total - chip_width)
        offsets.add(m * owned - min(m * owned // LANE * LANE, low + chip_width - window))
    grad_proj = finish(table([member * owned - my_start]), terms[0], came_up, came_down, owned, sorted(offsets))
    return grads, grad_proj


def solution(mesh):
    members, shards = mesh.shape["dp"], mesh.shape["fsdp"]
    placed = (
        P(None, ("dp", "fsdp"), None),
        P(("dp", "fsdp"), None),
        P("fsdp", None),
        P(),
        P(None, "fsdp", None),
    )
    return jax.shard_map(
        functools.partial(local, members, shards),
        mesh=mesh,
        in_specs=placed,
        out_specs=(P(None, ("dp", "fsdp"), None), P("fsdp", "dp")),
        check_vma=False,
    )
```

```python
import functools

import jax
import jax.numpy as jnp
from jax import lax
from jax.experimental import pallas as pl
from jax.experimental.pallas import tpu as pltpu
from jax.sharding import PartitionSpec as P

HS = 128
MAIN = 256
SLOT = 96
LANE = 128
FACTOR = HS ** (-0.5)
MIB = 1024 * 1024


def lasting(microseconds):
    return pl.CostEstimate(flops=int(microseconds * 575000000), bytes_accessed=1000, transcendentals=0)


def dot(left, right, left_dim, right_dim):
    return lax.dot_general(left, right, (((left_dim,), (right_dim,)), ((), ())), preferred_element_type=jnp.float32)


def in_hbm(array):
    return pltpu.with_memory_space_constraint(array, pltpu.HBM)


def window_kernel(peers, starts, cotangent, layer_scale, *refs):
    windows, (held, sems) = refs[:-2], refs[-2:]
    parts = len(windows) // peers
    width = held.shape[2]
    copies = []
    for k in range(peers):
        at = pl.ds(pl.multiple_of(starts[k], LANE), width)
        first = 0
        for part in range(parts):
            rows = pl.ds(first, windows[part].shape[0])
            copies.append(pltpu.make_async_copy(cotangent.at[rows, at], held.at[k, rows], sems.at[k, part]))
            first += windows[part].shape[0]
    for copy in copies:
        copy.start()
    for k in range(peers):
        scale = layer_scale[:, pl.ds(pl.multiple_of(starts[k], LANE), width)]
        first = 0
        for part in range(parts):
            copies[k * parts + part].wait()
            window = windows[k * parts + part]
            values = held[k, first:first + window.shape[0], :].astype(jnp.float32)
            window[...] = (values * scale).astype(jnp.bfloat16)
            first += window.shape[0]


def peer_windows(starts, cotangent, layer_scale, peers, width):
    rows, total = cotangent.shape
    first = rows * 2 // 5 // 16 * 16
    parts = (first, rows - first)
    arrays = pl.pallas_call(
        functools.partial(window_kernel, peers),
        grid_spec=pltpu.PrefetchScalarGridSpec(
            num_scalar_prefetch=1,
            grid=(1,),
            in_specs=[pl.BlockSpec(memory_space=pl.ANY), pl.BlockSpec((1, total), lambda i, s: (0, 0))],
            out_specs=[pl.BlockSpec((part, width), lambda i, s: (0, 0)) for part in parts] * peers,
            scratch_shapes=[
                pltpu.VMEM((peers, rows, width), jnp.bfloat16),
                pltpu.SemaphoreType.DMA((peers, len(parts))),
            ],
        ),
        out_shape=[pltpu.HBM((part, width), jnp.bfloat16) for part in parts] * peers,
        compiler_params=pltpu.CompilerParams(vmem_limit_bytes=8 * MIB),
        cost_estimate=lasting(60),
        name="peer_windows",
    )(starts, in_hbm(cotangent), layer_scale)
    return [arrays[part::len(parts)] for part in range(len(parts))]


def prepare_kernel(cotangent, layer_scale, turned):
    values = (cotangent[...].astype(jnp.float32) * layer_scale[...]).astype(jnp.bfloat16)
    spare = jnp.zeros((turned.shape[1] - values.shape[0], values.shape[1]), jnp.bfloat16)
    turned[...] = jnp.concatenate([values, spare], axis=0).T


def prepare(cotangent, layer_scale):
    rows, total = cotangent.shape
    lanes = -(-rows // LANE) * LANE
    steps = 5
    block = total // steps
    return pl.pallas_call(
        prepare_kernel,
        grid=(steps,),
        in_specs=[pl.BlockSpec((rows, block), lambda i: (0, i)), pl.BlockSpec((1, block), lambda i: (0, i))],
        out_specs=pl.BlockSpec((block, lanes), lambda i: (i, 0)),
        out_shape=pltpu.HBM((total, lanes), jnp.bfloat16),
        compiler_params=pltpu.CompilerParams(vmem_limit_bytes=8 * MIB),
        cost_estimate=lasting(60),
        name="scaled_cotangent",
    )(in_hbm(cotangent), layer_scale)


def arrange_kernel(sizes, order, attended, *refs):
    *outs, sems = refs
    copies = []
    for out, size in zip(outs, sizes):
        for j in range(size):
            n = len(copies)
            copies.append(pltpu.make_async_copy(attended.at[order[n]], out.at[j], sems.at[n]))
    for copy in copies:
        copy.start()
    for copy in copies:
        copy.wait()


def arrange(order, attended, sizes):
    _, depth, rows = attended.shape
    return pl.pallas_call(
        functools.partial(arrange_kernel, sizes),
        grid_spec=pltpu.PrefetchScalarGridSpec(
            num_scalar_prefetch=1,
            grid=(1,),
            in_specs=[pl.BlockSpec(memory_space=pl.ANY)],
            out_specs=[pl.BlockSpec((size, depth, rows), lambda i, o: (0, 0, 0)) for size in sizes],
            scratch_shapes=[pltpu.SemaphoreType.DMA((sum(sizes),))],
        ),
        out_shape=[jax.ShapeDtypeStruct((size, depth, rows), attended.dtype) for size in sizes],
        compiler_params=pltpu.CompilerParams(vmem_limit_bytes=6 * MIB),
        cost_estimate=lasting(2),
        name="attended_chunks",
    )(order, in_hbm(attended))


PAIR = 2
EXPONENT = FACTOR * 1.4426950408889634


def forward_kernel(counts, qkv, attended, main_probs, slot_probs):
    def marks(image, ids):
        lane = lax.broadcasted_iota(jnp.int32, (image.shape[0], HS), 1)
        first = jnp.where(image == ids[0], 1.0, 0.0)
        second = jnp.where(image == ids[1], 1.0, 0.0)
        own = jnp.where(lane == 0, first, jnp.where(lane == 1, second, 0.0))
        other = jnp.where(lane == 0, 1.0 - first, jnp.where(lane == 1, 1.0 - second, 0.0)) * -1e30
        return own.astype(jnp.bfloat16), other.astype(jnp.bfloat16)

    main_at = lax.broadcasted_iota(jnp.int32, (MAIN, HS), 0)
    main_marks = marks(jnp.where(main_at >= counts[0], 1, 0), (0, 1))

    def image(at):
        first = jnp.where(at < counts[2], 2, -1)
        return jnp.where(at < SLOT, first, jnp.where(at - SLOT < counts[3], 3, -1))

    slot_marks = marks(image(lax.broadcasted_iota(jnp.int32, (2 * SLOT, HS), 0)), (2, 3))
    valid = image(lax.broadcasted_iota(jnp.int32, (1, 2 * SLOT), 1)) >= 0
    parts = []
    for head in range(PAIR):
        lanes = slice(head * HS, (head + 1) * HS)
        parts.append((head, 0, MAIN, lanes, main_marks, None, main_probs))
        parts.append((head, MAIN, 2 * SLOT, lanes, slot_marks, valid, slot_probs))
    scores = []
    for head, first, rows, lanes, (mark_query, mark_key), _, _ in parts:
        query = jnp.concatenate([qkv[0, first:first + rows, lanes], mark_query], axis=1)
        key = jnp.concatenate([qkv[1, first:first + rows, lanes], mark_key], axis=1)
        scores.append(dot(key, query, 1, 1))
    probs = []
    for score, (_, _, _, _, _, good, _) in zip(scores, parts):
        weights = jnp.exp2((score - jnp.max(score, axis=0, keepdims=True)) * EXPONENT)
        scale = 1.0 / jnp.sum(weights, axis=0, keepdims=True)
        probs.append(weights * (scale if good is None else jnp.where(good, scale, 0.0)))
    for prob, (head, first, rows, lanes, _, _, probs_ref) in zip(probs, parts):
        probs_ref[head] = prob
        result = dot(qkv[2, first:first + rows, lanes], prob.astype(jnp.bfloat16), 0, 0)
        attended[lanes, first:first + rows] = result.astype(jnp.bfloat16)


def forward(counts, qkv):
    _, rows, width = qkv.shape
    heads = width // HS
    return pl.pallas_call(
        forward_kernel,
        grid_spec=pltpu.PrefetchScalarGridSpec(
            num_scalar_prefetch=1,
            grid=(-(-heads // PAIR),),
            in_specs=[pl.BlockSpec((3, rows, PAIR * HS), lambda h, c: (0, 0, h))],
            out_specs=[
                pl.BlockSpec((PAIR * HS, rows), lambda h, c: (h, 0)),
                pl.BlockSpec((PAIR, MAIN, MAIN), lambda h, c: (h, 0, 0)),
                pl.BlockSpec((PAIR, 2 * SLOT, 2 * SLOT), lambda h, c: (h, 0, 0)),
            ],
        ),
        out_shape=[
            pltpu.HBM((width, rows), jnp.bfloat16),
            pltpu.HBM((heads, MAIN, MAIN), jnp.float32),
            pltpu.HBM((heads, 2 * SLOT, 2 * SLOT), jnp.float32),
        ],
        compiler_params=pltpu.CompilerParams(vmem_limit_bytes=12 * MIB),
        cost_estimate=lasting(60),
        name="attention_forward",
    )(counts, qkv)


def backward_kernel(qkv, grad_mine, grad_other, main_probs, slot_probs, *rest):
    grads = rest[-1]
    parts = []
    for head in range(PAIR):
        lanes = slice(head * HS, (head + 1) * HS)
        for first, rows, probs_ref in ((0, MAIN, main_probs), (MAIN, 2 * SLOT, slot_probs)):
            parts.append((head, slice(first, first + rows), lanes, probs_ref))
    grad, dprobs, dscores = [], [], []
    for head, at, lanes, _ in parts:
        both = grad_mine[lanes, at] + grad_other[lanes, at].astype(jnp.float32)
        grad.append(both.astype(jnp.bfloat16))
    for g, (head, at, lanes, _) in zip(grad, parts):
        dprobs.append(dot(qkv[2, at, lanes], g, 1, 0))
    for g, (head, at, lanes, probs_ref) in zip(grad, parts):
        grads[2, at, lanes] = dot(probs_ref[head].astype(jnp.bfloat16), g, 1, 1).astype(jnp.bfloat16)
    for dprob, (head, at, lanes, probs_ref) in zip(dprobs, parts):
        probs = probs_ref[head]
        delta = jnp.sum(probs * dprob, axis=0, keepdims=True)
        dscores.append((probs * (dprob - delta) * FACTOR).astype(jnp.bfloat16))
    for dscore, (head, at, lanes, _) in zip(dscores, parts):
        grads[1, at, lanes] = dot(dscore, qkv[0, at, lanes], 1, 0).astype(jnp.bfloat16)
        grads[0, at, lanes] = dot(dscore, qkv[1, at, lanes], 0, 0).astype(jnp.bfloat16)


def backward(qkv, grad_mine, grad_other, main_probs, slot_probs, low, high, grads):
    _, rows, width = qkv.shape
    held = [] if grads is None else [grads]
    return pl.pallas_call(
        backward_kernel,
        grid=(high - low,),
        in_specs=[
            pl.BlockSpec((3, rows, PAIR * HS), lambda h: (0, 0, h + low)),
            pl.BlockSpec((PAIR * HS, rows), lambda h: (h + low, 0)),
            pl.BlockSpec((PAIR * HS, rows), lambda h: (h + low, 0)),
            pl.BlockSpec((PAIR, MAIN, MAIN), lambda h: (h + low, 0, 0)),
            pl.BlockSpec((PAIR, 2 * SLOT, 2 * SLOT), lambda h: (h + low, 0, 0)),
        ] + [pl.BlockSpec(memory_space=pl.ANY)] * len(held),
        out_specs=pl.BlockSpec((3, rows, PAIR * HS), lambda h: (0, 0, h + low)),
        out_shape=pltpu.HBM(qkv.shape, jnp.bfloat16),
        input_output_aliases={5: 0} if held else {},
        compiler_params=pltpu.CompilerParams(vmem_limit_bytes=14 * MIB),
        cost_estimate=lasting(2 * (high - low)),
        name="attention_backward",
    )(qkv if held else in_hbm(qkv), grad_mine, grad_other, main_probs, slot_probs, *map(in_hbm, held))


def grad_out_kernel(sizes, split, total, info, turned, turned_other, *refs):
    mine, other, columns, tall, mine_rows, other_rows, in_sems, out_sems = refs[-8:]
    count, depth, rows = mine_rows.shape
    core = info[0]
    at = pl.ds(pl.multiple_of(core * (total - split), LANE), split)
    loads = [
        pltpu.make_async_copy(source.at[at], columns.at[i], in_sems.at[i]) for i, source in enumerate((turned, turned_other))
    ]
    index = 0
    for j, size in enumerate(sizes):
        first = 0
        for piece in refs[index:index + size]:
            target = tall.at[j] if size == 1 else tall.at[j, pl.ds(first, piece.shape[0])]
            loads.append(pltpu.make_async_copy(piece, target, in_sems.at[len(loads)]))
            first += piece.shape[0]
        index += size
    for load in loads:
        load.start()
    for load in loads:
        load.wait()

    @pl.when(core == 1)
    def _():
        shared = 2 * split - total
        columns[:, :shared, :] = jnp.zeros((2, shared, columns.shape[2]), jnp.bfloat16)

    stores = []
    for i, (result, out) in enumerate(((mine_rows, mine), (other_rows, other))):
        if depth % 16 == 0:
            product = dot(tall[...].reshape(count * depth, split), columns[i], 1, 0)[:, :rows]
            result[...] = product.astype(result.dtype).reshape(count, depth, rows)
        else:
            for j in range(count):
                result[j] = dot(tall[j], columns[i], 1, 0)[:, :rows].astype(result.dtype)
        for j in range(count):
            stores.append(pltpu.make_async_copy(result.at[j], out.at[info[1 + j]], out_sems.at[i, j]))
            stores[-1].start()
    for store in stores:
        store.wait()


def grad_out_rows(info, turned, turned_other, rows, pieces, shards, held):
    total, lanes = turned.shape
    split = pieces[0][0].shape[1]
    depth = sum(p.shape[0] for p in pieces[0])
    sizes = [len(p) for p in pieces]
    arrays = [a for p in pieces for a in p]
    count = len(pieces)
    held = [] if held is None else list(held)
    return pl.pallas_call(
        functools.partial(grad_out_kernel, sizes, split, total),
        grid_spec=pltpu.PrefetchScalarGridSpec(
            num_scalar_prefetch=1,
            grid=(1,),
            in_specs=[pl.BlockSpec(memory_space=pl.ANY)] * (2 + len(arrays) + len(held)),
            out_specs=[pl.BlockSpec(memory_space=pl.ANY)] * 2,
            scratch_shapes=[
                pltpu.VMEM((2, split, lanes), jnp.bfloat16),
                pltpu.VMEM((count, depth, split), jnp.bfloat16),
                pltpu.VMEM((count, depth, rows), jnp.float32),
                pltpu.VMEM((count, depth, rows), jnp.bfloat16),
                pltpu.SemaphoreType.DMA((2 + len(arrays),)),
                pltpu.SemaphoreType.DMA((2, count)),
            ],
        ),
        out_shape=[
            pltpu.HBM((shards, depth, rows), jnp.float32),
            pltpu.HBM((shards, depth, rows), jnp.bfloat16),
        ],
        input_output_aliases={3 + len(arrays) + i: i for i in range(len(held))},
        compiler_params=pltpu.CompilerParams(vmem_limit_bytes=16 * MIB),
        cost_estimate=lasting(0.2 if held else 1.5 * len(pieces)),
        name="grad_out_rows",
    )(info, in_hbm(turned), turned_other, *arrays, *map(in_hbm, held))


def half_kernel(starts, weight, out, sem):
    copy = pltpu.make_async_copy(weight.at[:, pl.ds(pl.multiple_of(starts[0], LANE), out.shape[1])], out, sem)
    copy.start()
    copy.wait()


def half_columns(start, weight, width):
    return pl.pallas_call(
        half_kernel,
        grid_spec=pltpu.PrefetchScalarGridSpec(
            num_scalar_prefetch=1,
            grid=(1,),
            in_specs=[pl.BlockSpec(memory_space=pl.ANY)],
            out_specs=pl.BlockSpec(memory_space=pl.ANY),
            scratch_shapes=[pltpu.SemaphoreType.DMA],
        ),
        out_shape=jax.ShapeDtypeStruct((weight.shape[0], width), weight.dtype),
        compiler_params=pltpu.CompilerParams(vmem_limit_bytes=2 * MIB),
        cost_estimate=lasting(1),
        name="own_half_of_weight",
    )(start, in_hbm(weight))


def finish_kernel(offsets, start, term, came_up, came_down, out):
    total = term[...] + came_up[...].astype(jnp.float32) + came_down[...].astype(jnp.float32)
    for offset in offsets:

        @pl.when(start[0] == offset)
        def _():
            out[...] = total[:, offset:offset + out.shape[1]]


def finish(start, term, came_up, came_down, owned, offsets):
    depth, window = term.shape
    block = pl.BlockSpec((depth, window), lambda i, s: (0, 0))
    return pl.pallas_call(
        functools.partial(finish_kernel, offsets),
        grid_spec=pltpu.PrefetchScalarGridSpec(
            num_scalar_prefetch=1,
            grid=(1,),
            in_specs=[block] * 3,
            out_specs=pl.BlockSpec((depth, owned), lambda i, s: (0, 0)),
        ),
        out_shape=jax.ShapeDtypeStruct((depth, owned), jnp.float32),
        compiler_params=pltpu.CompilerParams(vmem_limit_bytes=8 * MIB),
        cost_estimate=lasting(2),
        name="last_sum",
    )(start, term, came_up, came_down)


def partial_kernel(chosen, turned_round, sources, parts, count, window, order, start, *refs):
    attended, columns = refs[:sources], refs[sources:sources * (1 + parts)]
    chunks, held, sems = refs[-3:]
    bases = refs[sources * (1 + parts):-3 - count]
    outs = refs[-3 - count:-3]
    depth, rows = chunks.shape[2:]
    at = pl.ds(pl.multiple_of(start[0], LANE), window)
    copies = []
    for i in range(sources):
        some, first = [], 0
        for part in range(parts):
            source = columns[i * parts + part]
            if chosen:
                some.append(pltpu.make_async_copy(source.at[at], held.at[i], sems.at[i, count + part]))
            else:
                target = held.at[i, pl.ds(first, source.shape[0])]
                some.append(pltpu.make_async_copy(source.at[:, at], target, sems.at[i, count + part]))
            first += source.shape[0]
        for j in range(count):
            source = attended[i].at[order[j] if chosen else turned_round[j] if i % 2 else j]
            some.append(pltpu.make_async_copy(source, chunks.at[i, j], sems.at[i, j]))
        copies.append(some)
    for some in copies:
        for copy in some:
            copy.start()
    most = 4 if depth % 16 == 0 else 1
    for first in range(0, count, most):
        some = min(most, count - first)
        total = None
        for i in range(sources):
            if first == 0:
                for copy in copies[i]:
                    copy.wait()
            tall = chunks[i, first:first + some].reshape(some * depth, rows) if some > 1 else chunks[i, first]
            part = dot(tall, held[i][:, :rows], 1, 1) if chosen else dot(tall, held[i], 1, 0)
            total = part if total is None else total + part
        for j in range(some):
            result = total[j * depth:(j + 1) * depth]
            if bases:
                result += bases[first + j][...].astype(jnp.float32)
            outs[first + j][...] = result.astype(outs[first + j].dtype)


def partial_products(order, start, attended, columns, window, bases=(), turned_round=()):
    _, depth, rows = attended[0].shape
    parts = len(columns) // len(attended)
    count, sources = order.shape[0], len(attended)
    block = pl.BlockSpec((depth, window), lambda j, o, s: (0, 0))
    return pl.pallas_call(
        functools.partial(partial_kernel, not bases, turned_round, sources, parts, count, window),
        grid_spec=pltpu.PrefetchScalarGridSpec(
            num_scalar_prefetch=2,
            grid=(1,),
            in_specs=[pl.BlockSpec(memory_space=pl.ANY)] * (sources * (1 + parts)) + [block] * len(bases),
            out_specs=[block] * count,
            scratch_shapes=[
                pltpu.VMEM((sources, count, depth, rows), jnp.bfloat16),
                pltpu.VMEM((sources, rows, window) if bases else (sources, window, columns[0].shape[1]), jnp.bfloat16),
                pltpu.SemaphoreType.DMA((sources, count + parts)),
            ],
        ),
        out_shape=[
            jax.ShapeDtypeStruct((depth, window), jnp.float32) if bases else pltpu.HBM((depth, window), jnp.bfloat16)
        ] * count,
        compiler_params=pltpu.CompilerParams(vmem_limit_bytes=(16 if bases else 18) * MIB),
        cost_estimate=lasting(3 if bases else 6),
        name="projection_peers" if bases else "projection_chip",
    )(order, start, *attended, *columns, *map(in_hbm, bases))


def windows_of(groups, owned, total):
    lows = [g * owned // LANE * LANE for g in range(groups)]
    width = max(-(-((g + 1) * owned) // LANE) * LANE - low for g, low in enumerate(lows))
    return width


def ring_of(count):
    return list(range(0, count, 2)) + list(range(count - 1, 0, -2))


def local(members, shards, query_key_value, cotangent, proj_weight, layer_scale, lengths):
    member = lax.axis_index("dp")
    shard = lax.axis_index("fsdp")
    core, chip, peers = member % 2, member // 2, members // 2
    ring = ring_of(shards)
    place = jnp.where(shard % 2 == 0, shard // 2, shards - 1 - shard // 2)
    ahead = [(ring[i], ring[(i + 1) % shards]) for i in range(shards)]
    behind = [(ring[i], ring[(i - 1) % shards]) for i in range(shards)]
    ways = [ahead, behind]
    streams = [
        [(d * shards + a, d * shards + b) for d in range(members) for a, b in ways[(d + turn) % 2]] for turn in range(2)
    ]
    half = shards // 2
    depth, total = proj_weight.shape
    rows, width = query_key_value.shape[1:]
    owned = total // members
    counts = lax.dynamic_index_in_dim(lengths[:, 0, :], member, 0, keepdims=False)

    def send(array, stream):
        return lax.ppermute(array, ("dp", "fsdp"), streams[stream])

    def swap(array, bit):
        return lax.ppermute(array, "dp", [(i, i ^ bit) for i in range(members)])

    def shard_at(offset):
        at = (place + (1 - 2 * core) * offset + shards) % shards
        return jnp.where(at < half, 2 * at, 2 * (shards - 1 - at) + 1)

    def table(values):
        return jnp.stack([jnp.asarray(v) for v in values]).astype(jnp.int32)

    chip_width, window = windows_of(peers, 2 * owned, total), windows_of(members, owned, total)

    def chip_start(chip):
        return jnp.minimum(chip * 2 * owned // LANE * LANE, total - chip_width)

    my_start = jnp.minimum(member * owned // LANE * LANE, chip_start(chip) + chip_width - window)
    starts = table([my_start, my_start - chip_start(chip)])

    split = -(-(total // LANE) // 2) * LANE
    mine = half_columns(table([core * (total - split)]), proj_weight, split)
    up, down = [mine], [mine]
    up.append(send(up[-1], 0))
    down.append(send(down[-1], 1))

    mine, cotangent = lax.optimization_barrier((mine, cotangent))
    scales = layer_scale.reshape(1, total)
    sent = peer_windows(
        table([chip_start(chip ^ k) for k in range(1, peers)] or [0]), cotangent, scales, peers - 1, chip_width
    )
    sent, cotangent = lax.optimization_barrier((sent, cotangent))
    came_columns = [[swap(array, 2 * k) for k, array in enumerate(part, 1)] for part in sent]
    turned = prepare(cotangent, scales)
    attended, main_probs, slot_probs = forward(counts, query_key_value)
    attended = attended.reshape(shards, depth, rows)
    near = [[o, -o] for o in range(half - 1, 0, -1)]
    groups = [[half] + near[0]] + near[1:-1] + [near[-1] + [0]]
    flat = table([shard_at(o) for group in groups for o in group])
    sizes = [len(group) for group in groups]
    orders = [flat[sum(sizes[:g]):sum(sizes[:g + 1])] for g in range(len(groups))]

    def rows_of(some, held):
        info = table([core] + [shard_at(o) for _, o in some])
        return grad_out_rows(info, turned, turned_other, rows, [p for p, _ in some], shards, held)

    up[1], down[1], attended, came_columns[0], turned = lax.optimization_barrier(
        (up[1], down[1], attended, came_columns[0], turned)
    )
    turned_other = swap(turned, 1)
    other_columns = [[swap(array, 1) for array in came_columns[0]]]
    attended_other = swap(attended, 1)
    chunks = list(arrange(flat, attended, sizes))
    attended_other, chunks = lax.optimization_barrier((attended_other, chunks))
    for _ in range(half - 3):
        up.append(send(up[-1], 0))
        down.append(send(down[-1], 1))
    bases = partial_products(
        flat, starts[:1], [in_hbm(attended), attended_other], [in_hbm(turned), turned_other], window
    )
    up[-1], down[-1], turned_other, attended_other, *bases = lax.optimization_barrier(
        (up[-1], down[-1], turned_other, attended_other, *bases)
    )
    bases = dict(zip([o for group in groups for o in group], bases))

    late, chunks = lax.optimization_barrier((came_columns[1], chunks))
    came = [[swap(chunks[0], 2 * k) for k in range(1, peers)]]
    other_columns.append([swap(array, 1) for array in late])
    came_columns[1] = late
    came.append([swap(chunks[1], 2 * k) for k in range(1, peers)])
    columns = []
    for k in range(peers - 1):
        for arrays in (came_columns, other_columns):
            columns += [in_hbm(part[k]) for part in arrays]
    pieces = [([mine], 0)]
    for step in range(1, half - 1):
        pieces += [([up[step]], -step), ([down[step]], step)]
    pieces[:-2] = [([in_hbm(array) for array in arrays], o) for arrays, o in pieces[:-2]]
    grad_out = rows_of(pieces, None)
    up.append(send(up[-1], 0))
    down.append(send(down[-1], 1))
    up[-1], down[-1], grad_out = lax.optimization_barrier((up[-1], down[-1], grad_out))
    far = send(up[-1], 0)
    came[0], near_up, near_down = lax.optimization_barrier((came[0], up[-1], down[-1]))

    def both_cores(arrays):
        return [a for c in arrays for a in (c, swap(c, 1))]

    def products(index, taken):
        group = groups[index]
        if not taken:
            return {o: bases[o] for o in group}
        turned_round = [group.index(-o) if -o in group else j for j, o in enumerate(group)]
        result = partial_products(orders[index], starts[1:], taken, columns, window, [bases[o] for o in group], turned_round)
        return dict(zip(group, result))

    terms = products(0, both_cores(came[0]))
    first = terms[half].astype(jnp.bfloat16)
    first, came[1], chunks, far = lax.optimization_barrier((first, came[1], chunks, far))
    came += [[swap(some, 2 * k) for k in range(1, peers)] for some in chunks[2:]]
    taken = both_cores(came[1])
    came_up, came_down = send(first, 0), None

    bounds = [0, 3, 5, -(-(width // HS) // PAIR)]
    grads = None
    for step in range(half, 1, -1):
        if step == half:
            came_up, following = lax.optimization_barrier((came_up, products(1, taken)))
            terms.update(following)
        going_up = (terms[step - 1] + came_up.astype(jnp.float32)).astype(jnp.bfloat16)
        going_down = terms[1 - step] if came_down is None else terms[1 - step] + came_down.astype(jnp.float32)
        going_down = going_down.astype(jnp.bfloat16)
        if step == half:
            going_up, going_down, near_up = lax.optimization_barrier((going_up, going_down, near_up))
            grad_out = rows_of([([near_up], 1 - half), ([near_down], half - 1), ([far], half)], grad_out)
            grad_mine = grad_out[0].reshape(width, rows)
            came[2], grad_other = lax.optimization_barrier((came[2], grad_out[1]))
            grad_other = swap(grad_other, 1).reshape(width, rows)
        elif step > 2:
            arrived = came[half - step + 1]
            going_up, going_down, arrived, grad_mine = lax.optimization_barrier((going_up, going_down, arrived, grad_mine))
            terms.update(products(half - step + 1, [in_hbm(array) for array in both_cores(arrived)]))
        else:
            going_up, going_down = lax.optimization_barrier((going_up, going_down))
        came_up, came_down = send(going_up, 0), send(going_down, 1)
    for low, high in zip(bounds, bounds[1:]):
        grads = backward(query_key_value, grad_mine, grad_other, main_probs, slot_probs, low, high, grads)
    came_up, came_down, grads = lax.optimization_barrier((came_up, came_down, grads))
    offsets = set()
    for m in range(members):
        low = min((m // 2) * 2 * owned // LANE * LANE, total - chip_width)
        offsets.add(m * owned - min(m * owned // LANE * LANE, low + chip_width - window))
    grad_proj = finish(table([member * owned - my_start]), terms[0], came_up, came_down, owned, sorted(offsets))
    return grads, grad_proj


def solution(mesh):
    members, shards = mesh.shape["dp"], mesh.shape["fsdp"]
    placed = (
        P(None, ("dp", "fsdp"), None),
        P(("dp", "fsdp"), None),
        P("fsdp", None),
        P(),
        P(None, "fsdp", None),
    )
    return jax.shard_map(
        functools.partial(local, members, shards),
        mesh=mesh,
        in_specs=placed,
        out_specs=(P(None, ("dp", "fsdp"), None), P("fsdp", "dp")),
        check_vma=False,
    )
```

```python
import functools

import jax
import jax.numpy as jnp
from jax import lax
from jax.experimental import pallas as pl
from jax.experimental.pallas import tpu as pltpu
from jax.sharding import PartitionSpec as P

HS = 128
MAIN = 256
SLOT = 96
LANE = 128
FACTOR = HS ** (-0.5)
MIB = 1024 * 1024


def lasting(microseconds):
    return pl.CostEstimate(flops=int(microseconds * 575000000), bytes_accessed=1000, transcendentals=0)


def dot(left, right, left_dim, right_dim):
    return lax.dot_general(left, right, (((left_dim,), (right_dim,)), ((), ())), preferred_element_type=jnp.float32)


def in_hbm(array):
    return pltpu.with_memory_space_constraint(array, pltpu.HBM)


def window_kernel(peers, starts, cotangent, layer_scale, *refs):
    windows, (held, sems) = refs[:-2], refs[-2:]
    parts = len(windows) // peers
    width = held.shape[2]
    copies = []
    for k in range(peers):
        at = pl.ds(pl.multiple_of(starts[k], LANE), width)
        first = 0
        for part in range(parts):
            rows = pl.ds(first, windows[part].shape[0])
            copies.append(pltpu.make_async_copy(cotangent.at[rows, at], held.at[k, rows], sems.at[k, part]))
            first += windows[part].shape[0]
    for copy in copies:
        copy.start()
    for k in range(peers):
        scale = layer_scale[:, pl.ds(pl.multiple_of(starts[k], LANE), width)]
        first = 0
        for part in range(parts):
            copies[k * parts + part].wait()
            window = windows[k * parts + part]
            values = held[k, first:first + window.shape[0], :].astype(jnp.float32)
            window[...] = (values * scale).astype(jnp.bfloat16)
            first += window.shape[0]


def peer_windows(starts, cotangent, layer_scale, peers, width):
    rows, total = cotangent.shape
    first = rows * 2 // 5 // 16 * 16
    parts = (first, rows - first)
    arrays = pl.pallas_call(
        functools.partial(window_kernel, peers),
        grid_spec=pltpu.PrefetchScalarGridSpec(
            num_scalar_prefetch=1,
            grid=(1,),
            in_specs=[pl.BlockSpec(memory_space=pl.ANY), pl.BlockSpec((1, total), lambda i, s: (0, 0))],
            out_specs=[pl.BlockSpec((part, width), lambda i, s: (0, 0)) for part in parts] * peers,
            scratch_shapes=[
                pltpu.VMEM((peers, rows, width), jnp.bfloat16),
                pltpu.SemaphoreType.DMA((peers, len(parts))),
            ],
        ),
        out_shape=[pltpu.HBM((part, width), jnp.bfloat16) for part in parts] * peers,
        compiler_params=pltpu.CompilerParams(vmem_limit_bytes=8 * MIB),
        cost_estimate=lasting(60),
        name="peer_windows",
    )(starts, in_hbm(cotangent), layer_scale)
    return [arrays[part::len(parts)] for part in range(len(parts))]


def prepare_kernel(cotangent, layer_scale, turned):
    values = (cotangent[...].astype(jnp.float32) * layer_scale[...]).astype(jnp.bfloat16)
    spare = jnp.zeros((turned.shape[1] - values.shape[0], values.shape[1]), jnp.bfloat16)
    turned[...] = jnp.concatenate([values, spare], axis=0).T


def prepare(cotangent, layer_scale):
    rows, total = cotangent.shape
    lanes = -(-rows // LANE) * LANE
    steps = 5
    block = total // steps
    return pl.pallas_call(
        prepare_kernel,
        grid=(steps,),
        in_specs=[pl.BlockSpec((rows, block), lambda i: (0, i)), pl.BlockSpec((1, block), lambda i: (0, i))],
        out_specs=pl.BlockSpec((block, lanes), lambda i: (i, 0)),
        out_shape=pltpu.HBM((total, lanes), jnp.bfloat16),
        compiler_params=pltpu.CompilerParams(vmem_limit_bytes=8 * MIB),
        cost_estimate=lasting(60),
        name="scaled_cotangent",
    )(in_hbm(cotangent), layer_scale)


def arrange_kernel(sizes, order, attended, *refs):
    *outs, sems = refs
    copies = []
    for out, size in zip(outs, sizes):
        for j in range(size):
            n = len(copies)
            copies.append(pltpu.make_async_copy(attended.at[order[n]], out.at[j], sems.at[n]))
    for copy in copies:
        copy.start()
    for copy in copies:
        copy.wait()


def arrange(order, attended, sizes):
    _, depth, rows = attended.shape
    return pl.pallas_call(
        functools.partial(arrange_kernel, sizes),
        grid_spec=pltpu.PrefetchScalarGridSpec(
            num_scalar_prefetch=1,
            grid=(1,),
            in_specs=[pl.BlockSpec(memory_space=pl.ANY)],
            out_specs=[pl.BlockSpec((size, depth, rows), lambda i, o: (0, 0, 0)) for size in sizes],
            scratch_shapes=[pltpu.SemaphoreType.DMA((sum(sizes),))],
        ),
        out_shape=[jax.ShapeDtypeStruct((size, depth, rows), attended.dtype) for size in sizes],
        compiler_params=pltpu.CompilerParams(vmem_limit_bytes=6 * MIB),
        cost_estimate=lasting(2),
        name="attended_chunks",
    )(order, in_hbm(attended))


PAIR = 2
EXPONENT = FACTOR * 1.4426950408889634


def forward_kernel(counts, qkv, attended, main_probs, slot_probs):
    def marks(image, ids):
        lane = lax.broadcasted_iota(jnp.int32, (image.shape[0], HS), 1)
        first = jnp.where(image == ids[0], 1.0, 0.0)
        second = jnp.where(image == ids[1], 1.0, 0.0)
        own = jnp.where(lane == 0, first, jnp.where(lane == 1, second, 0.0))
        other = jnp.where(lane == 0, 1.0 - first, jnp.where(lane == 1, 1.0 - second, 0.0)) * -1e30
        return own.astype(jnp.bfloat16), other.astype(jnp.bfloat16)

    main_at = lax.broadcasted_iota(jnp.int32, (MAIN, HS), 0)
    main_marks = marks(jnp.where(main_at >= counts[0], 1, 0), (0, 1))

    def image(at):
        first = jnp.where(at < counts[2], 2, -1)
        return jnp.where(at < SLOT, first, jnp.where(at - SLOT < counts[3], 3, -1))

    slot_marks = marks(image(lax.broadcasted_iota(jnp.int32, (2 * SLOT, HS), 0)), (2, 3))
    valid = image(lax.broadcasted_iota(jnp.int32, (1, 2 * SLOT), 1)) >= 0
    parts = []
    for head in range(PAIR):
        lanes = slice(head * HS, (head + 1) * HS)
        parts.append((head, 0, MAIN, lanes, main_marks, None, main_probs))
        parts.append((head, MAIN, 2 * SLOT, lanes, slot_marks, valid, slot_probs))
    scores = []
    for head, first, rows, lanes, (mark_query, mark_key), _, _ in parts:
        query = jnp.concatenate([qkv[0, first:first + rows, lanes], mark_query], axis=1)
        key = jnp.concatenate([qkv[1, first:first + rows, lanes], mark_key], axis=1)
        scores.append(dot(key, query, 1, 1))
    probs = []
    for score, (_, _, _, _, _, good, _) in zip(scores, parts):
        weights = jnp.exp2((score - jnp.max(score, axis=0, keepdims=True)) * EXPONENT)
        scale = 1.0 / jnp.sum(weights, axis=0, keepdims=True)
        probs.append(weights * (scale if good is None else jnp.where(good, scale, 0.0)))
    for prob, (head, first, rows, lanes, _, _, probs_ref) in zip(probs, parts):
        probs_ref[head] = prob
        result = dot(qkv[2, first:first + rows, lanes], prob.astype(jnp.bfloat16), 0, 0)
        attended[lanes, first:first + rows] = result.astype(jnp.bfloat16)


def forward(counts, qkv):
    _, rows, width = qkv.shape
    heads = width // HS
    return pl.pallas_call(
        forward_kernel,
        grid_spec=pltpu.PrefetchScalarGridSpec(
            num_scalar_prefetch=1,
            grid=(-(-heads // PAIR),),
            in_specs=[pl.BlockSpec((3, rows, PAIR * HS), lambda h, c: (0, 0, h))],
            out_specs=[
                pl.BlockSpec((PAIR * HS, rows), lambda h, c: (h, 0)),
                pl.BlockSpec((PAIR, MAIN, MAIN), lambda h, c: (h, 0, 0)),
                pl.BlockSpec((PAIR, 2 * SLOT, 2 * SLOT), lambda h, c: (h, 0, 0)),
            ],
        ),
        out_shape=[
            pltpu.HBM((width, rows), jnp.bfloat16),
            pltpu.HBM((heads, MAIN, MAIN), jnp.float32),
            pltpu.HBM((heads, 2 * SLOT, 2 * SLOT), jnp.float32),
        ],
        compiler_params=pltpu.CompilerParams(vmem_limit_bytes=12 * MIB),
        cost_estimate=lasting(60),
        name="attention_forward",
    )(counts, qkv)


def backward_kernel(qkv, grad_mine, grad_other, main_probs, slot_probs, *rest):
    grads = rest[-1]
    parts = []
    for head in range(PAIR):
        lanes = slice(head * HS, (head + 1) * HS)
        for first, rows, probs_ref in ((0, MAIN, main_probs), (MAIN, 2 * SLOT, slot_probs)):
            parts.append((head, slice(first, first + rows), lanes, probs_ref))
    grad, dprobs, dscores = [], [], []
    for head, at, lanes, _ in parts:
        both = grad_mine[lanes, at] + grad_other[lanes, at].astype(jnp.float32)
        grad.append(both.astype(jnp.bfloat16))
    for g, (head, at, lanes, _) in zip(grad, parts):
        dprobs.append(dot(qkv[2, at, lanes], g, 1, 0))
    for g, (head, at, lanes, probs_ref) in zip(grad, parts):
        grads[2, at, lanes] = dot(probs_ref[head].astype(jnp.bfloat16), g, 1, 1).astype(jnp.bfloat16)
    for dprob, (head, at, lanes, probs_ref) in zip(dprobs, parts):
        probs = probs_ref[head]
        delta = jnp.sum(probs * dprob, axis=0, keepdims=True)
        dscores.append((probs * (dprob - delta) * FACTOR).astype(jnp.bfloat16))
    for dscore, (head, at, lanes, _) in zip(dscores, parts):
        grads[1, at, lanes] = dot(dscore, qkv[0, at, lanes], 1, 0).astype(jnp.bfloat16)
        grads[0, at, lanes] = dot(dscore, qkv[1, at, lanes], 0, 0).astype(jnp.bfloat16)


def backward(qkv, grad_mine, grad_other, main_probs, slot_probs, low, high, grads):
    _, rows, width = qkv.shape
    held = [] if grads is None else [grads]
    return pl.pallas_call(
        backward_kernel,
        grid=(high - low,),
        in_specs=[
            pl.BlockSpec((3, rows, PAIR * HS), lambda h: (0, 0, h + low)),
            pl.BlockSpec((PAIR * HS, rows), lambda h: (h + low, 0)),
            pl.BlockSpec((PAIR * HS, rows), lambda h: (h + low, 0)),
            pl.BlockSpec((PAIR, MAIN, MAIN), lambda h: (h + low, 0, 0)),
            pl.BlockSpec((PAIR, 2 * SLOT, 2 * SLOT), lambda h: (h + low, 0, 0)),
        ] + [pl.BlockSpec(memory_space=pl.ANY)] * len(held),
        out_specs=pl.BlockSpec((3, rows, PAIR * HS), lambda h: (0, 0, h + low)),
        out_shape=pltpu.HBM(qkv.shape, jnp.bfloat16),
        input_output_aliases={5: 0} if held else {},
        compiler_params=pltpu.CompilerParams(vmem_limit_bytes=14 * MIB),
        cost_estimate=lasting(2 * (high - low)),
        name="attention_backward",
    )(qkv if held else in_hbm(qkv), grad_mine, grad_other, main_probs, slot_probs, *map(in_hbm, held))


def grad_out_kernel(sizes, split, total, info, turned, turned_other, *refs):
    mine, other, columns, tall, mine_rows, other_rows, in_sems, out_sems = refs[-8:]
    count, depth, rows = mine_rows.shape
    core = info[0]
    at = pl.ds(pl.multiple_of(core * (total - split), LANE), split)
    loads = [
        pltpu.make_async_copy(source.at[at], columns.at[i], in_sems.at[i]) for i, source in enumerate((turned, turned_other))
    ]
    index = 0
    for j, size in enumerate(sizes):
        first = 0
        for piece in refs[index:index + size]:
            target = tall.at[j] if size == 1 else tall.at[j, pl.ds(first, piece.shape[0])]
            loads.append(pltpu.make_async_copy(piece, target, in_sems.at[len(loads)]))
            first += piece.shape[0]
        index += size
    for load in loads:
        load.start()
    for load in loads:
        load.wait()

    @pl.when(core == 1)
    def _():
        shared = 2 * split - total
        columns[:, :shared, :] = jnp.zeros((2, shared, columns.shape[2]), jnp.bfloat16)

    stores = []
    for i, (result, out) in enumerate(((mine_rows, mine), (other_rows, other))):
        if depth % 16 == 0:
            product = dot(tall[...].reshape(count * depth, split), columns[i], 1, 0)[:, :rows]
            result[...] = product.astype(result.dtype).reshape(count, depth, rows)
        else:
            for j in range(count):
                result[j] = dot(tall[j], columns[i], 1, 0)[:, :rows].astype(result.dtype)
        for j in range(count):
            stores.append(pltpu.make_async_copy(result.at[j], out.at[info[1 + j]], out_sems.at[i, j]))
            stores[-1].start()
    for store in stores:
        store.wait()


def grad_out_rows(info, turned, turned_other, rows, pieces, shards, held):
    total, lanes = turned.shape
    split = pieces[0][0].shape[1]
    depth = sum(p.shape[0] for p in pieces[0])
    sizes = [len(p) for p in pieces]
    arrays = [a for p in pieces for a in p]
    count = len(pieces)
    held = [] if held is None else list(held)
    return pl.pallas_call(
        functools.partial(grad_out_kernel, sizes, split, total),
        grid_spec=pltpu.PrefetchScalarGridSpec(
            num_scalar_prefetch=1,
            grid=(1,),
            in_specs=[pl.BlockSpec(memory_space=pl.ANY)] * (2 + len(arrays) + len(held)),
            out_specs=[pl.BlockSpec(memory_space=pl.ANY)] * 2,
            scratch_shapes=[
                pltpu.VMEM((2, split, lanes), jnp.bfloat16),
                pltpu.VMEM((count, depth, split), jnp.bfloat16),
                pltpu.VMEM((count, depth, rows), jnp.float32),
                pltpu.VMEM((count, depth, rows), jnp.bfloat16),
                pltpu.SemaphoreType.DMA((2 + len(arrays),)),
                pltpu.SemaphoreType.DMA((2, count)),
            ],
        ),
        out_shape=[
            pltpu.HBM((shards, depth, rows), jnp.float32),
            pltpu.HBM((shards, depth, rows), jnp.bfloat16),
        ],
        input_output_aliases={3 + len(arrays) + i: i for i in range(len(held))},
        compiler_params=pltpu.CompilerParams(vmem_limit_bytes=16 * MIB),
        cost_estimate=lasting(0.2 if held else 1.5 * len(pieces)),
        name="grad_out_rows",
    )(info, in_hbm(turned), turned_other, *arrays, *map(in_hbm, held))


def half_kernel(starts, weight, out, sem):
    copy = pltpu.make_async_copy(weight.at[:, pl.ds(pl.multiple_of(starts[0], LANE), out.shape[1])], out, sem)
    copy.start()
    copy.wait()


def half_columns(start, weight, width):
    return pl.pallas_call(
        half_kernel,
        grid_spec=pltpu.PrefetchScalarGridSpec(
            num_scalar_prefetch=1,
            grid=(1,),
            in_specs=[pl.BlockSpec(memory_space=pl.ANY)],
            out_specs=pl.BlockSpec(memory_space=pl.ANY),
            scratch_shapes=[pltpu.SemaphoreType.DMA],
        ),
        out_shape=jax.ShapeDtypeStruct((weight.shape[0], width), weight.dtype),
        compiler_params=pltpu.CompilerParams(vmem_limit_bytes=2 * MIB),
        cost_estimate=lasting(1),
        name="own_half_of_weight",
    )(start, in_hbm(weight))


def finish_kernel(offsets, start, term, came_up, came_down, out):
    total = term[...] + came_up[...].astype(jnp.float32) + came_down[...].astype(jnp.float32)
    for offset in offsets:

        @pl.when(start[0] == offset)
        def _():
            out[...] = total[:, offset:offset + out.shape[1]]


def finish(start, term, came_up, came_down, owned, offsets):
    depth, window = term.shape
    block = pl.BlockSpec((depth, window), lambda i, s: (0, 0))
    return pl.pallas_call(
        functools.partial(finish_kernel, offsets),
        grid_spec=pltpu.PrefetchScalarGridSpec(
            num_scalar_prefetch=1,
            grid=(1,),
            in_specs=[block] * 3,
            out_specs=pl.BlockSpec((depth, owned), lambda i, s: (0, 0)),
        ),
        out_shape=jax.ShapeDtypeStruct((depth, owned), jnp.float32),
        compiler_params=pltpu.CompilerParams(vmem_limit_bytes=8 * MIB),
        cost_estimate=lasting(2),
        name="last_sum",
    )(start, term, came_up, came_down)


def partial_kernel(chosen, turned_round, sources, parts, count, window, order, start, *refs):
    per = 1 if chosen or len(turned_round) != 2 else 2
    attended, columns = refs[:sources * per], refs[sources * per:sources * (per + parts)]
    chunks, held, sems = refs[-3:]
    bases = refs[sources * (per + parts):-3 - count]
    outs = refs[-3 - count:-3]
    depth, rows = chunks.shape[2:]
    at = pl.ds(pl.multiple_of(start[0], LANE), window)
    copies = []
    for i in range(sources):
        some, first = [], 0
        for part in range(parts):
            source = columns[i * parts + part]
            if chosen:
                some.append(pltpu.make_async_copy(source.at[at], held.at[i], sems.at[i, count + part]))
            else:
                target = held.at[i, pl.ds(first, source.shape[0])]
                some.append(pltpu.make_async_copy(source.at[:, at], target, sems.at[i, count + part]))
            first += source.shape[0]
        for j in range(count):
            at_j = order[j] if chosen else turned_round[j] if i % 2 else j
            source = attended[i].at[at_j] if per == 1 else attended[i * per + at_j].at[0]
            some.append(pltpu.make_async_copy(source, chunks.at[i, j], sems.at[i, j]))
        copies.append(some)
    for some in copies:
        for copy in some:
            copy.start()
    most = 4 if depth % 16 == 0 else 1
    for first in range(0, count, most):
        some = min(most, count - first)
        total = None
        for i in range(sources):
            if first == 0:
                for copy in copies[i]:
                    copy.wait()
            tall = chunks[i, first:first + some].reshape(some * depth, rows) if some > 1 else chunks[i, first]
            part = dot(tall, held[i][:, :rows], 1, 1) if chosen else dot(tall, held[i], 1, 0)
            total = part if total is None else total + part
        for j in range(some):
            result = total[j * depth:(j + 1) * depth]
            if bases:
                result += bases[first + j][...].astype(jnp.float32)
            outs[first + j][...] = result.astype(outs[first + j].dtype)


def partial_products(order, start, attended, columns, window, bases=(), turned_round=()):
    _, depth, rows = attended[0].shape
    per = 2 if len(turned_round) == 2 else 1
    parts = len(columns) * per // len(attended)
    count, sources = order.shape[0], len(attended) // per
    block = pl.BlockSpec((depth, window), lambda j, o, s: (0, 0))
    return pl.pallas_call(
        functools.partial(partial_kernel, not bases, turned_round, sources, parts, count, window),
        grid_spec=pltpu.PrefetchScalarGridSpec(
            num_scalar_prefetch=2,
            grid=(1,),
            in_specs=[pl.BlockSpec(memory_space=pl.ANY)] * (sources * (per + parts)) + [block] * len(bases),
            out_specs=[block] * count,
            scratch_shapes=[
                pltpu.VMEM((sources, count, depth, rows), jnp.bfloat16),
                pltpu.VMEM((sources, rows, window) if bases else (sources, window, columns[0].shape[1]), jnp.bfloat16),
                pltpu.SemaphoreType.DMA((sources, count + parts)),
            ],
        ),
        out_shape=[
            jax.ShapeDtypeStruct((depth, window), jnp.float32) if bases else pltpu.HBM((depth, window), jnp.bfloat16)
        ] * count,
        compiler_params=pltpu.CompilerParams(vmem_limit_bytes=(16 if bases else 18) * MIB),
        cost_estimate=lasting(3 if bases else 6),
        name="projection_peers" if bases else "projection_chip",
    )(order, start, *attended, *columns, *map(in_hbm, bases))


def windows_of(groups, owned, total):
    lows = [g * owned // LANE * LANE for g in range(groups)]
    width = max(-(-((g + 1) * owned) // LANE) * LANE - low for g, low in enumerate(lows))
    return width


def ring_of(count):
    return list(range(0, count, 2)) + list(range(count - 1, 0, -2))


def local(members, shards, query_key_value, cotangent, proj_weight, layer_scale, lengths):
    member = lax.axis_index("dp")
    shard = lax.axis_index("fsdp")
    core, chip, peers = member % 2, member // 2, members // 2
    ring = ring_of(shards)
    place = jnp.where(shard % 2 == 0, shard // 2, shards - 1 - shard // 2)
    ahead = [(ring[i], ring[(i + 1) % shards]) for i in range(shards)]
    behind = [(ring[i], ring[(i - 1) % shards]) for i in range(shards)]
    ways = [ahead, behind]
    streams = [
        [(d * shards + a, d * shards + b) for d in range(members) for a, b in ways[(d + turn) % 2]] for turn in range(2)
    ]
    half = shards // 2
    depth, total = proj_weight.shape
    rows, width = query_key_value.shape[1:]
    owned = total // members
    counts = lax.dynamic_index_in_dim(lengths[:, 0, :], member, 0, keepdims=False)

    def send(array, stream):
        return lax.ppermute(array, ("dp", "fsdp"), streams[stream])

    def swap(array, bit):
        return lax.ppermute(array, "dp", [(i, i ^ bit) for i in range(members)])

    def shard_at(offset):
        at = (place + (1 - 2 * core) * offset + shards) % shards
        return jnp.where(at < half, 2 * at, 2 * (shards - 1 - at) + 1)

    def table(values):
        return jnp.stack([jnp.asarray(v) for v in values]).astype(jnp.int32)

    chip_width, window = windows_of(peers, 2 * owned, total), windows_of(members, owned, total)

    def chip_start(chip):
        return jnp.minimum(chip * 2 * owned // LANE * LANE, total - chip_width)

    my_start = jnp.minimum(member * owned // LANE * LANE, chip_start(chip) + chip_width - window)
    starts = table([my_start, my_start - chip_start(chip)])

    split = -(-(total // LANE) // 2) * LANE
    mine = half_columns(table([core * (total - split)]), proj_weight, split)
    up, down = [mine], [mine]
    up.append(send(up[-1], 0))
    down.append(send(down[-1], 1))

    mine, cotangent = lax.optimization_barrier((mine, cotangent))
    scales = layer_scale.reshape(1, total)
    sent = peer_windows(
        table([chip_start(chip ^ k) for k in range(1, peers)] or [0]), cotangent, scales, peers - 1, chip_width
    )
    sent, cotangent = lax.optimization_barrier((sent, cotangent))
    came_columns = [[swap(array, 2 * k) for k, array in enumerate(part, 1)] for part in sent]
    turned = prepare(cotangent, scales)
    attended, main_probs, slot_probs = forward(counts, query_key_value)
    attended = attended.reshape(shards, depth, rows)
    near = [[o, -o] for o in range(half - 1, 0, -1)]
    groups = [[half] + near[0]] + near[1:-1] + [near[-1] + [0]]
    flat = table([shard_at(o) for group in groups for o in group])
    sizes = [len(group) for group in groups]
    orders = [flat[sum(sizes[:g]):sum(sizes[:g + 1])] for g in range(len(groups))]

    def rows_of(some, held):
        info = table([core] + [shard_at(o) for _, o in some])
        return grad_out_rows(info, turned, turned_other, rows, [p for p, _ in some], shards, held)

    up[1], down[1], attended, came_columns[0], turned = lax.optimization_barrier(
        (up[1], down[1], attended, came_columns[0], turned)
    )
    turned_other = swap(turned, 1)
    other_columns = [[swap(array, 1) for array in came_columns[0]]]
    attended_other = swap(attended, 1)
    chunks = list(arrange(flat, attended, [n for size in sizes for n in ([1, 1] if size == 2 else [size])]))
    bounds = [0]
    for size in sizes:
        bounds.append(bounds[-1] + (2 if size == 2 else 1))
    attended_other, chunks = lax.optimization_barrier((attended_other, chunks))
    for _ in range(half - 3):
        up.append(send(up[-1], 0))
        down.append(send(down[-1], 1))
    bases = partial_products(
        flat, starts[:1], [in_hbm(attended), attended_other], [in_hbm(turned), turned_other], window
    )
    up[-1], down[-1], turned_other, attended_other, *bases = lax.optimization_barrier(
        (up[-1], down[-1], turned_other, attended_other, *bases)
    )
    bases = dict(zip([o for group in groups for o in group], bases))

    late, chunks = lax.optimization_barrier((came_columns[1], chunks))
    came = [[swap(chunks[0], 2 * k) for k in range(1, peers)]]
    halves = [[swap(chunks[1], 2 * k) for k in range(1, peers)]]
    other_columns.append([swap(array, 1) for array in late])
    came_columns[1] = late
    columns = []
    for k in range(peers - 1):
        for arrays in (came_columns, other_columns):
            columns += [in_hbm(part[k]) for part in arrays]
    pieces = [([mine], 0)]
    for step in range(1, half - 1):
        pieces += [([up[step]], -step), ([down[step]], step)]
    pieces[:-2] = [([in_hbm(array) for array in arrays], o) for arrays, o in pieces[:-2]]
    grad_out = rows_of(pieces, None)
    up.append(send(up[-1], 0))
    down.append(send(down[-1], 1))
    up[-1], down[-1], grad_out = lax.optimization_barrier((up[-1], down[-1], grad_out))
    far = send(up[-1], 0)
    came[0], near_up, near_down = lax.optimization_barrier((came[0], up[-1], down[-1]))

    def both_cores(arrays):
        per = len(arrays) // max(peers - 1, 1)
        held = [arrays[n:n + per] for n in range(0, len(arrays), per)]
        return [a for some in held for a in (*some, *[swap(c, 1) for c in some])]

    def products(index, taken):
        group = groups[index]
        if not taken:
            return {o: bases[o] for o in group}
        turned_round = [group.index(-o) if -o in group else j for j, o in enumerate(group)]
        result = partial_products(orders[index], starts[1:], taken, columns, window, [bases[o] for o in group], turned_round)
        return dict(zip(group, result))

    terms = products(0, both_cores(came[0]))
    first = terms[half].astype(jnp.bfloat16)
    first, halves[0], chunks, far = lax.optimization_barrier((first, halves[0], chunks, far))
    halves.append([swap(chunks[2], 2 * k) for k in range(1, peers)])
    came.append([pair[k] for k in range(peers - 1) for pair in halves])
    came_up, came_down = send(first, 0), None

    steps = [0, 3, 5, -(-(width // HS) // PAIR)]
    grads = None
    for step in range(half, 1, -1):
        going_up = (terms[step - 1] + came_up.astype(jnp.float32)).astype(jnp.bfloat16)
        going_down = terms[1 - step] if came_down is None else terms[1 - step] + came_down.astype(jnp.float32)
        going_down = going_down.astype(jnp.bfloat16)
        if step == half:
            going_up, going_down, near_up, chunks = lax.optimization_barrier((going_up, going_down, near_up, chunks))
            for g in range(2, len(groups)):
                came.append([swap(some, 2 * k) for k in range(1, peers) for some in chunks[bounds[g]:bounds[g + 1]]])
            near_up, came[1] = lax.optimization_barrier((near_up, came[1]))
            terms.update(products(1, both_cores(came[1])))
            grad_out = rows_of([([near_up], 1 - half), ([near_down], half - 1), ([far], half)], grad_out)
            grad_mine = grad_out[0].reshape(width, rows)
            came[2], grad_other = lax.optimization_barrier((came[2], grad_out[1]))
            grad_other = swap(grad_other, 1).reshape(width, rows)
        elif step > 2:
            arrived = came[half - step + 1]
            going_up, going_down, arrived, grad_mine = lax.optimization_barrier((going_up, going_down, arrived, grad_mine))
            terms.update(products(half - step + 1, [in_hbm(array) for array in both_cores(arrived)]))
        else:
            going_up, going_down = lax.optimization_barrier((going_up, going_down))
        came_up, came_down = send(going_up, 0), send(going_down, 1)
    for low, high in zip(steps, steps[1:]):
        grads = backward(query_key_value, grad_mine, grad_other, main_probs, slot_probs, low, high, grads)
    came_up, came_down, grads = lax.optimization_barrier((came_up, came_down, grads))
    offsets = set()
    for m in range(members):
        low = min((m // 2) * 2 * owned // LANE * LANE, total - chip_width)
        offsets.add(m * owned - min(m * owned // LANE * LANE, low + chip_width - window))
    grad_proj = finish(table([member * owned - my_start]), terms[0], came_up, came_down, owned, sorted(offsets))
    return grads, grad_proj


def solution(mesh):
    members, shards = mesh.shape["dp"], mesh.shape["fsdp"]
    placed = (
        P(None, ("dp", "fsdp"), None),
        P(("dp", "fsdp"), None),
        P("fsdp", None),
        P(),
        P(None, "fsdp", None),
    )
    return jax.shard_map(
        functools.partial(local, members, shards),
        mesh=mesh,
        in_specs=placed,
        out_specs=(P(None, ("dp", "fsdp"), None), P("fsdp", "dp")),
        check_vma=False,
    )
```

```python
import functools

import jax
import jax.numpy as jnp
from jax import lax
from jax.experimental import pallas as pl
from jax.experimental.pallas import tpu as pltpu
from jax.sharding import PartitionSpec as P

HS = 128
MAIN = 256
SLOT = 96
LANE = 128
FACTOR = HS ** (-0.5)
MIB = 1024 * 1024


def lasting(microseconds):
    return pl.CostEstimate(flops=int(microseconds * 575000000), bytes_accessed=1000, transcendentals=0)


def dot(left, right, left_dim, right_dim):
    return lax.dot_general(left, right, (((left_dim,), (right_dim,)), ((), ())), preferred_element_type=jnp.float32)


def in_hbm(array):
    return pltpu.with_memory_space_constraint(array, pltpu.HBM)


def window_kernel(peers, starts, cotangent, layer_scale, *refs):
    windows, (held, sems) = refs[:-2], refs[-2:]
    parts = len(windows) // peers
    width = held.shape[2]
    copies = []
    for k in range(peers):
        at = pl.ds(pl.multiple_of(starts[k], LANE), width)
        first = 0
        for part in range(parts):
            rows = pl.ds(first, windows[part].shape[0])
            copies.append(pltpu.make_async_copy(cotangent.at[rows, at], held.at[k, rows], sems.at[k, part]))
            first += windows[part].shape[0]
    for copy in copies:
        copy.start()
    for k in range(peers):
        scale = layer_scale[:, pl.ds(pl.multiple_of(starts[k], LANE), width)]
        first = 0
        for part in range(parts):
            copies[k * parts + part].wait()
            window = windows[k * parts + part]
            values = held[k, first:first + window.shape[0], :].astype(jnp.float32)
            window[...] = (values * scale).astype(jnp.bfloat16)
            first += window.shape[0]


def peer_windows(starts, cotangent, layer_scale, peers, width):
    rows, total = cotangent.shape
    first = rows * 2 // 5 // 16 * 16
    parts = (first, rows - first)
    arrays = pl.pallas_call(
        functools.partial(window_kernel, peers),
        grid_spec=pltpu.PrefetchScalarGridSpec(
            num_scalar_prefetch=1,
            grid=(1,),
            in_specs=[pl.BlockSpec(memory_space=pl.ANY), pl.BlockSpec((1, total), lambda i, s: (0, 0))],
            out_specs=[pl.BlockSpec((part, width), lambda i, s: (0, 0)) for part in parts] * peers,
            scratch_shapes=[
                pltpu.VMEM((peers, rows, width), jnp.bfloat16),
                pltpu.SemaphoreType.DMA((peers, len(parts))),
            ],
        ),
        out_shape=[pltpu.HBM((part, width), jnp.bfloat16) for part in parts] * peers,
        compiler_params=pltpu.CompilerParams(vmem_limit_bytes=8 * MIB),
        cost_estimate=lasting(60),
        name="peer_windows",
    )(starts, in_hbm(cotangent), layer_scale)
    return [arrays[part::len(parts)] for part in range(len(parts))]


def prepare_kernel(cotangent, layer_scale, turned):
    values = (cotangent[...].astype(jnp.float32) * layer_scale[...]).astype(jnp.bfloat16)
    spare = jnp.zeros((turned.shape[1] - values.shape[0], values.shape[1]), jnp.bfloat16)
    turned[...] = jnp.concatenate([values, spare], axis=0).T


def prepare(cotangent, layer_scale):
    rows, total = cotangent.shape
    lanes = -(-rows // LANE) * LANE
    steps = 5
    block = total // steps
    return pl.pallas_call(
        prepare_kernel,
        grid=(steps,),
        in_specs=[pl.BlockSpec((rows, block), lambda i: (0, i)), pl.BlockSpec((1, block), lambda i: (0, i))],
        out_specs=pl.BlockSpec((block, lanes), lambda i: (i, 0)),
        out_shape=pltpu.HBM((total, lanes), jnp.bfloat16),
        compiler_params=pltpu.CompilerParams(vmem_limit_bytes=8 * MIB),
        cost_estimate=lasting(60),
        name="scaled_cotangent",
    )(in_hbm(cotangent), layer_scale)


def arrange_kernel(sizes, order, attended, *refs):
    *outs, sems = refs
    copies = []
    for out, size in zip(outs, sizes):
        for j in range(size):
            n = len(copies)
            copies.append(pltpu.make_async_copy(attended.at[order[n]], out.at[j], sems.at[n]))
    for copy in copies:
        copy.start()
    for copy in copies:
        copy.wait()


def arrange(order, attended, sizes):
    _, depth, rows = attended.shape
    return pl.pallas_call(
        functools.partial(arrange_kernel, sizes),
        grid_spec=pltpu.PrefetchScalarGridSpec(
            num_scalar_prefetch=1,
            grid=(1,),
            in_specs=[pl.BlockSpec(memory_space=pl.ANY)],
            out_specs=[pl.BlockSpec((size, depth, rows), lambda i, o: (0, 0, 0)) for size in sizes],
            scratch_shapes=[pltpu.SemaphoreType.DMA((sum(sizes),))],
        ),
        out_shape=[jax.ShapeDtypeStruct((size, depth, rows), attended.dtype) for size in sizes],
        compiler_params=pltpu.CompilerParams(vmem_limit_bytes=6 * MIB),
        cost_estimate=lasting(2),
        name="attended_chunks",
    )(order, in_hbm(attended))


PAIR = 2
EXPONENT = FACTOR * 1.4426950408889634


def forward_kernel(counts, qkv, attended, main_probs, slot_probs):
    def marks(image, ids):
        lane = lax.broadcasted_iota(jnp.int32, (image.shape[0], HS), 1)
        first = jnp.where(image == ids[0], 1.0, 0.0)
        second = jnp.where(image == ids[1], 1.0, 0.0)
        own = jnp.where(lane == 0, first, jnp.where(lane == 1, second, 0.0))
        other = jnp.where(lane == 0, 1.0 - first, jnp.where(lane == 1, 1.0 - second, 0.0)) * -1e30
        return own.astype(jnp.bfloat16), other.astype(jnp.bfloat16)

    main_at = lax.broadcasted_iota(jnp.int32, (MAIN, HS), 0)
    main_marks = marks(jnp.where(main_at >= counts[0], 1, 0), (0, 1))

    def image(at):
        first = jnp.where(at < counts[2], 2, -1)
        return jnp.where(at < SLOT, first, jnp.where(at - SLOT < counts[3], 3, -1))

    slot_marks = marks(image(lax.broadcasted_iota(jnp.int32, (2 * SLOT, HS), 0)), (2, 3))
    valid = image(lax.broadcasted_iota(jnp.int32, (1, 2 * SLOT), 1)) >= 0
    parts = []
    for head in range(PAIR):
        lanes = slice(head * HS, (head + 1) * HS)
        parts.append((head, 0, MAIN, lanes, main_marks, None, main_probs))
        parts.append((head, MAIN, 2 * SLOT, lanes, slot_marks, valid, slot_probs))
    scores = []
    for head, first, rows, lanes, (mark_query, mark_key), _, _ in parts:
        query = jnp.concatenate([qkv[0, first:first + rows, lanes], mark_query], axis=1)
        key = jnp.concatenate([qkv[1, first:first + rows, lanes], mark_key], axis=1)
        scores.append(dot(key, query, 1, 1))
    probs = []
    for score, (_, _, _, _, _, good, _) in zip(scores, parts):
        weights = jnp.exp2((score - jnp.max(score, axis=0, keepdims=True)) * EXPONENT)
        scale = 1.0 / jnp.sum(weights, axis=0, keepdims=True)
        probs.append(weights * (scale if good is None else jnp.where(good, scale, 0.0)))
    for prob, (head, first, rows, lanes, _, _, probs_ref) in zip(probs, parts):
        probs_ref[head] = prob
        result = dot(qkv[2, first:first + rows, lanes], prob.astype(jnp.bfloat16), 0, 0)
        attended[lanes, first:first + rows] = result.astype(jnp.bfloat16)


def forward(counts, qkv):
    _, rows, width = qkv.shape
    heads = width // HS
    return pl.pallas_call(
        forward_kernel,
        grid_spec=pltpu.PrefetchScalarGridSpec(
            num_scalar_prefetch=1,
            grid=(-(-heads // PAIR),),
            in_specs=[pl.BlockSpec((3, rows, PAIR * HS), lambda h, c: (0, 0, h))],
            out_specs=[
                pl.BlockSpec((PAIR * HS, rows), lambda h, c: (h, 0)),
                pl.BlockSpec((PAIR, MAIN, MAIN), lambda h, c: (h, 0, 0)),
                pl.BlockSpec((PAIR, 2 * SLOT, 2 * SLOT), lambda h, c: (h, 0, 0)),
            ],
        ),
        out_shape=[
            pltpu.HBM((width, rows), jnp.bfloat16),
            pltpu.HBM((heads, MAIN, MAIN), jnp.float32),
            pltpu.HBM((heads, 2 * SLOT, 2 * SLOT), jnp.float32),
        ],
        compiler_params=pltpu.CompilerParams(vmem_limit_bytes=12 * MIB),
        cost_estimate=lasting(60),
        name="attention_forward",
    )(counts, qkv)


def backward_kernel(qkv, grad_mine, grad_other, main_probs, slot_probs, *rest):
    grads = rest[-1]
    parts = []
    for head in range(PAIR):
        lanes = slice(head * HS, (head + 1) * HS)
        for first, rows, probs_ref in ((0, MAIN, main_probs), (MAIN, 2 * SLOT, slot_probs)):
            parts.append((head, slice(first, first + rows), lanes, probs_ref))
    grad, dprobs, dscores = [], [], []
    for head, at, lanes, _ in parts:
        both = grad_mine[lanes, at] + grad_other[lanes, at].astype(jnp.float32)
        grad.append(both.astype(jnp.bfloat16))
    for g, (head, at, lanes, _) in zip(grad, parts):
        dprobs.append(dot(qkv[2, at, lanes], g, 1, 0))
    for g, (head, at, lanes, probs_ref) in zip(grad, parts):
        grads[2, at, lanes] = dot(probs_ref[head].astype(jnp.bfloat16), g, 1, 1).astype(jnp.bfloat16)
    for dprob, (head, at, lanes, probs_ref) in zip(dprobs, parts):
        probs = probs_ref[head]
        delta = jnp.sum(probs * dprob, axis=0, keepdims=True)
        dscores.append((probs * (dprob - delta) * FACTOR).astype(jnp.bfloat16))
    for dscore, (head, at, lanes, _) in zip(dscores, parts):
        grads[1, at, lanes] = dot(dscore, qkv[0, at, lanes], 1, 0).astype(jnp.bfloat16)
        grads[0, at, lanes] = dot(dscore, qkv[1, at, lanes], 0, 0).astype(jnp.bfloat16)


def backward(qkv, grad_mine, grad_other, main_probs, slot_probs, low, high, grads):
    _, rows, width = qkv.shape
    held = [] if grads is None else [grads]
    return pl.pallas_call(
        backward_kernel,
        grid=(high - low,),
        in_specs=[
            pl.BlockSpec((3, rows, PAIR * HS), lambda h: (0, 0, h + low)),
            pl.BlockSpec((PAIR * HS, rows), lambda h: (h + low, 0)),
            pl.BlockSpec((PAIR * HS, rows), lambda h: (h + low, 0)),
            pl.BlockSpec((PAIR, MAIN, MAIN), lambda h: (h + low, 0, 0)),
            pl.BlockSpec((PAIR, 2 * SLOT, 2 * SLOT), lambda h: (h + low, 0, 0)),
        ] + [pl.BlockSpec(memory_space=pl.ANY)] * len(held),
        out_specs=pl.BlockSpec((3, rows, PAIR * HS), lambda h: (0, 0, h + low)),
        out_shape=pltpu.HBM(qkv.shape, jnp.bfloat16),
        input_output_aliases={5: 0} if held else {},
        compiler_params=pltpu.CompilerParams(vmem_limit_bytes=14 * MIB),
        cost_estimate=lasting(2 * (high - low)),
        name="attention_backward",
    )(qkv if held else in_hbm(qkv), grad_mine, grad_other, main_probs, slot_probs, *map(in_hbm, held))


def grad_out_kernel(sizes, split, total, info, turned, turned_other, *refs):
    mine, other, columns, tall, mine_rows, other_rows, in_sems, out_sems = refs[-8:]
    count, depth, rows = mine_rows.shape
    core = info[0]
    at = pl.ds(pl.multiple_of(core * (total - split), LANE), split)
    loads = [
        pltpu.make_async_copy(source.at[at], columns.at[i], in_sems.at[i]) for i, source in enumerate((turned, turned_other))
    ]
    index = 0
    for j, size in enumerate(sizes):
        first = 0
        for piece in refs[index:index + size]:
            target = tall.at[j] if size == 1 else tall.at[j, pl.ds(first, piece.shape[0])]
            loads.append(pltpu.make_async_copy(piece, target, in_sems.at[len(loads)]))
            first += piece.shape[0]
        index += size
    for load in loads:
        load.start()
    for load in loads:
        load.wait()

    @pl.when(core == 1)
    def _():
        shared = 2 * split - total
        columns[:, :shared, :] = jnp.zeros((2, shared, columns.shape[2]), jnp.bfloat16)

    stores = []
    for i, (result, out) in enumerate(((mine_rows, mine), (other_rows, other))):
        if depth % 16 == 0:
            product = dot(tall[...].reshape(count * depth, split), columns[i], 1, 0)[:, :rows]
            result[...] = product.astype(result.dtype).reshape(count, depth, rows)
        else:
            for j in range(count):
                result[j] = dot(tall[j], columns[i], 1, 0)[:, :rows].astype(result.dtype)
        for j in range(count):
            stores.append(pltpu.make_async_copy(result.at[j], out.at[info[1 + j]], out_sems.at[i, j]))
            stores[-1].start()
    for store in stores:
        store.wait()


def grad_out_rows(info, turned, turned_other, rows, pieces, shards, held):
    total, lanes = turned.shape
    split = pieces[0][0].shape[1]
    depth = sum(p.shape[0] for p in pieces[0])
    sizes = [len(p) for p in pieces]
    arrays = [a for p in pieces for a in p]
    count = len(pieces)
    held = [] if held is None else list(held)
    return pl.pallas_call(
        functools.partial(grad_out_kernel, sizes, split, total),
        grid_spec=pltpu.PrefetchScalarGridSpec(
            num_scalar_prefetch=1,
            grid=(1,),
            in_specs=[pl.BlockSpec(memory_space=pl.ANY)] * (2 + len(arrays) + len(held)),
            out_specs=[pl.BlockSpec(memory_space=pl.ANY)] * 2,
            scratch_shapes=[
                pltpu.VMEM((2, split, lanes), jnp.bfloat16),
                pltpu.VMEM((count, depth, split), jnp.bfloat16),
                pltpu.VMEM((count, depth, rows), jnp.float32),
                pltpu.VMEM((count, depth, rows), jnp.bfloat16),
                pltpu.SemaphoreType.DMA((2 + len(arrays),)),
                pltpu.SemaphoreType.DMA((2, count)),
            ],
        ),
        out_shape=[
            pltpu.HBM((shards, depth, rows), jnp.float32),
            pltpu.HBM((shards, depth, rows), jnp.bfloat16),
        ],
        input_output_aliases={3 + len(arrays) + i: i for i in range(len(held))},
        compiler_params=pltpu.CompilerParams(vmem_limit_bytes=16 * MIB),
        cost_estimate=lasting(0.2 if held else 1.5 * len(pieces)),
        name="grad_out_rows",
    )(info, in_hbm(turned), turned_other, *arrays, *map(in_hbm, held))


def half_kernel(starts, weight, out, sem):
    copy = pltpu.make_async_copy(weight.at[:, pl.ds(pl.multiple_of(starts[0], LANE), out.shape[1])], out, sem)
    copy.start()
    copy.wait()


def half_columns(start, weight, width):
    return pl.pallas_call(
        half_kernel,
        grid_spec=pltpu.PrefetchScalarGridSpec(
            num_scalar_prefetch=1,
            grid=(1,),
            in_specs=[pl.BlockSpec(memory_space=pl.ANY)],
            out_specs=pl.BlockSpec(memory_space=pl.ANY),
            scratch_shapes=[pltpu.SemaphoreType.DMA],
        ),
        out_shape=jax.ShapeDtypeStruct((weight.shape[0], width), weight.dtype),
        compiler_params=pltpu.CompilerParams(vmem_limit_bytes=2 * MIB),
        cost_estimate=lasting(1),
        name="own_half_of_weight",
    )(start, in_hbm(weight))


def finish_kernel(offsets, start, term, came_up, came_down, out):
    total = term[...] + came_up[...].astype(jnp.float32) + came_down[...].astype(jnp.float32)
    for offset in offsets:

        @pl.when(start[0] == offset)
        def _():
            out[...] = total[:, offset:offset + out.shape[1]]


def finish(start, term, came_up, came_down, owned, offsets):
    depth, window = term.shape
    block = pl.BlockSpec((depth, window), lambda i, s: (0, 0))
    return pl.pallas_call(
        functools.partial(finish_kernel, offsets),
        grid_spec=pltpu.PrefetchScalarGridSpec(
            num_scalar_prefetch=1,
            grid=(1,),
            in_specs=[block] * 3,
            out_specs=pl.BlockSpec((depth, owned), lambda i, s: (0, 0)),
        ),
        out_shape=jax.ShapeDtypeStruct((depth, owned), jnp.float32),
        compiler_params=pltpu.CompilerParams(vmem_limit_bytes=8 * MIB),
        cost_estimate=lasting(2),
        name="last_sum",
    )(start, term, came_up, came_down)


def partial_kernel(chosen, turned_round, sources, parts, count, window, order, start, *refs):
    attended, columns = refs[:sources], refs[sources:sources * (1 + parts)]
    chunks, held, sems = refs[-3:]
    bases = refs[sources * (1 + parts):-3 - count]
    outs = refs[-3 - count:-3]
    depth, rows = chunks.shape[2:]
    at = pl.ds(pl.multiple_of(start[0], LANE), window)
    copies = []
    for i in range(sources):
        some, first = [], 0
        for part in range(parts):
            source = columns[i * parts + part]
            if chosen:
                some.append(pltpu.make_async_copy(source.at[at], held.at[i], sems.at[i, count + part]))
            else:
                target = held.at[i, pl.ds(first, source.shape[0])]
                some.append(pltpu.make_async_copy(source.at[:, at], target, sems.at[i, count + part]))
            first += source.shape[0]
        for j in range(count):
            source = attended[i].at[order[j] if chosen else turned_round[j] if i % 2 else j]
            some.append(pltpu.make_async_copy(source, chunks.at[i, j], sems.at[i, j]))
        copies.append(some)
    for some in copies:
        for copy in some:
            copy.start()
    most = 4 if depth % 16 == 0 else 1
    for first in range(0, count, most):
        some = min(most, count - first)
        total = None
        for i in range(sources):
            if first == 0:
                for copy in copies[i]:
                    copy.wait()
            tall = chunks[i, first:first + some].reshape(some * depth, rows) if some > 1 else chunks[i, first]
            part = dot(tall, held[i][:, :rows], 1, 1) if chosen else dot(tall, held[i], 1, 0)
            total = part if total is None else total + part
        for j in range(some):
            result = total[j * depth:(j + 1) * depth]
            if bases:
                result += bases[first + j][...].astype(jnp.float32)
            outs[first + j][...] = result.astype(outs[first + j].dtype)


def partial_products(order, start, attended, columns, window, bases=(), turned_round=()):
    _, depth, rows = attended[0].shape
    parts = len(columns) // len(attended)
    count, sources = order.shape[0], len(attended)
    block = pl.BlockSpec((depth, window), lambda j, o, s: (0, 0))
    return pl.pallas_call(
        functools.partial(partial_kernel, not bases, turned_round, sources, parts, count, window),
        grid_spec=pltpu.PrefetchScalarGridSpec(
            num_scalar_prefetch=2,
            grid=(1,),
            in_specs=[pl.BlockSpec(memory_space=pl.ANY)] * (sources * (1 + parts)) + [block] * len(bases),
            out_specs=[block] * count,
            scratch_shapes=[
                pltpu.VMEM((sources, count, depth, rows), jnp.bfloat16),
                pltpu.VMEM((sources, rows, window) if bases else (sources, window, columns[0].shape[1]), jnp.bfloat16),
                pltpu.SemaphoreType.DMA((sources, count + parts)),
            ],
        ),
        out_shape=[
            jax.ShapeDtypeStruct((depth, window), jnp.float32) if bases else pltpu.HBM((depth, window), jnp.bfloat16)
        ] * count,
        compiler_params=pltpu.CompilerParams(vmem_limit_bytes=(16 if bases else 18) * MIB),
        cost_estimate=lasting(3 if bases else 6),
        name="projection_peers" if bases else "projection_chip",
    )(order, start, *attended, *columns, *map(in_hbm, bases))


def windows_of(groups, owned, total):
    lows = [g * owned // LANE * LANE for g in range(groups)]
    width = max(-(-((g + 1) * owned) // LANE) * LANE - low for g, low in enumerate(lows))
    return width


def ring_of(count):
    return list(range(0, count, 2)) + list(range(count - 1, 0, -2))


def local(members, shards, query_key_value, cotangent, proj_weight, layer_scale, lengths):
    member = lax.axis_index("dp")
    shard = lax.axis_index("fsdp")
    core, chip, peers = member % 2, member // 2, members // 2
    ring = ring_of(shards)
    place = jnp.where(shard % 2 == 0, shard // 2, shards - 1 - shard // 2)
    ahead = [(ring[i], ring[(i + 1) % shards]) for i in range(shards)]
    behind = [(ring[i], ring[(i - 1) % shards]) for i in range(shards)]
    ways = [ahead, behind]
    streams = [
        [(d * shards + a, d * shards + b) for d in range(members) for a, b in ways[(d + turn) % 2]] for turn in range(2)
    ]
    half = shards // 2
    depth, total = proj_weight.shape
    rows, width = query_key_value.shape[1:]
    owned = total // members
    counts = lax.dynamic_index_in_dim(lengths[:, 0, :], member, 0, keepdims=False)

    def send(array, stream):
        return lax.ppermute(array, ("dp", "fsdp"), streams[stream])

    def swap(array, bit):
        return lax.ppermute(array, "dp", [(i, i ^ bit) for i in range(members)])

    def shard_at(offset):
        at = (place + (1 - 2 * core) * offset + shards) % shards
        return jnp.where(at < half, 2 * at, 2 * (shards - 1 - at) + 1)

    def table(values):
        return jnp.stack([jnp.asarray(v) for v in values]).astype(jnp.int32)

    chip_width, window = windows_of(peers, 2 * owned, total), windows_of(members, owned, total)

    def chip_start(chip):
        return jnp.minimum(chip * 2 * owned // LANE * LANE, total - chip_width)

    my_start = jnp.minimum(member * owned // LANE * LANE, chip_start(chip) + chip_width - window)
    starts = table([my_start, my_start - chip_start(chip)])

    split = -(-(total // LANE) // 2) * LANE
    mine = half_columns(table([core * (total - split)]), proj_weight, split)
    up, down = [mine], [mine]
    up.append(send(up[-1], 0))
    down.append(send(down[-1], 1))

    mine, cotangent = lax.optimization_barrier((mine, cotangent))
    scales = layer_scale.reshape(1, total)
    sent = peer_windows(
        table([chip_start(chip ^ k) for k in range(1, peers)] or [0]), cotangent, scales, peers - 1, chip_width
    )
    sent, cotangent = lax.optimization_barrier((sent, cotangent))
    came_columns = [[swap(array, 2 * k) for k, array in enumerate(part, 1)] for part in sent]
    turned = prepare(cotangent, scales)
    attended, main_probs, slot_probs = forward(counts, query_key_value)
    attended = attended.reshape(shards, depth, rows)
    near = [[o, -o] for o in range(half - 1, 0, -1)]
    groups = [[half] + near[0]] + near[1:-1] + [near[-1] + [0]]
    flat = table([shard_at(o) for group in groups for o in group])
    sizes = [len(group) for group in groups]
    orders = [flat[sum(sizes[:g]):sum(sizes[:g + 1])] for g in range(len(groups))]

    def rows_of(some, held):
        info = table([core] + [shard_at(o) for _, o in some])
        return grad_out_rows(info, turned, turned_other, rows, [p for p, _ in some], shards, held)

    up[1], down[1], attended, came_columns[0], turned = lax.optimization_barrier(
        (up[1], down[1], attended, came_columns[0], turned)
    )
    turned_other = swap(turned, 1)
    other_columns = [[swap(array, 1) for array in came_columns[0]]]
    attended_other = swap(attended, 1)
    chunks = list(arrange(flat, attended, sizes))
    attended_other, chunks = lax.optimization_barrier((attended_other, chunks))
    for _ in range(half - 3):
        up.append(send(up[-1], 0))
        down.append(send(down[-1], 1))
    bases = partial_products(
        flat, starts[:1], [in_hbm(attended), attended_other], [in_hbm(turned), turned_other], window
    )
    up[-1], down[-1], turned_other, attended_other, *bases = lax.optimization_barrier(
        (up[-1], down[-1], turned_other, attended_other, *bases)
    )
    bases = dict(zip([o for group in groups for o in group], bases))

    late, chunks = lax.optimization_barrier((came_columns[1], chunks))
    came = [[swap(chunks[0], 2 * k) for k in range(1, peers)]]
    other_columns.append([swap(array, 1) for array in late])
    came_columns[1] = late
    came.append([swap(chunks[1], 2 * k) for k in range(1, peers)])
    columns = []
    for k in range(peers - 1):
        for arrays in (came_columns, other_columns):
            columns += [in_hbm(part[k]) for part in arrays]
    pieces = [([mine], 0)]
    for step in range(1, half - 1):
        pieces += [([up[step]], -step), ([down[step]], step)]
    pieces[:-2] = [([in_hbm(array) for array in arrays], o) for arrays, o in pieces[:-2]]
    grad_out = rows_of(pieces, None)
    up.append(send(up[-1], 0))
    down.append(send(down[-1], 1))
    up[-1], down[-1], grad_out = lax.optimization_barrier((up[-1], down[-1], grad_out))
    far = send(up[-1], 0)
    came[0], near_up, near_down = lax.optimization_barrier((came[0], up[-1], down[-1]))

    def both_cores(arrays):
        return [a for c in arrays for a in (c, swap(c, 1))]

    def products(index, taken):
        group = groups[index]
        if not taken:
            return {o: bases[o] for o in group}
        turned_round = [group.index(-o) if -o in group else j for j, o in enumerate(group)]
        result = partial_products(orders[index], starts[1:], taken, columns, window, [bases[o] for o in group], turned_round)
        return dict(zip(group, result))

    terms = products(0, both_cores(came[0]))
    first = terms[half].astype(jnp.bfloat16)
    first, came[1], chunks, far = lax.optimization_barrier((first, came[1], chunks, far))
    came += [[swap(some, 2 * k) for k in range(1, peers)] for some in chunks[2:]]
    taken = both_cores(came[1])
    came_up, came_down = send(first, 0), None

    bounds = [0, 2, 5, -(-(width // HS) // PAIR)]
    grads = None
    for step in range(half, 1, -1):
        if step == half:
            came_up, following = lax.optimization_barrier((came_up, products(1, taken)))
            terms.update(following)
        going_up = (terms[step - 1] + came_up.astype(jnp.float32)).astype(jnp.bfloat16)
        going_down = terms[1 - step] if came_down is None else terms[1 - step] + came_down.astype(jnp.float32)
        going_down = going_down.astype(jnp.bfloat16)
        if step == half:
            going_up, going_down, near_up = lax.optimization_barrier((going_up, going_down, near_up))
            grad_out = rows_of([([near_up], 1 - half), ([near_down], half - 1), ([far], half)], grad_out)
            grad_mine = grad_out[0].reshape(width, rows)
            came[2], grad_other = lax.optimization_barrier((came[2], grad_out[1]))
            grad_other = swap(grad_other, 1).reshape(width, rows)
        elif step > 2:
            arrived = came[half - step + 1]
            going_up, going_down, arrived, grad_mine = lax.optimization_barrier((going_up, going_down, arrived, grad_mine))
            terms.update(products(half - step + 1, [in_hbm(array) for array in both_cores(arrived)]))
        else:
            going_up, going_down = lax.optimization_barrier((going_up, going_down))
        came_up, came_down = send(going_up, 0), send(going_down, 1)
    for low, high in zip(bounds, bounds[1:]):
        grads = backward(query_key_value, grad_mine, grad_other, main_probs, slot_probs, low, high, grads)
    came_up, came_down, grads = lax.optimization_barrier((came_up, came_down, grads))
    offsets = set()
    for m in range(members):
        low = min((m // 2) * 2 * owned // LANE * LANE, total - chip_width)
        offsets.add(m * owned - min(m * owned // LANE * LANE, low + chip_width - window))
    grad_proj = finish(table([member * owned - my_start]), terms[0], came_up, came_down, owned, sorted(offsets))
    return grads, grad_proj


def solution(mesh):
    members, shards = mesh.shape["dp"], mesh.shape["fsdp"]
    placed = (
        P(None, ("dp", "fsdp"), None),
        P(("dp", "fsdp"), None),
        P("fsdp", None),
        P(),
        P(None, "fsdp", None),
    )
    return jax.shard_map(
        functools.partial(local, members, shards),
        mesh=mesh,
        in_specs=placed,
        out_specs=(P(None, ("dp", "fsdp"), None), P("fsdp", "dp")),
        check_vma=False,
    )
```
